32 devices in a mesh: gen: 16 (over z, y, core), tp: 2 (over x).
Axes of the slice: x: 2, y: 2, z: 4, core: 2. Of those that a mesh axis runs over, the one named last changes fastest.
Arguments:
- tokens_in: bfloat16 [2048, 5120], P('gen', 'tp'), may hold values from -6 to 6
- w_kv: bfloat16 [5120, 2048], P('tp'), may hold values from -0.078125 to 0.078125
- queries: bfloat16 [1024, 2, 40, 128], P('gen', None, 'tp'), may hold values from -8 to 8
- k_cache: bfloat16 [896, 8, 64, 128], P('gen', 'tp'), may hold values from -8 to 8
- v_cache: bfloat16 [896, 8, 64, 128], P('gen', 'tp'), may hold values from -5 to 5
- page_table: int32 [1024, 32], P('gen'), may hold values from 0 to 55, as said below
- lengths: int32 [1024], P('gen'), may hold values from 1 to 2048, as said below
- move_dest: int32 [256, 1], replicated, may hold values from 0 to 15; in each aligned block of 16 rows (0 to 15, 16 to 31, ...) at most 2 rows name the same one
- move_page: int32 [256], replicated, may hold values from 0 to 55
- move_seq: int32 [256], replicated, may hold values from 0 to 63
Outputs:
- attended: bfloat16 [1024, 2, 40, 128], P('gen', None, 'tp')
- new_kv: bfloat16 [2048, 2048], P('gen', 'tp')
The draws below stay inside these ranges and needn't reach their ends.
Inputs may be any that keep to these rules, and one draw needn't show every extreme that they name: `page_table`: each row names 32 different pages. `lengths`: some sequence has exactly 2048 positions in every draw. `move_dest`: rows r * 16 to (r + 1) * 16 - 1 are the moves of source device r; among one source's rows no destination appears more than 2 times, a bound that some block reaches.
All inputs are finite; a program needn't handle non-finite values.
Results may differ from the reference program's by a relative error of at most 0.0043.
Values may be sent and summed in bfloat16 or wider, within the bound.
No kernel may reach another device: no remote copies, remote signals or barrier semaphores. Data moves between devices by JAX's collectives and lax.ppermute only.
A program may use at most 192 MiB of HBM per device.

```python
import math
import jax
import jax.numpy as jnp
import numpy as np
from jax import lax

D = 5120
HEADS = 40
KV_HEADS = 8
HD = 128
GROUP = 5
SEQ_DEV = 64
STEPS = 2
PAGE = 64
MAXP = 32
POOL = 56
CAP = 2
SEQS = 1024
TOKENS = 2048
POOL_ALL = 896
MOVES_DEV = 16
MOVES = 256
N_GEN = 16


def draw_k_cache(key, part):
    full_shape = (POOL_ALL, KV_HEADS, PAGE, HD)
    values_drawn = jnp.clip(jax.random.normal(jax.random.fold_in(key, 1), full_shape, jnp.float32), -5.0, 5.0)
    return values_drawn.astype(jnp.bfloat16)


def draw_queries(key, part):
    full_shape = (SEQS, STEPS, HEADS, HD)
    values_drawn = jnp.clip(jax.random.normal(jax.random.fold_in(key, 2), full_shape, jnp.float32), -5.0, 5.0)
    return values_drawn.astype(jnp.bfloat16)


def draw_page_table(key, part):
    row_keys = jax.random.split(jax.random.fold_in(key, 11), SEQS)
    chosen = jax.vmap(lambda row_key: jax.random.permutation(row_key, POOL)[:MAXP])(row_keys)
    return chosen.astype(jnp.int32)


def draw_lengths(key, part):
    longest = MAXP * PAGE
    factor = jax.random.randint(jax.random.fold_in(key, 13), (SEQS // SEQ_DEV,), 1, 5)
    upper_limit = jnp.repeat(longest * factor // 4, SEQ_DEV, total_repeat_length=SEQS)
    drawn_lengths = jax.random.randint(jax.random.fold_in(key, 17), (SEQS,), 1, upper_limit + 1)
    full_index = jax.random.randint(jax.random.fold_in(key, 19), (), 0, SEQS)
    drawn_lengths = jnp.where(jnp.arange(SEQS) == full_index, longest, drawn_lengths)
    return drawn_lengths.astype(jnp.int32)


def with_ends(values, own_key, low, largest):
    longest = values.shape.index(max(values.shape))
    spots = []
    for shift in (0, 1):
        where = [jax.random.randint(jax.random.fold_in(own_key, axis), (), 0, length) for axis, length in enumerate(values.shape)]
        where[longest] = (where[longest] + shift) % values.shape[longest]
        spots.append(tuple(where))
    return values.at[spots[0]].set(low).at[spots[1]].set(largest)


def block_scale(rng, dims, cuts, low, top_value):
    def one(dim, parts):
        draws = jax.random.uniform(jax.random.fold_in(jax.random.fold_in(rng, 6), dim), (parts,), jnp.float32, low / len(cuts), top_value / len(cuts))
        return jnp.repeat(jnp.exp(draws), dims[dim] // parts).reshape((-1,) + (1,) * (len(dims) - dim - 1))

    level = one(*cuts[0])
    for cut in cuts[1:]:
        level = level * one(*cut)
    return level


def assign_block(own_key, own, number, rows, number_of, top, limit, lean):
    order = jax.random.permutation(own_key, number_of)
    crowded, usual = load_shares(number_of, rows * top, limit, lean, True), load_shares(number_of, rows * top, limit, lean, False)
    places = jnp.arange(number_of)

    def named(tallies, offset_by):
        used = int((tallies > 0).sum())
        fixed = max(1, used // 4)
        moved = fixed + (places - fixed + offset_by * (used - fixed)) % max(1, number_of - fixed)
        return jnp.zeros((number_of,), jnp.int32).at[order[jnp.where(places < fixed, places, moved)]].set(jnp.asarray(tallies, jnp.int32))

    tallies = jnp.where(number % 4 == 0, named(crowded, number // 4), named(usual, number - number // 4 - 1))
    mixed = jax.random.permutation(jax.random.fold_in(own, 3), number_of)
    donor, taker = mixed[0:number_of // 2 * 2:2], mixed[1:number_of // 2 * 2:2]
    room = jnp.minimum(tallies[donor] - 1, limit - tallies[taker]) // 2
    room = jnp.where((donor == order[0]) | (taker == order[0]) | (tallies[taker] == 0), 0, jnp.maximum(room, 0))
    moved = jax.random.randint(jax.random.fold_in(own, 4), (number_of // 2,), 0, 1 << 20) % (room + 1)
    tallies = tallies.at[donor].add(-moved).at[taker].add(moved)
    items = jnp.searchsorted(jnp.cumsum(tallies), jnp.arange(rows * top), side="right").astype(jnp.int32)
    table = items.reshape(top, rows).T
    table = table[jax.random.permutation(jax.random.fold_in(own, 1), rows)]
    offset_by = jax.random.randint(jax.random.fold_in(own, 2), (rows, 1), 0, top)
    return jnp.take_along_axis(table, (jnp.arange(top)[None, :] + offset_by) % top, axis=1)


def load_shares(amount, total, bound, skew, full):
    weights = [(1 << 20) // math.isqrt(rank ** skew) + 1 for rank in range(1, amount + 1)]
    largest = bound if full else min(bound, max(-(-total // amount), total * weights[0] // sum(weights)))
    least = 1 if total - largest >= amount - 1 else 0
    given, spare = [largest] + [least] * (amount - 1), total - largest - least * (amount - 1)
    while spare > 0:
        candidates = [i for i in range(1, amount) if given[i] < largest] or [i for i in range(1, amount) if given[i] < bound]
        pool, budget = sum([weights[i] for i in candidates]), spare
        for i in candidates:
            more = min(bound - given[i], max(1, budget * weights[i] // pool), spare)
            given[i] = given[i] + more
            spare = spare - more
    return np.array(given)


def scatter_about(rng, extent, width, bound, cuts=(), dtype=jnp.bfloat16):
    factor_of = block_scale(rng, extent, cuts, -0.22, 0.18) if cuts else 1.0
    result = jax.random.normal(rng, extent, jnp.float32) * width * factor_of
    return jnp.minimum(jnp.maximum(result, -bound), bound).astype(dtype)


def setup_inputs(seed: int = 0) -> dict:
    seeds = jax.random.split(jax.random.key(seed), 11)
    tokens_in = scatter_about(seeds[0], (TOKENS, D), 1.0, 6.0, ((0, 16), (1, 2)))
    w_kv = scatter_about(seeds[1], (D, KV_HEADS * 2 * HD), D ** -0.5, 0.078125, ((0, 2),))
    queries = draw_queries(jax.random.fold_in(seeds[10], 71), 0)
    k_cache = draw_k_cache(jax.random.fold_in(seeds[10], 71), 0)
    v_cache = scatter_about(seeds[4], (POOL_ALL, KV_HEADS, PAGE, HD), 1.0, 5.0, ((0, 16), (1, 2)))
    page_table = draw_page_table(jax.random.fold_in(seeds[10], 71), 0)
    lengths = draw_lengths(jax.random.fold_in(seeds[10], 71), 0)
    move_dest_keys = jax.random.split(jax.random.fold_in(seeds[7], 1), MOVES // MOVES_DEV)
    move_dest_turns = jax.random.permutation(jax.random.fold_in(seeds[7], 3), MOVES // MOVES_DEV)
    move_dest = jax.vmap(lambda own, number: assign_block(jax.random.fold_in(seeds[7], 2), own, number, MOVES_DEV, N_GEN, 1, CAP, 2))(move_dest_keys, move_dest_turns).reshape((MOVES, 1))
    move_page = with_ends(jax.random.randint(seeds[8], (MOVES,), 0, POOL), jax.random.fold_in(seeds[8], 1), 0, POOL - 1).astype(jnp.int32)
    move_seq = with_ends(jax.random.randint(seeds[9], (MOVES,), 0, SEQ_DEV), jax.random.fold_in(seeds[9], 1), 0, SEQ_DEV - 1).astype(jnp.int32)
    return dict(tokens_in=tokens_in, w_kv=w_kv, queries=queries, k_cache=k_cache, v_cache=v_cache, page_table=page_table, lengths=lengths, move_dest=move_dest, move_page=move_page, move_seq=move_seq)


NEGATIVE = -1e+30

def slot_tables(move_dest, move_page, move_seq, dest_index):
    destinations = move_dest.reshape(N_GEN, MOVES_DEV)
    page_ids = move_page.reshape(N_GEN, MOVES_DEV)
    owner_ids = move_seq.reshape(N_GEN, MOVES_DEV)
    position = jnp.arange(MOVES_DEV)
    earlier = position[None, :] < position[:, None]
    same_dest = destinations[:, :, None] == destinations[:, None, :]
    move_ranks = lax.optimization_barrier(jnp.sum(jnp.where(same_dest & earlier[None], 1, 0), axis=2)).astype(jnp.int32)
    matches = (destinations[:, :, None] == dest_index) & (move_ranks[:, :, None] == jnp.arange(CAP)[None, None, :])
    matches = matches.astype(jnp.int32)
    arrived = lax.optimization_barrier(jnp.sum(matches, axis=1)).reshape(-1).astype(jnp.int32)
    page_at = lax.optimization_barrier(jnp.sum(matches * page_ids[:, :, None], axis=1)).reshape(-1).astype(jnp.int32)
    owner_seq = lax.optimization_barrier(jnp.sum(matches * owner_ids[:, :, None], axis=1)).reshape(-1).astype(jnp.int32)
    return (arrived, page_at, owner_seq)

def to_bf16(values):
    return lax.optimization_barrier(values.astype(jnp.bfloat16)).astype(jnp.float32)

def reference(tokens_in, w_kv, queries, k_cache, v_cache, page_table, lengths, move_dest, move_page, move_seq):
    score_scale = 1.0 / math.sqrt(HD)
    new_kv = jnp.dot(tokens_in, w_kv, preferred_element_type=jnp.float32).astype(jnp.bfloat16)
    fresh_grid = new_kv.reshape(SEQS, STEPS, KV_HEADS, 2, HD)
    query_grid = queries.reshape(SEQS, STEPS, KV_HEADS, GROUP, HD)

    def one_device(dev_index):
        first_seq = (dev_index * SEQ_DEV).astype(jnp.int32)
        query_dev = lax.dynamic_slice_in_dim(query_grid, first_seq, SEQ_DEV, 0).astype(jnp.float32)
        fresh_dev = lax.dynamic_slice_in_dim(fresh_grid, first_seq, SEQ_DEV, 0).astype(jnp.float32)
        page_rows = lax.dynamic_slice_in_dim(page_table, first_seq, SEQ_DEV, 0) + (dev_index * POOL).astype(jnp.int32)
        seq_lengths = lax.dynamic_slice_in_dim(lengths, first_seq, SEQ_DEV, 0)
        arrived, page_at, owner_seq = slot_tables(move_dest, move_page, move_seq, dev_index)
        slot_rows = (jnp.arange(N_GEN * CAP) // CAP).astype(jnp.int32) * POOL + page_at
        slot_keys = k_cache[slot_rows].astype(jnp.float32)
        slot_values = v_cache[slot_rows].astype(jnp.float32)
        slot_query = query_dev[owner_seq]
        slot_scores = jnp.einsum('nicgd,ncpd->nicgp', slot_query, slot_keys) * score_scale
        slot_max = lax.optimization_barrier(jnp.max(slot_scores, axis=-1))
        slot_w = to_bf16(jnp.exp(slot_scores - slot_max[..., None]))
        slot_total = lax.optimization_barrier(jnp.sum(slot_w, axis=-1))
        slot_sum = jnp.einsum('nicgp,ncpd->nicgd', slot_w, slot_values)
        landed = arrived > 0
        slot_max = jnp.where(landed[:, None, None, None], slot_max, NEGATIVE)
        member = (owner_seq[None, :] == jnp.arange(SEQ_DEV)[:, None]) & landed[None, :]
        member_f = member.astype(jnp.float32)
        moved_max = lax.optimization_barrier(jnp.max(jnp.where(member[:, :, None, None, None], slot_max[None], NEGATIVE), axis=1))
        positions = jnp.arange(MAXP * PAGE)
        visible = positions[None, :] < seq_lengths[:, None]
        causal = jnp.arange(STEPS)[None, :] <= jnp.arange(STEPS)[:, None]

        def per_head(head_index):
            query_head = query_dev[:, :, head_index]
            stale_keys = k_cache[page_rows, head_index].astype(jnp.float32).reshape(SEQ_DEV, MAXP * PAGE, HD)
            stale_values = v_cache[page_rows, head_index].astype(jnp.float32).reshape(SEQ_DEV, MAXP * PAGE, HD)
            local_scores = jnp.einsum('sigd,sjd->sigj', query_head, stale_keys) * score_scale
            local_max = lax.optimization_barrier(jnp.max(jnp.where(visible[:, None, None, :], local_scores, NEGATIVE), axis=-1))
            new_keys = fresh_dev[:, :, head_index, 0]
            new_values = fresh_dev[:, :, head_index, 1]
            new_scores = jnp.einsum('sigd,skd->sigk', query_head, new_keys) * score_scale
            new_max = lax.optimization_barrier(jnp.max(jnp.where(causal[None, :, None, :], new_scores, NEGATIVE), axis=-1))
            biggest = jnp.maximum(jnp.maximum(local_max, new_max), moved_max[:, :, head_index])
            local_w = to_bf16(jnp.where(visible[:, None, None, :], jnp.exp(local_scores - biggest[..., None]), 0.0))
            new_w = jnp.where(causal[None, :, None, :], jnp.exp(new_scores - biggest[..., None]), 0.0)
            factor = jnp.exp(slot_max[:, :, head_index] - biggest[owner_seq])
            moved_total = jnp.einsum('sn,nig->sig', member_f, factor * slot_total[:, :, head_index])
            moved_sum = jnp.einsum('sn,nigd->sigd', member_f, factor[..., None] * slot_sum[:, :, head_index])
            numerator = jnp.einsum('sigj,sjd->sigd', local_w, stale_values) + moved_sum + jnp.einsum('sigk,skd->sigd', new_w, new_values)
            denominator = lax.optimization_barrier(jnp.sum(local_w, axis=-1)) + moved_total + lax.optimization_barrier(jnp.sum(new_w, axis=-1))
            return numerator / denominator[..., None]
        by_head = lax.map(per_head, jnp.arange(KV_HEADS))
        return jnp.transpose(by_head, (1, 2, 0, 3, 4))
    every_device = lax.map(one_device, jnp.arange(N_GEN))
    attended = every_device.reshape(SEQS, STEPS, HEADS, HD).astype(jnp.bfloat16)
    return (attended, new_kv)
```

```python
import functools
import math

import jax
import jax.numpy as jnp
from jax import lax
from jax.experimental import pallas as pl
from jax.experimental.pallas import tpu as pltpu
from jax.sharding import PartitionSpec as P

CAP = 2
NEGATIVE = -1e30
LOG2E = 1.4426950408889634
LANES = 128
VMEM_LIMIT = 56 * 1024 * 1024


def whole(array):
    return pl.BlockSpec(array.shape, lambda *_: (0,) * array.ndim)


def smem():
    return pl.BlockSpec(memory_space=pltpu.SMEM)


def padded(rows):
    return (rows + 7) // 8 * 8


def slot_rows(steps, heads):
    step_rows = padded(heads + 3)
    return step_rows, (steps * step_rows + 15) // 16 * 16


def gather_kernel(
    dest_ref, seq_ref, me_ref, q_ref, owner_ref, landed_ref, slot_ref, out_ref, *, groups, per_source
):
    me = me_ref[0]
    slots = groups * CAP
    seqs, steps, heads, head_dim = q_ref.shape
    step_rows, rows = slot_rows(steps, heads)

    def clear(n, _):
        owner_ref[n] = 0
        landed_ref[n] = 0
        return 0

    lax.fori_loop(0, slots, clear, 0, unroll=8)
    owner_ref[slots] = 0
    landed_ref[slots] = 0

    def one_source(src, _):
        count = jnp.int32(0)
        for k in range(per_source):
            row = src * per_source + k
            hit = dest_ref[row] == me
            place = jnp.where(hit, src * CAP + count, slots)
            owner_ref[place] = seq_ref[row]
            landed_ref[place] = 1
            count = count + hit.astype(jnp.int32)
        return 0

    lax.fori_loop(0, groups, one_source, 0)

    for k in range(per_source):
        mine = dest_ref[me * per_source + k]
        rank = jnp.int32(0)
        for j in range(k):
            rank = rank + (dest_ref[me * per_source + j] == mine).astype(jnp.int32)
        slot_ref[k] = mine * CAP + rank

    zeros = jnp.zeros((step_rows - heads, head_dim), jnp.float32)

    def one_slot(n, _):
        block = q_ref[owner_ref[n]].astype(jnp.float32)
        parts = []
        for i in range(steps):
            parts += [block[i], zeros]
        if rows > steps * step_rows:
            parts.append(jnp.zeros((rows - steps * step_rows, head_dim), jnp.float32))
        out_ref[n] = jnp.concatenate(parts, axis=0).astype(jnp.bfloat16)
        return 0

    lax.fori_loop(0, slots, one_slot, 0, unroll=4)


def gather(dest, seq, me, queries, groups):
    per_source = dest.shape[0] // groups
    slots = groups * CAP
    seqs, steps, heads, head_dim = queries.shape
    _, rows = slot_rows(steps, heads)
    return pl.pallas_call(
        functools.partial(gather_kernel, groups=groups, per_source=per_source),
        in_specs=[smem(), smem(), smem(), pl.BlockSpec(memory_space=pltpu.VMEM)],
        out_specs=[smem(), smem(), smem(), pl.BlockSpec(memory_space=pltpu.VMEM)],
        out_shape=[
            jax.ShapeDtypeStruct((slots + 1,), jnp.int32),
            jax.ShapeDtypeStruct((slots + 1,), jnp.int32),
            jax.ShapeDtypeStruct((per_source,), jnp.int32),
            jax.ShapeDtypeStruct((slots, rows, head_dim), jnp.bfloat16),
        ],
        compiler_params=pltpu.CompilerParams(vmem_limit_bytes=VMEM_LIMIT),
        cost_estimate=pl.CostEstimate(flops=0, bytes_accessed=4 * queries.size, transcendentals=0),
        name="gather_queries",
    )(dest, seq, me, queries)


def project_kernel(shift_ref, x_ref, w_ref, own_ref, send_ref, *, blocks):
    product = jnp.dot(x_ref[...], w_ref[...], preferred_element_type=jnp.float32)
    step = pl.program_id(0)

    @pl.when(step < blocks)
    def _():
        own_ref[...] = product

    @pl.when(step >= blocks)
    def _():
        send_ref[0] = product


def project(tokens, w_kv, tp, tp_index):
    rows, depth = tokens.shape
    columns = w_kv.shape[1] // tp
    width = min(256, columns)
    blocks = columns // width
    shift = jnp.reshape(tp_index, (1,)).astype(jnp.int32)

    def w_map(step, shift_ref):
        owner = lax.rem(shift_ref[0] + step // blocks, tp)
        return (0, owner * blocks + lax.rem(step, blocks))

    def send_map(step, shift_ref):
        after = jnp.maximum(step - blocks, 0)
        return (after // blocks, 0, lax.rem(after, blocks))

    return pl.pallas_call(
        functools.partial(project_kernel, blocks=blocks),
        grid_spec=pltpu.PrefetchScalarGridSpec(
            num_scalar_prefetch=1,
            grid=(tp * blocks,),
            in_specs=[
                pl.BlockSpec((rows, depth), lambda step, shift_ref: (0, 0)),
                pl.BlockSpec((depth, width), w_map),
            ],
            out_specs=[
                pl.BlockSpec(
                    (rows, width), lambda step, shift_ref: (0, jnp.minimum(step, blocks - 1))
                ),
                pl.BlockSpec((1, rows, width), send_map),
            ],
        ),
        out_shape=[
            jax.ShapeDtypeStruct((rows, columns), jnp.float32),
            jax.ShapeDtypeStruct((tp - 1, rows, columns), jnp.float32),
        ],
        compiler_params=pltpu.CompilerParams(vmem_limit_bytes=VMEM_LIMIT),
        cost_estimate=pl.CostEstimate(
            flops=2 * rows * depth * columns * tp,
            bytes_accessed=2 * w_kv.size + 2 * tokens.size + 4 * rows * columns * tp,
            transcendentals=0,
        ),
        name="project_kv",
    )(shift, tokens, w_kv)


def local_kernel(
    q_ref, k_ref, v_ref, table_ref, length_ref, out_ref, lse_ref, query, bias, scores, top, total,
    *, width, first_head, per_group, scale
):
    seqs, steps, heads, head_dim = q_ref.shape
    page = k_ref.shape[2]
    blocks = scores.shape[0]
    step_rows = padded(heads)
    groups = steps * per_group
    rows = groups * seqs
    pages = width // page
    tiles = width // LANES
    head = pl.program_id(0)

    @pl.when(head == 0)
    def _():
        spread = query.reshape(seqs * steps, step_rows, head_dim)
        spread[:, :heads, :] = q_ref[...].reshape(seqs * steps, heads, head_dim).astype(jnp.float32)
        across = lax.broadcasted_iota(jnp.int32, (seqs, seqs), 1)
        down = lax.broadcasted_iota(jnp.int32, (seqs, seqs), 0)
        lengths = jnp.broadcast_to(length_ref[...].astype(jnp.float32), (seqs, seqs))
        lengths = jnp.sum(jnp.where(down == across, lengths, 0.0), axis=1, keepdims=True)
        lane = lax.broadcasted_iota(jnp.int32, (seqs, LANES), 1)
        used = jnp.zeros((seqs, LANES), jnp.float32)
        table = table_ref[...]
        for j in range(table.shape[1]):
            inside = jnp.clip(lengths - float(page * j), 0.0, float(page))
            used = used + jnp.where(table[:, j : j + 1] == lane, inside, 0.0)
        used = used.astype(jnp.bfloat16)

        def one_block(b, _):
            key = lax.broadcasted_iota(jnp.int32, (LANES, width), 1) + b * width
            owner = lax.broadcasted_iota(jnp.int32, (LANES, width), 0)
            expand = jnp.where(key // page == owner, 1.0, 0.0).astype(jnp.bfloat16)
            count = jnp.dot(used, expand, preferred_element_type=jnp.float32)
            position = lax.broadcasted_iota(jnp.int32, (seqs, width), 1) % page
            bias[b] = jnp.where(position.astype(jnp.float32) < count, 0.0, NEGATIVE)
            return 0

        lax.fori_loop(0, blocks, one_block, 0)

    parts = []
    for i in range(steps):
        for g in range(per_group):
            start = i * step_rows + (first_head + head) * per_group + g
            parts.append(query[pl.ds(start, seqs, stride=steps * step_rows), :])
    head_query = jnp.concatenate(parts, axis=0).astype(jnp.bfloat16)
    top[...] = jnp.full(top.shape, NEGATIVE, jnp.float32)
    total[...] = jnp.zeros(total.shape, jnp.float32)

    def score_block(b, _):
        keys = k_ref[pl.ds(b * pages, pages), 0].reshape(width, head_dim)
        s = lax.dot_general(
            head_query, keys, (((1,), (1,)), ((), ())), preferred_element_type=jnp.float32
        )
        s = (s.reshape(groups, seqs, width) + bias[b][None]).reshape(rows, width)
        scores[b] = s
        largest = s[:, :LANES]
        for t in range(1, tiles):
            largest = jnp.maximum(largest, s[:, t * LANES : (t + 1) * LANES])
        top[...] = jnp.maximum(top[...], largest)
        return 0

    lax.fori_loop(0, blocks, score_block, 0)
    top[...] = jnp.broadcast_to(jnp.max(top[...], axis=1, keepdims=True), top.shape)
    ones = jnp.ones((width, head_dim), jnp.bfloat16)

    def value_block(b, _):
        values = v_ref[pl.ds(b * pages, pages), 0].reshape(width, head_dim)
        values = jnp.concatenate([values, ones], axis=1)
        biggest = top[...]
        weights = jnp.concatenate(
            [
                jnp.exp2((scores[b, :, t * LANES : (t + 1) * LANES] - biggest) * scale).astype(
                    jnp.bfloat16
                )
                for t in range(tiles)
            ],
            axis=1,
        )
        total[...] += jnp.dot(weights, values, preferred_element_type=jnp.float32)
        return 0

    lax.fori_loop(0, blocks, value_block, 0)
    weight_sum = total[:, head_dim:]
    out_ref[0] = total[:, :head_dim] / weight_sum
    lse_ref[0] = top[...] * scale + jnp.log2(weight_sum)


def local_attention(queries, k_cache, v_cache, page_table, lengths, first_head, count, scale):
    seqs, steps, heads, head_dim = queries.shape
    pool, kv_heads, page, _ = k_cache.shape
    per_group = heads // kv_heads
    rows = steps * per_group * seqs
    keys = pool * page
    width = keys // 4
    cache_spec = pl.BlockSpec((pool, 1, page, head_dim), lambda h: (0, first_head + h, 0, 0))
    out_spec = pl.BlockSpec((1, rows, head_dim), lambda h: (h, 0, 0))
    out_shape = jax.ShapeDtypeStruct((count, rows, head_dim), jnp.float32)
    return pl.pallas_call(
        functools.partial(
            local_kernel, width=width, first_head=first_head, per_group=per_group, scale=scale
        ),
        grid=(count,),
        in_specs=[whole(queries), cache_spec, cache_spec, whole(page_table), whole(lengths)],
        out_specs=[out_spec, out_spec],
        out_shape=[out_shape, out_shape],
        scratch_shapes=[
            pltpu.VMEM((seqs * steps * padded(heads), head_dim), jnp.float32),
            pltpu.VMEM((keys // width, seqs, width), jnp.float32),
            pltpu.VMEM((keys // width, rows, width), jnp.float32),
            pltpu.VMEM((rows, LANES), jnp.float32),
            pltpu.VMEM((rows, 2 * head_dim), jnp.float32),
        ],
        compiler_params=pltpu.CompilerParams(vmem_limit_bytes=VMEM_LIMIT),
        cost_estimate=pl.CostEstimate(
            flops=6 * count * rows * keys * head_dim,
            bytes_accessed=4 * count * keys * head_dim + 8 * count * rows * head_dim,
            transcendentals=count * rows * keys,
        ),
        name="local_attention",
    )(queries, k_cache, v_cache, page_table, lengths)


def moved_kernel(
    slot_ref, page_ref, q_ref, k_hbm, v_hbm, out_ref, keys, values, sems, *, steps, heads, scale
):
    moves, kv_heads, page, head_dim = keys.shape
    per_group = heads // kv_heads
    step_rows, rows = slot_rows(steps, heads)
    columns = kv_heads * page

    def copies(k):
        source = page_ref[k]
        return (
            pltpu.make_async_copy(k_hbm.at[source], keys.at[k], sems.at[0, k]),
            pltpu.make_async_copy(v_hbm.at[source], values.at[k], sems.at[1, k]),
        )

    def start(k, _):
        for copy in copies(k):
            copy.start()
        return 0

    lax.fori_loop(0, moves, start, 0)
    out_ref[...] = jnp.zeros(out_ref.shape, jnp.bfloat16)
    row = lax.broadcasted_iota(jnp.int32, (rows, columns), 0)
    column = lax.broadcasted_iota(jnp.int32, (rows, columns), 1)
    same_head = (lax.rem(row, step_rows) // per_group) == column // page
    tall = lax.broadcasted_iota(jnp.int32, (rows, LANES), 0)
    lane = lax.broadcasted_iota(jnp.int32, (rows, LANES), 1)
    ones = jnp.ones((columns, head_dim), jnp.bfloat16)

    def one_move(k):
        s = lax.dot_general(
            q_ref[slot_ref[k]],
            keys[k].reshape(columns, head_dim),
            (((1,), (1,)), ((), ())),
            preferred_element_type=jnp.float32,
        )
        s = jnp.where(same_head, s, NEGATIVE)
        biggest = jnp.max(s, axis=1, keepdims=True)
        weights = jnp.exp2((s - biggest) * scale).astype(jnp.bfloat16)
        both = jnp.concatenate([values[k].reshape(columns, head_dim), ones], axis=1)
        summed = jnp.dot(weights, both, preferred_element_type=jnp.float32)
        weight_sum = summed[:, head_dim:]
        lse = biggest * scale + jnp.log2(weight_sum)
        lse = jnp.sum(jnp.where(tall == lane, lse, 0.0), axis=0, keepdims=True)
        high = lse.astype(jnp.bfloat16).astype(jnp.float32)
        middle = (lse - high).astype(jnp.bfloat16).astype(jnp.float32)
        low = lse - high - middle
        result = summed[:, :head_dim] / weight_sum
        for offset, piece in enumerate((high, middle, low)):
            result = jnp.where(tall == heads + offset, piece, result)
        out_ref[slot_ref[k]] = result.astype(jnp.bfloat16)

    def wait(k, _):
        for copy in copies(k):
            copy.wait()
        return 0

    lax.fori_loop(0, moves, wait, 0)
    batch = min(8, moves)

    def some_moves(b, _):
        for k in range(batch):
            one_move(b * batch + k)
        return 0

    lax.fori_loop(0, moves // batch, some_moves, 0)


def moved_attention(slots, pages, received, k_cache, v_cache, steps, heads, scale):
    moves = slots.shape[0]
    _, kv_heads, page, head_dim = k_cache.shape
    return pl.pallas_call(
        functools.partial(moved_kernel, steps=steps, heads=heads, scale=scale),
        in_specs=[
            smem(),
            smem(),
            pl.BlockSpec(memory_space=pltpu.VMEM),
            pl.BlockSpec(memory_space=pl.ANY),
            pl.BlockSpec(memory_space=pl.ANY),
        ],
        out_specs=pl.BlockSpec(memory_space=pltpu.VMEM),
        out_shape=jax.ShapeDtypeStruct(received.shape, jnp.bfloat16),
        scratch_shapes=[
            pltpu.VMEM((moves, kv_heads, page, head_dim), jnp.bfloat16),
            pltpu.VMEM((moves, kv_heads, page, head_dim), jnp.bfloat16),
            pltpu.SemaphoreType.DMA((2, moves)),
        ],
        compiler_params=pltpu.CompilerParams(vmem_limit_bytes=VMEM_LIMIT),
        cost_estimate=pl.CostEstimate(
            flops=4 * moves * 48 * 256 * 256,
            bytes_accessed=4 * moves * kv_heads * page * head_dim + 4 * received.size,
            transcendentals=moves * 48 * 256,
        ),
        name="moved_attention",
    )(slots, pages, received, k_cache, v_cache)


def final_kernel(
    owner_ref, landed_ref, q_ref, own_ref, other_ref, *refs, scale, local_count, per_group
):
    local = refs[: 2 * local_count]
    slot_ref, out_ref, new_ref, query, fresh, state, state_lse = refs[2 * local_count :]
    seqs, steps, heads, head_dim = q_ref.shape
    step_rows = padded(heads)
    slot_step, slot_size = slot_rows(steps, heads)
    stride = steps * step_rows
    spread = query.reshape(seqs * steps, step_rows, head_dim)
    spread[:, :heads, :] = q_ref[...].reshape(seqs * steps, heads, head_dim).astype(jnp.float32)
    new = own_ref[...]
    for k in range(other_ref.shape[0]):
        new = new + other_ref[k]
    new = new.astype(jnp.bfloat16)
    new_ref[...] = new
    for column in range(fresh.shape[0]):
        fresh[column] = new[:, column * head_dim : (column + 1) * head_dim].astype(jnp.float32)

    head = 0
    for part in range(local_count):
        out_part, lse_part = local[2 * part], local[2 * part + 1]
        for h in range(out_part.shape[0]):
            keys, values = [], []
            for j in range(steps):
                every = pl.ds(j, seqs, stride=steps)
                keys.append(fresh[2 * head, every, :])
                values.append(fresh[2 * head + 1, every, :])
            for i in range(steps):
                for g in range(per_group):
                    place = pl.ds(i * step_rows + head * per_group + g, seqs, stride=stride)
                    block = (i * per_group + g) * seqs
                    q = query[place, :]
                    lse = lse_part[h, block : block + seqs, :]
                    new_scores = [
                        jnp.sum(q * keys[j], axis=1, keepdims=True) * scale for j in range(i + 1)
                    ]
                    biggest = lse
                    for s in new_scores:
                        biggest = jnp.maximum(biggest, s)
                    weight = jnp.exp2(lse - biggest)
                    summed = weight * out_part[h, block : block + seqs, :]
                    for j, s in enumerate(new_scores):
                        w = jnp.exp2(s - biggest)
                        weight = weight + w
                        summed = summed + w * values[j]
                    state[place, :] = summed / weight
                    state_lse[place, :] = biggest + jnp.log2(weight)
            head += 1

    tall = lax.broadcasted_iota(jnp.int32, (slot_size, LANES), 0)
    lane = lax.broadcasted_iota(jnp.int32, (slot_size, LANES), 1)

    def one_slot(n, _):
        @pl.when(landed_ref[n] > 0)
        def _():
            block = slot_ref[n].astype(jnp.float32)
            packed = block[heads : heads + 1] + block[heads + 1 : heads + 2]
            packed = packed + block[heads + 2 : heads + 3]
            slot_lse = jnp.sum(jnp.where(tall == lane, packed, 0.0), axis=1, keepdims=True)
            for i in range(steps):
                place = pl.ds(owner_ref[n] * stride + i * step_rows, step_rows)
                rows = slice(i * slot_step, i * slot_step + step_rows)
                lse = state_lse[place, :]
                biggest = jnp.maximum(lse, slot_lse[rows])
                old = jnp.exp2(lse - biggest)
                come = jnp.exp2(slot_lse[rows] - biggest)
                weight = old + come
                state[place, :] = (old * state[place, :] + come * block[rows]) / weight
                state_lse[place, :] = biggest + jnp.log2(weight)

        return 0

    lax.fori_loop(0, slot_ref.shape[0], one_slot, 0)
    done = state.reshape(seqs * steps, step_rows, head_dim)[:, :heads, :]
    out_ref[...] = done.astype(jnp.bfloat16).reshape(out_ref.shape)


def finish(owner, landed, queries, own, other, local, slots, per_group, scale):
    seqs, steps, heads, head_dim = queries.shape
    flat = (seqs * steps * padded(heads), head_dim)
    vmem = pl.BlockSpec(memory_space=pltpu.VMEM)
    return pl.pallas_call(
        functools.partial(
            final_kernel, scale=scale, local_count=len(local) // 2, per_group=per_group
        ),
        in_specs=[smem(), smem()] + [vmem] * (4 + len(local)),
        out_specs=[vmem, vmem],
        out_shape=[
            jax.ShapeDtypeStruct(queries.shape, jnp.bfloat16),
            jax.ShapeDtypeStruct(own.shape, jnp.bfloat16),
        ],
        scratch_shapes=[
            pltpu.VMEM(flat, jnp.float32),
            pltpu.VMEM((own.shape[1] // head_dim, own.shape[0], head_dim), jnp.float32),
            pltpu.VMEM(flat, jnp.float32),
            pltpu.VMEM(flat, jnp.float32),
        ],
        compiler_params=pltpu.CompilerParams(vmem_limit_bytes=VMEM_LIMIT),
        cost_estimate=pl.CostEstimate(
            flops=40 * queries.size, bytes_accessed=16 * queries.size, transcendentals=0
        ),
        name="combine",
    )(owner, landed, queries, own, other, *local, slots)


def per_device(
    tokens_in, w_kv, queries, k_cache, v_cache, page_table, lengths, move_dest, move_page, move_seq
):
    groups = lax.axis_size("gen")
    me = lax.axis_index("gen").astype(jnp.int32)
    tp = lax.axis_size("tp")
    tp_index = lax.axis_index("tp")
    seqs, steps, heads, head_dim = queries.shape
    kv_heads = k_cache.shape[1]
    per_group = heads // kv_heads
    per_source = move_dest.shape[0] // groups
    scale = LOG2E / math.sqrt(head_dim)

    def exchange(array):
        return lax.all_to_all(array, "gen", split_axis=0, concat_axis=0, tiled=True)

    owner, landed, slots, to_send = gather(
        move_dest.reshape(-1), move_seq, me.reshape(1), queries, groups
    )
    received = exchange(to_send)
    own, partial = project(tokens_in, w_kv, tp, tp_index)
    pieces = []
    for k in range(1, tp):
        pairs = [(i, (i + k) % tp) for i in range(tp)]
        pieces.append(lax.ppermute(partial[k - 1], "tp", pairs))
    other = jnp.stack(pieces)

    lengths_row = lengths.reshape(1, seqs)
    early = max(1, kv_heads // 2)
    local = list(
        local_attention(queries, k_cache, v_cache, page_table, lengths_row, 0, early, scale)
    )
    pages = lax.dynamic_slice_in_dim(move_page, me * per_source, per_source, 0)
    received, local[0] = lax.optimization_barrier((received, local[0]))
    answers = moved_attention(slots, pages, received, k_cache, v_cache, steps, heads, scale)
    if early < kv_heads:
        late_queries, answers = lax.optimization_barrier((queries, answers))
        local += list(
            local_attention(
                late_queries, k_cache, v_cache, page_table, lengths_row, early, kv_heads - early,
                scale,
            )
        )
    returned = exchange(answers)
    attended, new_kv = finish(owner, landed, queries, own, other, local, returned, per_group, scale)
    return (attended, new_kv)


def solution(mesh):
    return jax.shard_map(
        per_device,
        mesh=mesh,
        in_specs=(
            P("gen", "tp"),
            P("tp", None),
            P("gen", None, "tp", None),
            P("gen", "tp", None, None),
            P("gen", "tp", None, None),
            P("gen", None),
            P("gen"),
            P(),
            P(),
            P(),
        ),
        out_specs=(P("gen", None, "tp", None), P("gen", "tp")),
        check_vma=False,
    )
```

```python
import functools
import math

import jax
import jax.numpy as jnp
from jax import lax
from jax.experimental import pallas as pl
from jax.experimental.pallas import tpu as pltpu
from jax.sharding import PartitionSpec as P

CAP = 2
NEGATIVE = -1e30
LOG2E = 1.4426950408889634
LANES = 128
VMEM_LIMIT = 56 * 1024 * 1024


def smem():
    return pl.BlockSpec(memory_space=pltpu.SMEM)


def vmem():
    return pl.BlockSpec(memory_space=pltpu.VMEM)


def hbm():
    return pl.BlockSpec(memory_space=pl.ANY)


def answer_rows(rows):
    return (rows + 3 + 15) // 16 * 16


def gather_kernel(dest_ref, seq_ref, me_ref, q_ref, owner_ref, slot_ref, out_ref, *, groups):
    me = me_ref[0]
    slots = groups * CAP
    per_source = slot_ref.shape[0]

    def clear(n, _):
        owner_ref[n] = -1
        return 0

    lax.fori_loop(0, slots, clear, 0, unroll=8)

    def one_source(src, _):
        count = jnp.int32(0)
        for k in range(per_source):
            row = src * per_source + k
            hit = dest_ref[row] == me
            owner_ref[jnp.where(hit, src * CAP + count, slots)] = seq_ref[row]
            count = count + hit.astype(jnp.int32)
        return 0

    lax.fori_loop(0, groups, one_source, 0)

    def one_slot(n, _):
        out_ref[n] = q_ref[jnp.maximum(owner_ref[n], 0)]
        return 0

    lax.fori_loop(0, slots, one_slot, 0, unroll=8)

    for k in range(per_source):
        mine = dest_ref[me * per_source + k]
        rank = jnp.int32(0)
        for j in range(k):
            rank = rank + (dest_ref[me * per_source + j] == mine).astype(jnp.int32)
        slot_ref[k] = mine * CAP + rank


def gather(dest, seq, me, queries, groups):
    per_source = dest.shape[0] // groups
    slots = groups * CAP
    seqs, rows, head_dim = queries.shape
    return pl.pallas_call(
        functools.partial(gather_kernel, groups=groups),
        in_specs=[smem(), smem(), smem(), vmem()],
        out_specs=[smem(), smem(), vmem()],
        out_shape=[
            jax.ShapeDtypeStruct((slots + 1,), jnp.int32),
            jax.ShapeDtypeStruct((per_source,), jnp.int32),
            jax.ShapeDtypeStruct((slots, rows, head_dim), jnp.bfloat16),
        ],
        compiler_params=pltpu.CompilerParams(vmem_limit_bytes=VMEM_LIMIT),
        cost_estimate=pl.CostEstimate(flops=0, bytes_accessed=4 * queries.size, transcendentals=0),
        name="gather_queries",
    )(dest, seq, me, queries)


def make_bias(table_ref, length_ref, bias, page):
    blocks, seqs, width = bias.shape
    pool = 64
    lengths = length_ref[...].astype(jnp.float32)
    page_id = lax.broadcasted_iota(jnp.int32, (pool, seqs), 0)
    used = jnp.zeros((pool, seqs), jnp.float32)
    for j in range(table_ref.shape[0]):
        inside = jnp.clip(lengths - float(page * j), 0.0, float(page))
        used = used + jnp.where(table_ref[j : j + 1, :] == page_id, inside, 0.0)
    used = used.T.astype(jnp.bfloat16)

    def one_block(b, _):
        key = lax.broadcasted_iota(jnp.int32, (pool, width), 1) + b * width
        owner = lax.broadcasted_iota(jnp.int32, (pool, width), 0)
        expand = jnp.where(key // page == owner, 1.0, 0.0).astype(jnp.bfloat16)
        count = jnp.dot(used, expand, preferred_element_type=jnp.float32)
        position = lax.broadcasted_iota(jnp.int32, (seqs, width), 1) % page
        bias[b] = jnp.where(position.astype(jnp.float32) < count, 0.0, NEGATIVE)
        return 0

    lax.fori_loop(0, blocks, one_block, 0)


class Attend:
    def __init__(self, query, bias, keys, values, scores, tops, packed, total, scale, per_head):
        self.query, self.bias, self.keys, self.values = query, bias, keys, values
        self.scores, self.tops, self.packed, self.total = scores, tops, packed, total
        self.scale, self.per_head = scale, per_head
        self.blocks, self.seqs, self.width = bias.shape
        self.head_dim = query.shape[1]
        self.stride = query.shape[0] // self.seqs
        self.rows = per_head * self.seqs
        self.pages = self.width // keys.shape[2]

    def start_scores(self, h, head):
        for r in range(self.per_head):
            rows = self.query[pl.ds(head * self.per_head + r, self.seqs, stride=self.stride), :]
            self.packed[pl.ds(r * self.seqs, self.seqs), :] = rows.astype(jnp.bfloat16)
        self.tops[h % 2][...] = jnp.full(self.tops[0].shape, NEGATIVE, jnp.float32)

    def score_block(self, h, b):
        top = self.tops[h % 2]
        keys = self.keys[h, pl.ds(b * self.pages, self.pages)].reshape(self.width, self.head_dim)
        s = lax.dot_general(
            self.packed[...], keys, (((1,), (1,)), ((), ())), preferred_element_type=jnp.float32
        )
        s = s.reshape(self.per_head, self.seqs, self.width) + self.bias[b][None]
        s = s.reshape(self.rows, self.width)
        self.scores[h % 2][b] = s
        largest = s[:, :LANES]
        for t in range(1, self.width // LANES):
            largest = jnp.maximum(largest, s[:, t * LANES : (t + 1) * LANES])
        top[...] = jnp.maximum(top[...], largest)

    def start_values(self, h):
        top = self.tops[h % 2]
        top[...] = jnp.broadcast_to(jnp.max(top[...], axis=1, keepdims=True), top.shape)
        self.total[...] = jnp.zeros(self.total.shape, jnp.float32)

    def value_block(self, h, b):
        scores, biggest = self.scores[h % 2], self.tops[h % 2][...]
        values = self.values[h, pl.ds(b * self.pages, self.pages)]
        values = values.reshape(self.width, self.head_dim)
        ones = jnp.ones((self.width, self.head_dim), jnp.bfloat16)
        weights = []
        for t in range(self.width // LANES):
            s = scores[b, :, t * LANES : (t + 1) * LANES]
            weights.append(jnp.exp2((s - biggest) * self.scale).astype(jnp.bfloat16))
        self.total[...] += jnp.dot(
            jnp.concatenate(weights, axis=1),
            jnp.concatenate([values, ones], axis=1),
            preferred_element_type=jnp.float32,
        )

    def run(self, first, count, ready, take):
        for h in range(count + 1):
            if h < count:
                ready(h)
                self.start_scores(h, first + h)
            if h > 0:
                self.start_values(h - 1)

            def one_block(b, _, h=h):
                if h < count:
                    self.score_block(h, b)
                if h > 0:
                    self.value_block(h - 1, b)
                return 0

            lax.fori_loop(0, self.blocks, one_block, 0)
            if h > 0:
                take(h - 1)


def cache_copies(k_hbm, v_hbm, keys, values, sems, first):
    def copies(h):
        return (
            pltpu.make_async_copy(k_hbm.at[:, first + h], keys.at[h], sems.at[0, h]),
            pltpu.make_async_copy(v_hbm.at[:, first + h], values.at[h], sems.at[1, h]),
        )

    return copies


def attend_scratch(count, pool, page, head_dim, seqs, per_head, stride):
    keys = pool * page
    width = keys // 2
    rows = per_head * seqs
    slots = max(count, 1)
    return [
        pltpu.VMEM((seqs * stride, head_dim), jnp.bfloat16),
        pltpu.VMEM((seqs * stride, head_dim), jnp.float32),
        pltpu.VMEM((keys // width, seqs, width), jnp.float32),
        pltpu.VMEM((slots, pool, page, head_dim), jnp.bfloat16),
        pltpu.VMEM((slots, pool, page, head_dim), jnp.bfloat16),
        pltpu.VMEM((keys // width, rows, width), jnp.float32),
        pltpu.VMEM((keys // width, rows, width), jnp.float32),
        pltpu.VMEM((rows, LANES), jnp.float32),
        pltpu.VMEM((rows, LANES), jnp.float32),
        pltpu.VMEM((rows, head_dim), jnp.bfloat16),
        pltpu.VMEM((rows, 2 * head_dim), jnp.float32),
        pltpu.SemaphoreType.DMA((2, slots)),
        pltpu.SemaphoreType.DMA((1,)),
    ]


def early_kernel(
    place_ref, table_ref, length_ref, q_hbm, k_hbm, v_hbm, x_hbm, w_hbm, *refs,
    tp, scale, count, per_head,
):
    outs = 2 if count else 0
    local, (own_ref, send_ref) = refs[:outs], refs[outs : outs + 2]
    (x, w, x_sem, w_sems, raw, query, bias, keys, values, s0, s1, t0, t1, packed, total,
     sems, q_sem) = refs[outs + 2 :]
    blocks, _, width = w.shape
    copies = cache_copies(k_hbm, v_hbm, keys, values, sems, 0)
    x_copy = pltpu.make_async_copy(x_hbm, x, x_sem.at[0])
    per_owner = blocks // tp

    def w_copy(b):
        owner = lax.rem(place_ref[0] + b // per_owner, tp)
        first = pl.multiple_of((owner * per_owner + b % per_owner) * width, width)
        return pltpu.make_async_copy(w_hbm.at[:, pl.ds(first, width)], w.at[b], w_sems.at[b])

    if count:
        q_copy = pltpu.make_async_copy(q_hbm, raw, q_sem.at[0])
        q_copy.start()
        for h in range(count):
            for copy in copies(h):
                copy.start()
    x_copy.start()
    for b in range(blocks):
        w_copy(b).start()
    if count:
        make_bias(table_ref, length_ref, bias, keys.shape[2])
        q_copy.wait()
        query[...] = raw[...].astype(jnp.float32)
        attend = Attend(
            query, bias, keys, values, (s0, s1), (t0, t1), packed, total, scale, per_head
        )

        def ready(h):
            for copy in copies(h):
                copy.wait()

        def take(h):
            weight_sum = total[:, keys.shape[3] :]
            local[0][h] = total[:, : keys.shape[3]] / weight_sum
            local[1][h] = attend.tops[h % 2][...] * scale + jnp.log2(weight_sum)

        attend.run(0, count, ready, take)
    x_copy.wait()
    for b in range(blocks):
        w_copy(b).wait()
        product = jnp.dot(x[...], w[b], preferred_element_type=jnp.float32)
        part = slice(b % per_owner * width, (b % per_owner + 1) * width)
        if b < per_owner:
            own_ref[:, part] = product
        else:
            send_ref[b // per_owner - 1, :, part] = product


def early_work(place, table, lengths, queries, k_cache, v_cache, tokens, w_kv, tp, count, scale):
    seqs, stride, head_dim = queries.shape
    pool, kv_heads, page, _ = k_cache.shape
    per_head = stride // kv_heads
    rows, depth = tokens.shape
    columns = w_kv.shape[1] // tp
    width = min(256, columns)
    local_shape = jax.ShapeDtypeStruct((count, per_head * seqs, head_dim), jnp.float32)
    local = [local_shape, local_shape] if count else []
    return pl.pallas_call(
        functools.partial(early_kernel, tp=tp, scale=scale, count=count, per_head=per_head),
        in_specs=[smem(), vmem(), vmem()] + [hbm()] * 5,
        out_specs=[vmem()] * (len(local) + 2),
        out_shape=local + [
            jax.ShapeDtypeStruct((rows, columns), jnp.float32),
            jax.ShapeDtypeStruct((tp - 1, rows, columns), jnp.float32),
        ],
        scratch_shapes=[
            pltpu.VMEM((rows, depth), jnp.bfloat16),
            pltpu.VMEM((w_kv.shape[1] // width, depth, width), jnp.bfloat16),
            pltpu.SemaphoreType.DMA((1,)),
            pltpu.SemaphoreType.DMA((w_kv.shape[1] // width,)),
        ] + attend_scratch(count, pool, page, head_dim, seqs, per_head, stride),
        compiler_params=pltpu.CompilerParams(vmem_limit_bytes=VMEM_LIMIT),
        cost_estimate=pl.CostEstimate(
            flops=2 * tokens.size * w_kv.shape[1] + 8 * count * per_head * seqs * pool * page * head_dim,
            bytes_accessed=2 * w_kv.size + 4 * count * pool * page * head_dim,
            transcendentals=count * per_head * seqs * pool * page,
        ),
        name="early_heads_and_new_kv",
    )(place, table, lengths, queries.reshape(seqs * stride, head_dim), k_cache, v_cache, tokens, w_kv)


def late_kernel(
    table_ref, length_ref, own_ref, other_ref, q_hbm, k_hbm, v_hbm, *refs,
    scale, early, count, per_head, steps,
):
    ins = 2 if early else 0
    before, (state, state_lse, new_ref) = refs[:ins], refs[ins : ins + 3]
    (fresh, raw, query, bias, keys, values, s0, s1, t0, t1, packed, total,
     sems, q_sem) = refs[ins + 3 :]
    head_dim = keys.shape[3]
    seqs = bias.shape[1]
    stride = query.shape[0] // seqs
    copies = cache_copies(k_hbm, v_hbm, keys, values, sems, early)
    q_copy = pltpu.make_async_copy(q_hbm, raw, q_sem.at[0])
    q_copy.start()
    for h in range(count):
        for copy in copies(h):
            copy.start()
    make_bias(table_ref, length_ref, bias, keys.shape[2])
    q_copy.wait()
    query[...] = raw[...].astype(jnp.float32)
    new = own_ref[...]
    for k in range(other_ref.shape[0]):
        new = new + other_ref[k]
    new = new.astype(jnp.bfloat16)
    new_ref[...] = new
    for column in range(fresh.shape[0]):
        fresh[column] = new[:, column * head_dim : (column + 1) * head_dim].astype(jnp.float32)

    def join(head, part):
        new_keys, new_values = [], []
        for j in range(steps):
            every = pl.ds(j, seqs, stride=steps)
            new_keys.append(fresh[2 * head, every, :])
            new_values.append(fresh[2 * head + 1, every, :])
        for r in range(per_head):
            place = pl.ds(head * per_head + r, seqs, stride=stride)
            biggest, weight, summed = part(pl.ds(r * seqs, seqs))
            q = query[place, :]
            new_scores = [
                jnp.sum(q * new_keys[j], axis=1, keepdims=True) * scale
                for j in range(r % steps + 1)
            ]
            top = biggest
            for s in new_scores:
                top = jnp.maximum(top, s)
            factor = jnp.exp2(biggest - top)
            weight = factor * weight
            summed = factor * summed
            for j, s in enumerate(new_scores):
                w = jnp.exp2(s - top)
                weight = weight + w
                summed = summed + w * new_values[j]
            state[place, :] = summed / weight
            state_lse[place, :] = top + jnp.log2(weight)

    for h in range(early):
        join(h, lambda rows, h=h: (before[1][h, rows, :], 1.0, before[0][h, rows, :]))
    attend = Attend(query, bias, keys, values, (s0, s1), (t0, t1), packed, total, scale, per_head)

    def ready(h):
        for copy in copies(h):
            copy.wait()

    def take(h):
        top = attend.tops[h % 2]
        join(
            early + h,
            lambda rows: (top[rows, :] * scale, total[rows, head_dim:], total[rows, :head_dim]),
        )

    attend.run(early, count, ready, take)


def late_work(table, lengths, own, other, queries, k_cache, v_cache, before, steps, early, scale):
    seqs, stride, head_dim = queries.shape
    pool, kv_heads, page, _ = k_cache.shape
    per_head = stride // kv_heads
    count = kv_heads - early
    state = jax.ShapeDtypeStruct((seqs * stride, head_dim), jnp.float32)
    return pl.pallas_call(
        functools.partial(
            late_kernel, scale=scale, early=early, count=count, per_head=per_head, steps=steps
        ),
        in_specs=[vmem()] * 4 + [hbm()] * 3 + [vmem()] * len(before),
        out_specs=[vmem()] * 3,
        out_shape=[state, state, jax.ShapeDtypeStruct(own.shape, jnp.bfloat16)],
        scratch_shapes=[
            pltpu.VMEM((own.shape[1] // head_dim, own.shape[0], head_dim), jnp.float32)
        ] + attend_scratch(count, pool, page, head_dim, seqs, per_head, stride),
        compiler_params=pltpu.CompilerParams(vmem_limit_bytes=VMEM_LIMIT),
        cost_estimate=pl.CostEstimate(
            flops=8 * count * per_head * seqs * pool * page * head_dim,
            bytes_accessed=4 * count * pool * page * head_dim + 8 * seqs * stride * head_dim,
            transcendentals=count * per_head * seqs * pool * page,
        ),
        name="late_heads_and_new_keys",
    )(
        table, lengths, own, other, queries.reshape(seqs * stride, head_dim), k_cache, v_cache,
        *before,
    )


def moved_kernel(
    slot_ref, page_ref, me_ref, q_ref, k_hbm, v_hbm, out_ref, keys, values, sems, *, scale
):
    moves, kv_heads, page, head_dim = keys.shape
    rows = q_ref.shape[1]
    padding = out_ref.shape[1] - rows
    columns = kv_heads * page

    def copies(k):
        source = page_ref[me_ref[0] * moves + k]
        return (
            pltpu.make_async_copy(k_hbm.at[source], keys.at[k], sems.at[0, k]),
            pltpu.make_async_copy(v_hbm.at[source], values.at[k], sems.at[1, k]),
        )

    def start(k, _):
        for copy in copies(k):
            copy.start()
        return 0

    lax.fori_loop(0, moves, start, 0)
    out_ref[...] = jnp.zeros(out_ref.shape, jnp.bfloat16)
    row = lax.broadcasted_iota(jnp.int32, (rows, columns), 0)
    column = lax.broadcasted_iota(jnp.int32, (rows, columns), 1)
    other_head = jnp.where(row // (rows // kv_heads) == column // page, 0.0, NEGATIVE)
    tall = lax.broadcasted_iota(jnp.int32, (rows, LANES), 0)
    lane = lax.broadcasted_iota(jnp.int32, (rows, LANES), 1)
    spare = lax.broadcasted_iota(jnp.int32, (padding, LANES), 0)
    ones = jnp.ones((columns, head_dim), jnp.bfloat16)

    def one_move(k):
        s = lax.dot_general(
            q_ref[slot_ref[k]],
            keys[k].reshape(columns, head_dim),
            (((1,), (1,)), ((), ())),
            preferred_element_type=jnp.float32,
        )
        s = s + other_head
        biggest = jnp.max(s, axis=1, keepdims=True)
        weights = jnp.exp2((s - biggest) * scale).astype(jnp.bfloat16)
        both = jnp.concatenate([values[k].reshape(columns, head_dim), ones], axis=1)
        summed = jnp.dot(weights, both, preferred_element_type=jnp.float32)
        weight_sum = summed[:, head_dim:]
        lse = biggest * scale + jnp.log2(weight_sum)
        lse = jnp.sum(jnp.where(tall == lane, lse, 0.0), axis=0, keepdims=True)
        high = lse.astype(jnp.bfloat16).astype(jnp.float32)
        middle = (lse - high).astype(jnp.bfloat16).astype(jnp.float32)
        low = lse - high - middle
        pieces = jnp.where(spare == 0, high, jnp.where(spare == 1, middle, low))
        result = jnp.concatenate([summed[:, :head_dim] / weight_sum, pieces], axis=0)
        out_ref[slot_ref[k]] = result.astype(jnp.bfloat16)

    def wait(k, _):
        for copy in copies(k):
            copy.wait()
        return 0

    lax.fori_loop(0, moves, wait, 0)
    batch = min(8, moves)

    def some_moves(b, _):
        for k in range(batch):
            one_move(b * batch + k)
        return 0

    lax.fori_loop(0, moves // batch, some_moves, 0)


def moved_attention(slots, pages, me, received, k_cache, v_cache, scale):
    moves = slots.shape[0]
    _, kv_heads, page, head_dim = k_cache.shape
    count, rows, _ = received.shape
    return pl.pallas_call(
        functools.partial(moved_kernel, scale=scale),
        in_specs=[smem(), smem(), smem(), vmem(), hbm(), hbm()],
        out_specs=vmem(),
        out_shape=jax.ShapeDtypeStruct((count, answer_rows(rows), head_dim), jnp.bfloat16),
        scratch_shapes=[
            pltpu.VMEM((moves, kv_heads, page, head_dim), jnp.bfloat16),
            pltpu.VMEM((moves, kv_heads, page, head_dim), jnp.bfloat16),
            pltpu.SemaphoreType.DMA((2, moves)),
        ],
        compiler_params=pltpu.CompilerParams(vmem_limit_bytes=VMEM_LIMIT),
        cost_estimate=pl.CostEstimate(
            flops=4 * moves * rows * kv_heads * page * head_dim,
            bytes_accessed=4 * moves * kv_heads * page * head_dim + 4 * received.size,
            transcendentals=moves * rows * kv_heads * page,
        ),
        name="moved_attention",
    )(slots, pages, me, received, k_cache, v_cache)


def join_kernel(owner_ref, state_ref, lse_ref, slot_ref, out_ref, state, state_lse):
    rows = out_ref.shape[1]
    slot_size = slot_ref.shape[1]
    state[...] = state_ref[...]
    state_lse[...] = lse_ref[...]
    tall = lax.broadcasted_iota(jnp.int32, (rows, LANES), 0)
    lane = lax.broadcasted_iota(jnp.int32, (rows, LANES), 1)

    def one_slot(n, _):
        @pl.when(owner_ref[n] >= 0)
        def _():
            seq = owner_ref[n]
            block = slot_ref[n].astype(jnp.float32)
            packed = block[rows : rows + 1] + block[rows + 1 : rows + 2] + block[rows + 2 : rows + 3]
            come_lse = jnp.sum(jnp.where(tall == lane, packed, 0.0), axis=1, keepdims=True)
            lse = state_lse[seq]
            top = jnp.maximum(lse, come_lse)
            old = jnp.exp2(lse - top)
            come = jnp.exp2(come_lse - top)
            weight = old + come
            state[seq] = (old * state[seq] + come * block[:rows]) / weight
            state_lse[seq] = top + jnp.log2(weight)

        return 0

    lax.fori_loop(0, slot_ref.shape[0], one_slot, 0)
    out_ref[...] = state[...].astype(jnp.bfloat16)


def join_moved(owner, state, state_lse, answers, seqs):
    shape = (seqs, state.shape[0] // seqs, state.shape[1])
    return pl.pallas_call(
        join_kernel,
        in_specs=[smem()] + [vmem()] * 3,
        out_specs=vmem(),
        out_shape=jax.ShapeDtypeStruct(shape, jnp.bfloat16),
        scratch_shapes=[pltpu.VMEM(shape, jnp.float32), pltpu.VMEM(shape, jnp.float32)],
        compiler_params=pltpu.CompilerParams(vmem_limit_bytes=VMEM_LIMIT),
        cost_estimate=pl.CostEstimate(
            flops=10 * state.size, bytes_accessed=10 * state.size, transcendentals=0
        ),
        name="join_moved",
    )(owner, state.reshape(shape), state_lse.reshape(shape), answers)


def per_device(
    tokens_in, w_kv, queries, k_cache, v_cache, page_table, lengths, move_dest, move_page, move_seq
):
    groups = lax.axis_size("gen")
    me = lax.axis_index("gen").astype(jnp.int32).reshape(1)
    tp = lax.axis_size("tp")
    place = lax.axis_index("tp").astype(jnp.int32).reshape(1)
    seqs, steps, heads, head_dim = queries.shape
    kv_heads = k_cache.shape[1]
    scale = LOG2E / math.sqrt(head_dim)

    def exchange(array):
        return lax.all_to_all(array, "gen", split_axis=0, concat_axis=0, tiled=True)

    rows = queries.transpose(0, 2, 1, 3).reshape(seqs, heads * steps, head_dim)
    table = page_table.T
    lengths = lengths.reshape(1, seqs)
    owner, slots, to_send = gather(move_dest.reshape(-1), move_seq, me, rows, groups)
    early = kv_heads // 4
    early_rows, to_send = lax.optimization_barrier((rows, to_send))
    received = exchange(to_send)
    *before, own, partial = early_work(
        place, table, lengths, early_rows, k_cache, v_cache, tokens_in, w_kv, tp, early, scale
    )
    pieces = []
    for k in range(1, tp):
        pairs = [(i, (i + k) % tp) for i in range(tp)]
        pieces.append(lax.ppermute(partial[k - 1], "tp", pairs))
    other = jnp.stack(pieces)
    received, own = lax.optimization_barrier((received, own))
    answers = moved_attention(slots, move_page, me, received, k_cache, v_cache, scale)
    late_rows, answers = lax.optimization_barrier((rows, answers))
    returned = exchange(answers)
    state, state_lse, new_kv = late_work(
        table, lengths, own, other, late_rows, k_cache, v_cache, before, steps, early, scale
    )
    attended = join_moved(owner, state, state_lse, returned, seqs)
    attended = attended.reshape(seqs, heads, steps, head_dim).transpose(0, 2, 1, 3)
    return (attended, new_kv)


def solution(mesh):
    return jax.shard_map(
        per_device,
        mesh=mesh,
        in_specs=(
            P("gen", "tp"),
            P("tp", None),
            P("gen", None, "tp", None),
            P("gen", "tp", None, None),
            P("gen", "tp", None, None),
            P("gen", None),
            P("gen"),
            P(),
            P(),
            P(),
        ),
        out_specs=(P("gen", None, "tp", None), P("gen", "tp")),
        check_vma=False,
    )
```

```python
import functools
import math

import jax
import jax.numpy as jnp
from jax import lax
from jax.experimental import pallas as pl
from jax.experimental.pallas import tpu as pltpu
from jax.sharding import PartitionSpec as P

CAP = 2
NEGATIVE = -1e30
LOG2E = 1.4426950408889634
LANES = 128
MIB = 1024 * 1024


def smem():
    return pl.BlockSpec(memory_space=pltpu.SMEM)


def vmem():
    return pl.BlockSpec(memory_space=pltpu.VMEM)


def hbm():
    return pl.BlockSpec(memory_space=pltpu.HBM)


def stay(array):
    return pltpu.with_memory_space_constraint(array, pltpu.HBM)


def limit(mib):
    return pltpu.CompilerParams(vmem_limit_bytes=mib * MIB)


def padded(rows):
    return (rows + 7) // 8 * 8


def answer_rows(rows):
    return (rows + 3 + 15) // 16 * 16


def fill_owner(dest, seq, me, owner, per_source):
    groups = dest.shape[0] // per_source
    slots = groups * CAP

    def clear(n, _):
        owner[n] = -1
        return 0

    lax.fori_loop(0, slots, clear, 0, unroll=8)

    def one_source(source, _):
        count = jnp.int32(0)
        for k in range(per_source):
            row = source * per_source + k
            hit = dest[row] == me
            owner[jnp.where(hit, source * CAP + count, slots)] = seq[row]
            count = count + hit.astype(jnp.int32)
        return 0

    lax.fori_loop(0, groups, one_source, 0)


def first_slots(owner, first, seen):
    def unseen(n, _):
        seen[n] = -1
        return 0

    lax.fori_loop(0, seen.shape[0], unseen, 0, unroll=8)

    def first_slot(n, _):
        sequence = owner[n]
        place = jnp.maximum(sequence, 0)
        earlier = seen[place]
        mine = jnp.where(earlier < 0, n, earlier)
        seen[place] = jnp.where(sequence < 0, earlier, mine)
        first[n] = jnp.where(sequence < 0, -1, mine)
        return 0

    lax.fori_loop(0, first.shape[0], first_slot, 0)


def gather_kernel(
    dest_hbm, seq_hbm, q_hbm, out_ref, dest, seq, owner, queries, sems, *, per_source
):
    me = lax.axis_index("gen")
    copies = [
        pltpu.make_async_copy(dest_hbm, dest, sems.at[0]),
        pltpu.make_async_copy(seq_hbm, seq, sems.at[1]),
        pltpu.make_async_copy(q_hbm, queries, sems.at[2]),
    ]
    for copy in copies:
        copy.start()
    copies[0].wait()
    copies[1].wait()
    fill_owner(dest, seq, me, owner, per_source)
    copies[2].wait()

    def one_slot(n, _):
        out_ref[n] = queries[jnp.maximum(owner[n], 0)]
        return 0

    lax.fori_loop(0, out_ref.shape[0], one_slot, 0, unroll=8)


def gather(dest, seq, queries, groups):
    slots = groups * CAP
    _, rows, head_dim = queries.shape
    return pl.pallas_call(
        functools.partial(gather_kernel, per_source=dest.shape[0] // groups),
        in_specs=[hbm()] * 3,
        out_specs=vmem(),
        out_shape=jax.ShapeDtypeStruct((slots, rows, head_dim), jnp.bfloat16),
        scratch_shapes=[
            pltpu.SMEM(dest.shape, jnp.int32),
            pltpu.SMEM(seq.shape, jnp.int32),
            pltpu.SMEM((slots + 1,), jnp.int32),
            pltpu.VMEM(queries.shape, jnp.bfloat16),
            pltpu.SemaphoreType.DMA((3,)),
        ],
        compiler_params=limit(4),
        cost_estimate=pl.CostEstimate(flops=0, bytes_accessed=4 * queries.size, transcendentals=0),
        name="gather_queries",
    )(stay(dest), stay(seq), stay(queries))


def make_bias(table_ref, length_ref, bias, page):
    blocks, seqs, width = bias.shape
    pool = padded(blocks * width // page)
    lengths = length_ref[...].astype(jnp.float32)
    page_id = lax.broadcasted_iota(jnp.int32, (pool, seqs), 0)
    used = jnp.zeros((pool, seqs), jnp.float32)
    for j in range(table_ref.shape[0]):
        inside = jnp.clip(lengths - float(page * j), 0.0, float(page))
        used = used + jnp.where(table_ref[j : j + 1, :] == page_id, inside, 0.0)
    used = used.T.astype(jnp.bfloat16)

    def one_block(b, _):
        key = lax.broadcasted_iota(jnp.int32, (pool, width), 1) + b * width
        owner = lax.broadcasted_iota(jnp.int32, (pool, width), 0)
        expand = jnp.where(key // page == owner, 1.0, 0.0).astype(jnp.bfloat16)
        count = jnp.dot(used, expand, preferred_element_type=jnp.float32)
        position = lax.broadcasted_iota(jnp.int32, (seqs, width), 1) % page
        bias[b] = jnp.where(position.astype(jnp.float32) < count, 0.0, NEGATIVE)
        return 0

    lax.fori_loop(0, blocks, one_block, 0)


class Attend:
    def __init__(self, query, bias, keys, values, scores, tops, packed, total, scale, per_head):
        self.query, self.bias, self.keys, self.values = query, bias, keys, values
        self.scores, self.tops, self.packed, self.total = scores, tops, packed, total
        self.scale, self.per_head = scale, per_head
        self.blocks, self.seqs, self.width = bias.shape
        self.head_dim = query.shape[1]
        self.stride = query.shape[0] // self.seqs
        self.rows = per_head * self.seqs
        self.pages = self.width // keys.shape[2]

    def start_scores(self, h, head):
        for r in range(self.per_head):
            rows = self.query[pl.ds(head * self.per_head + r, self.seqs, stride=self.stride), :]
            self.packed[pl.ds(r * self.seqs, self.seqs), :] = rows.astype(jnp.bfloat16)
        self.tops[h % 2][...] = jnp.full(self.tops[0].shape, NEGATIVE, jnp.float32)

    def product(self, keys):
        return lax.dot_general(
            self.packed[...], keys, (((1,), (1,)), ((), ())), preferred_element_type=jnp.float32
        )

    def score_block(self, h, b):
        top = self.tops[h % 2]
        keys = self.keys[h, pl.ds(b * self.pages, self.pages)].reshape(self.width, self.head_dim)
        s = self.product(keys).reshape(self.per_head, self.seqs, self.width) + self.bias[b][None]
        s = s.reshape(self.rows, self.width)
        self.scores[h % 2][b] = s
        largest = s[:, :LANES]
        for t in range(1, self.width // LANES):
            largest = jnp.maximum(largest, s[:, t * LANES : (t + 1) * LANES])
        top[...] = jnp.maximum(top[...], largest)

    def start_values(self, h):
        top = self.tops[h % 2]
        top[...] = jnp.broadcast_to(jnp.max(top[...], axis=1, keepdims=True), top.shape)
        self.total[...] = jnp.zeros(self.total.shape, jnp.float32)

    def weigh(self, weights, values):
        return jnp.dot(
            weights,
            jnp.concatenate([values, jnp.ones(values.shape, jnp.bfloat16)], axis=1),
            preferred_element_type=jnp.float32,
        )

    def value_block(self, h, b):
        scores, biggest = self.scores[h % 2], self.tops[h % 2][...]
        values = self.values[h, pl.ds(b * self.pages, self.pages)]
        weights = []
        for t in range(self.width // LANES):
            s = scores[b, :, t * LANES : (t + 1) * LANES]
            weights.append(jnp.exp2((s - biggest) * self.scale).astype(jnp.bfloat16))
        self.total[...] += self.weigh(
            jnp.concatenate(weights, axis=1), values.reshape(self.width, self.head_dim)
        )

    def run(self, first, count, keys_ready, values_ready, take):
        for h in range(count + 1):
            if h < count:
                keys_ready(h)
                self.start_scores(h, first + h)
            if h > 0:
                values_ready(h - 1)
                self.start_values(h - 1)

            def one_block(b, _, h=h):
                if h < count:
                    self.score_block(h, b)
                if h > 0:
                    self.value_block(h - 1, b)
                return 0

            lax.fori_loop(0, self.blocks, one_block, 0)
            if h > 0:
                take(h - 1)


def attend_scratch(seqs, per_head, pool, page, head_dim, pairs):
    keys = pool * page
    width = keys // 2
    rows = per_head * seqs
    scores = [pltpu.VMEM((keys // width, rows, width), jnp.float32) for _ in range(pairs)]
    tops = [pltpu.VMEM((rows, LANES), jnp.float32) for _ in range(pairs)]
    return scores + tops + [
        pltpu.VMEM((rows, head_dim), jnp.bfloat16),
        pltpu.VMEM((rows, 2 * head_dim), jnp.float32),
    ]


def start_all(copies):
    for copy in copies:
        copy.start()


def wait_all(copies):
    for copy in copies:
        copy.wait()


def early_kernel(
    table_hbm, length_hbm, pages_hbm, q_hbm, x_hbm, dest_hbm, seq_hbm, k_hbm, v_hbm, w_hbm, *refs,
    tp, scale, count, per_head,
):
    outs = 2 if count else 0
    local_hbm = refs[:outs]
    own_hbm, owner_hbm, first_hbm, send_ref, move_keys, move_values = refs[outs : outs + 6]
    (table, lengths, pages, raw, query, bias, x, dest, seq, owner, first, seen, w, keys, values, own,
     small_sems, cache_sems, move_sems, w_sems, out_sems, *attend_refs) = refs[outs + 6 :]
    pairs = min(count, 2)
    scores, tops = attend_refs[:pairs], attend_refs[pairs : 2 * pairs]
    blocks, _, width = w.shape
    moves = move_keys.shape[0]
    head_dim = keys.shape[3]
    per_owner = blocks // tp
    me, place = lax.axis_index("gen"), lax.axis_index("tp")
    small = [
        pltpu.make_async_copy(source, target, small_sems.at[k])
        for k, (source, target) in enumerate(
            [(dest_hbm, dest), (seq_hbm, seq), (table_hbm, table), (length_hbm, lengths),
             (pages_hbm, pages), (q_hbm, raw), (x_hbm, x)]
        )
    ]
    own_copy = pltpu.make_async_copy(own, own_hbm, out_sems.at[2])
    table_copies = [
        pltpu.make_async_copy(owner, owner_hbm, out_sems.at[3]),
        pltpu.make_async_copy(first, first_hbm, out_sems.at[4]),
    ]

    def key_copy(h):
        return pltpu.make_async_copy(k_hbm.at[:, h], keys.at[h], cache_sems.at[0, h])

    def value_copy(h):
        return pltpu.make_async_copy(v_hbm.at[:, h], values.at[h], cache_sems.at[1, h])

    def w_copy(b):
        owner = lax.rem(place + b // per_owner, tp)
        start = pl.multiple_of((owner * per_owner + b % per_owner) * width, width)
        return pltpu.make_async_copy(w_hbm.at[:, pl.ds(start, width)], w.at[b], w_sems.at[b])

    def move_copies(k):
        page = pages[me * moves + k]
        return (
            pltpu.make_async_copy(k_hbm.at[page], move_keys.at[k], move_sems.at[0, k]),
            pltpu.make_async_copy(v_hbm.at[page], move_values.at[k], move_sems.at[1, k]),
        )

    def start_move(k, _):
        start_all(move_copies(k))
        return 0

    def wait_move(k, _):
        wait_all(move_copies(k))
        return 0

    def start_weights(first, last):
        for b in range(first, last):
            w_copy(b).start()

    start_all(small[:6])
    if count:
        key_copy(0).start()
    wait_all(small[:2])
    fill_owner(dest, seq, me, owner, moves)
    first_slots(owner, first, seen)
    start_all(table_copies)
    wait_all(small[2:6])
    if count:
        make_bias(table, lengths, bias, keys.shape[2])
        query[...] = raw[...].astype(jnp.float32)
        packed, total, out, out_lse = attend_refs[2 * pairs :]
        attend = Attend(query, bias, keys, values, scores, tops, packed, total, scale, per_head)
        local_copies = [
            pltpu.make_async_copy(out, local_hbm[0], out_sems.at[0]),
            pltpu.make_async_copy(out_lse, local_hbm[1], out_sems.at[1]),
        ]

        def keys_ready(h):
            key_copy(h).wait()
            value_copy(h).start()
            if h + 1 < count:
                key_copy(h + 1).start()
            if h == count - 1:
                small[6].start()
                start_weights(0, blocks // 2)

        def values_ready(h):
            value_copy(h).wait()
            if h == count - 1:
                start_weights(blocks // 2, blocks)
                lax.fori_loop(0, moves, start_move, 0)

        def take(h):
            weight_sum = total[:, head_dim:]
            out[h] = total[:, :head_dim] / weight_sum
            out_lse[h] = attend.tops[h % 2][...] * scale + jnp.log2(weight_sum)

        attend.run(0, count, keys_ready, values_ready, take)
        start_all(local_copies)
    else:
        small[6].start()
        start_weights(0, blocks)
        lax.fori_loop(0, moves, start_move, 0)
    small[6].wait()
    for b in range(blocks):
        w_copy(b).wait()
        product = jnp.dot(x[...], w[b], preferred_element_type=jnp.float32)
        part = slice(b % per_owner * width, (b % per_owner + 1) * width)
        if b < per_owner:
            own[:, part] = product
            if b == per_owner - 1:
                own_copy.start()
        else:
            send_ref[b // per_owner - 1, :, part] = product.astype(jnp.bfloat16)
    lax.fori_loop(0, moves, wait_move, 0)
    own_copy.wait()
    wait_all(table_copies)
    if count:
        wait_all(local_copies)


def early_work(
    table, lengths, pages, queries, tokens, dest, seq, k_cache, v_cache, w_kv, groups, tp, count, scale
):
    seqs, stride, head_dim = queries.shape
    pool, kv_heads, page, _ = k_cache.shape
    per_head = stride // kv_heads
    rows, depth = tokens.shape
    moves, slots = dest.shape[0] // groups, groups * CAP
    columns = w_kv.shape[1] // tp
    width = min(512, columns)
    blocks = w_kv.shape[1] // width
    keys = pool * page
    f32, bf16 = jnp.float32, jnp.bfloat16
    local_shape = (count, per_head * seqs, head_dim)
    local = [pltpu.HBM(local_shape, f32)] * 2 if count else []
    scratch = [
        pltpu.VMEM(table.shape, jnp.int32),
        pltpu.VMEM(lengths.shape, jnp.int32),
        pltpu.SMEM(pages.shape, jnp.int32),
        pltpu.VMEM((seqs * stride, head_dim), bf16),
        pltpu.VMEM((seqs * stride, head_dim), f32),
        pltpu.VMEM((2, seqs, keys // 2), f32),
        pltpu.VMEM((rows, depth), bf16),
        pltpu.SMEM(dest.shape, jnp.int32),
        pltpu.SMEM(seq.shape, jnp.int32),
        pltpu.SMEM((slots + 1,), jnp.int32),
        pltpu.SMEM((slots,), jnp.int32),
        pltpu.SMEM((seqs,), jnp.int32),
        pltpu.VMEM((blocks, depth, width), bf16),
        pltpu.VMEM((max(count, 1), pool, page, head_dim), bf16),
        pltpu.VMEM((max(count, 1), pool, page, head_dim), bf16),
        pltpu.VMEM((rows, columns), f32),
        pltpu.SemaphoreType.DMA((7,)),
        pltpu.SemaphoreType.DMA((2, max(count, 1))),
        pltpu.SemaphoreType.DMA((2, moves)),
        pltpu.SemaphoreType.DMA((blocks,)),
        pltpu.SemaphoreType.DMA((5,)),
    ]
    if count:
        scratch += attend_scratch(seqs, per_head, pool, page, head_dim, min(count, 2))
        scratch += [pltpu.VMEM(local_shape, f32)] * 2
    return pl.pallas_call(
        functools.partial(early_kernel, tp=tp, scale=scale, count=count, per_head=per_head),
        in_specs=[hbm()] * 10,
        out_specs=[hbm()] * (len(local) + 3) + [vmem()] * 3,
        out_shape=local + [
            pltpu.HBM((rows, columns), f32),
            pltpu.HBM((slots + 1,), jnp.int32),
            pltpu.HBM((slots,), jnp.int32),
            jax.ShapeDtypeStruct((tp - 1, rows, columns), bf16),
            jax.ShapeDtypeStruct((moves,) + k_cache.shape[1:], bf16),
            jax.ShapeDtypeStruct((moves,) + k_cache.shape[1:], bf16),
        ],
        scratch_shapes=scratch,
        compiler_params=limit(44),
        cost_estimate=pl.CostEstimate(
            flops=2 * tokens.size * w_kv.shape[1] + 8 * count * per_head * seqs * keys * head_dim,
            bytes_accessed=2 * w_kv.size + 4 * count * keys * head_dim,
            transcendentals=count * per_head * seqs * keys,
        ),
        name="early_heads_and_new_kv",
    )(
        stay(table), stay(lengths), stay(pages), stay(queries.reshape(seqs * stride, head_dim)),
        stay(tokens), stay(dest), stay(seq), stay(k_cache), stay(v_cache), stay(w_kv),
    )


def late_kernel(
    table_hbm, length_hbm, q_hbm, k_hbm, v_hbm, own_hbm, *refs, scale, early, count, per_head
):
    ins = 2 if early else 0
    before_hbm = refs[:ins]
    state, state_lse, query, own = refs[ins : ins + 4]
    table, lengths, raw, bias, keys, values, sems, cache_sems, *attend_refs = refs[ins + 4 :]
    pairs = min(count, 2)
    scores, tops = attend_refs[:pairs], attend_refs[pairs : 2 * pairs]
    packed, total = attend_refs[2 * pairs : 2 * pairs + 2]
    before = attend_refs[2 * pairs + 2 :]
    seqs, stride, head_dim = state.shape
    flat = (seqs * stride, head_dim)
    rows, rows_lse = state.reshape(flat), state_lse.reshape(flat)
    pairs_in = [(table_hbm, table), (length_hbm, lengths), (q_hbm, raw), (own_hbm, own)]
    pairs_in += list(zip(before_hbm, before))
    small = [
        pltpu.make_async_copy(source, target, sems.at[k])
        for k, (source, target) in enumerate(pairs_in)
    ]

    def key_copy(h):
        return pltpu.make_async_copy(k_hbm.at[:, early + h], keys.at[h], cache_sems.at[0, h])

    def value_copy(h):
        return pltpu.make_async_copy(v_hbm.at[:, early + h], values.at[h], cache_sems.at[1, h])

    start_all(small[:3])
    key_copy(0).start()
    wait_all(small[:2])
    make_bias(table, lengths, bias, keys.shape[2])
    small[2].wait()
    query[...] = raw[...].astype(jnp.float32)
    attend = Attend(query, bias, keys, values, scores, tops, packed, total, scale, per_head)

    def keys_ready(h):
        key_copy(h).wait()
        value_copy(h).start()
        if h + 1 < count:
            key_copy(h + 1).start()
        if h == count - 1:
            start_all(small[3:])

    def values_ready(h):
        value_copy(h).wait()

    def take(h):
        top = attend.tops[h % 2]
        for r in range(per_head):
            place = pl.ds((early + h) * per_head + r, seqs, stride=stride)
            part = pl.ds(r * seqs, seqs)
            weight_sum = total[part, head_dim:]
            rows[place, :] = total[part, :head_dim] / weight_sum
            rows_lse[place, :] = top[part, :] * scale + jnp.log2(weight_sum)

    attend.run(early, count, keys_ready, values_ready, take)
    wait_all(small[3:])
    for h in range(early):
        for r in range(per_head):
            place = pl.ds(h * per_head + r, seqs, stride=stride)
            part = pl.ds(r * seqs, seqs)
            rows[place, :] = before[0][h, part, :]
            rows_lse[place, :] = before[1][h, part, :]


def late_work(table, lengths, queries, k_cache, v_cache, own, before, early, scale):
    pool, kv_heads, page, head_dim = k_cache.shape
    seqs, stride, _ = queries.shape
    per_head = stride // kv_heads
    count = kv_heads - early
    rows = per_head * seqs
    keys = pool * page
    pairs = min(count, 2)
    f32, bf16 = jnp.float32, jnp.bfloat16
    state = jax.ShapeDtypeStruct((seqs, padded(stride), head_dim), f32)
    return pl.pallas_call(
        functools.partial(late_kernel, scale=scale, early=early, count=count, per_head=per_head),
        in_specs=[hbm()] * (6 + len(before)),
        out_specs=[vmem()] * 4,
        out_shape=[
            state,
            state,
            jax.ShapeDtypeStruct((seqs * stride, head_dim), f32),
            jax.ShapeDtypeStruct(own.shape, f32),
        ],
        scratch_shapes=[
            pltpu.VMEM(table.shape, jnp.int32),
            pltpu.VMEM(lengths.shape, jnp.int32),
            pltpu.VMEM((seqs * stride, head_dim), bf16),
            pltpu.VMEM((2, seqs, keys // 2), f32),
            pltpu.VMEM((count, pool, page, head_dim), bf16),
            pltpu.VMEM((count, pool, page, head_dim), bf16),
            pltpu.SemaphoreType.DMA((6,)),
            pltpu.SemaphoreType.DMA((2, count)),
        ] + attend_scratch(seqs, per_head, pool, page, head_dim, pairs) + [
            pltpu.VMEM(array.shape, f32) for array in before
        ],
        compiler_params=limit(40),
        cost_estimate=pl.CostEstimate(
            flops=8 * count * rows * keys * head_dim,
            bytes_accessed=4 * count * keys * head_dim,
            transcendentals=count * rows * keys,
        ),
        name="late_heads",
    )(
        stay(table), stay(lengths), stay(queries.reshape(seqs * stride, head_dim)), stay(k_cache),
        stay(v_cache), stay(own), *[stay(array) for array in before],
    )


def new_kernel(
    own_ref, other_ref, query, old_ref, old_lse_ref, new_hbm, state, state_lse, new, fresh, sem,
    *, per_head, steps, scale,
):
    seqs, stride, head_dim = state.shape
    flat = (seqs * stride, head_dim)
    rows, rows_lse = state.reshape(flat), state_lse.reshape(flat)
    old, old_lse = old_ref.reshape(flat), old_lse_ref.reshape(flat)
    real = query.shape[0] // seqs
    partial = own_ref[...]
    for k in range(other_ref.shape[0]):
        partial = partial + other_ref[k].astype(jnp.float32)
    new[...] = partial.astype(jnp.bfloat16)
    copy = pltpu.make_async_copy(new, new_hbm, sem.at[0])
    copy.start()
    for column in range(fresh.shape[0]):
        columns = slice(column * head_dim, (column + 1) * head_dim)
        fresh[column] = new[:, columns].astype(jnp.float32)
    for h in range(real // per_head):
        new_keys, new_values = [], []
        for j in range(steps):
            every = pl.ds(j, seqs, stride=steps)
            new_keys.append(fresh[2 * h, every, :])
            new_values.append(fresh[2 * h + 1, every, :])
        for r in range(per_head):
            place = pl.ds(h * per_head + r, seqs, stride=stride)
            q = query[pl.ds(h * per_head + r, seqs, stride=real), :]
            scores = [
                jnp.sum(q * new_keys[j], axis=1, keepdims=True) * scale
                for j in range(r % steps + 1)
            ]
            lse = old_lse[place, :]
            top = lse
            for s in scores:
                top = jnp.maximum(top, s)
            weight = jnp.exp2(lse - top)
            summed = weight * old[place, :]
            for j, s in enumerate(scores):
                w = jnp.exp2(s - top)
                weight = weight + w
                summed = summed + w * new_values[j]
            rows[place, :] = summed / weight
            rows_lse[place, :] = top + jnp.log2(weight)
    copy.wait()


def join_new(own, other, query, old, old_lse, per_head, steps, scale):
    head_dim = query.shape[1]
    return pl.pallas_call(
        functools.partial(new_kernel, per_head=per_head, steps=steps, scale=scale),
        in_specs=[vmem()] * 5,
        out_specs=[hbm(), vmem(), vmem()],
        out_shape=[
            jax.ShapeDtypeStruct(own.shape, jnp.bfloat16),
            jax.ShapeDtypeStruct(old.shape, jnp.float32),
            jax.ShapeDtypeStruct(old.shape, jnp.float32),
        ],
        scratch_shapes=[
            pltpu.VMEM(own.shape, jnp.bfloat16),
            pltpu.VMEM((own.shape[1] // head_dim, own.shape[0], head_dim), jnp.float32),
            pltpu.SemaphoreType.DMA((1,)),
        ],
        compiler_params=limit(8),
        cost_estimate=pl.CostEstimate(
            flops=20 * query.size, bytes_accessed=20 * query.size, transcendentals=4 * query.size
        ),
        name="join_new",
    )(own, other, query, old, old_lse)


def moved_kernel(dest_ref, q_ref, keys, values, out_ref, slot, *, scale):
    moves, kv_heads, page, head_dim = keys.shape
    rows = q_ref.shape[1]
    padding = out_ref.shape[1] - rows
    columns = kv_heads * page
    me = lax.axis_index("gen")
    for k in range(moves):
        mine = dest_ref[me * moves + k]
        rank = jnp.int32(0)
        for j in range(k):
            rank = rank + (dest_ref[me * moves + j] == mine).astype(jnp.int32)
        slot[k] = mine * CAP + rank
    out_ref[...] = jnp.zeros(out_ref.shape, jnp.bfloat16)
    row = lax.broadcasted_iota(jnp.int32, (rows, columns), 0)
    column = lax.broadcasted_iota(jnp.int32, (rows, columns), 1)
    other_head = jnp.where(row // (rows // kv_heads) == column // page, 0.0, NEGATIVE)
    tall = lax.broadcasted_iota(jnp.int32, (rows, LANES), 0)
    lane = lax.broadcasted_iota(jnp.int32, (rows, LANES), 1)
    spare = lax.broadcasted_iota(jnp.int32, (padding, LANES), 0)
    ones = jnp.ones((columns, head_dim), jnp.bfloat16)

    def one_move(k):
        s = lax.dot_general(
            q_ref[slot[k]],
            keys[k].reshape(columns, head_dim),
            (((1,), (1,)), ((), ())),
            preferred_element_type=jnp.float32,
        )
        s = s + other_head
        biggest = jnp.max(s, axis=1, keepdims=True)
        weights = jnp.exp2((s - biggest) * scale).astype(jnp.bfloat16)
        both = jnp.concatenate([values[k].reshape(columns, head_dim), ones], axis=1)
        summed = jnp.dot(weights, both, preferred_element_type=jnp.float32)
        weight_sum = summed[:, head_dim:]
        lse = biggest * scale + jnp.log2(weight_sum)
        lse = jnp.sum(jnp.where(tall == lane, lse, 0.0), axis=0, keepdims=True)
        high = lse.astype(jnp.bfloat16).astype(jnp.float32)
        middle = (lse - high).astype(jnp.bfloat16).astype(jnp.float32)
        low = lse - high - middle
        pieces = jnp.where(spare == 0, high, jnp.where(spare == 1, middle, low))
        result = jnp.concatenate([summed[:, :head_dim] / weight_sum, pieces], axis=0)
        return result.astype(jnp.bfloat16)

    batch = min(16, moves)

    def some_moves(b, _):
        results = [one_move(b * batch + k) for k in range(batch)]
        for k in range(batch):
            out_ref[slot[b * batch + k]] = results[k]
        return 0

    lax.fori_loop(0, moves // batch, some_moves, 0)


def moved_attention(dest, received, move_keys, move_values, scale):
    moves, kv_heads, page, head_dim = move_keys.shape
    count, rows, _ = received.shape
    return pl.pallas_call(
        functools.partial(moved_kernel, scale=scale),
        in_specs=[smem(), vmem(), vmem(), vmem()],
        out_specs=vmem(),
        out_shape=jax.ShapeDtypeStruct((count, answer_rows(rows), head_dim), jnp.bfloat16),
        scratch_shapes=[pltpu.SMEM((moves,), jnp.int32)],
        compiler_params=limit(4),
        cost_estimate=pl.CostEstimate(
            flops=4 * moves * rows * kv_heads * page * head_dim,
            bytes_accessed=4 * received.size,
            transcendentals=moves * rows * kv_heads * page,
        ),
        name="moved_attention",
    )(dest, received, move_keys, move_values)


def join_kernel(owner_ref, first_ref, state_ref, lse_ref, slot_ref, out_ref, states, states_lse):
    seqs, rows, head_dim = out_ref.shape
    count = slot_ref.shape[0]
    out_ref[...] = state_ref[:, :rows, :].astype(jnp.bfloat16)
    tall = lax.broadcasted_iota(jnp.int32, (rows, LANES), 0)
    lane = lax.broadcasted_iota(jnp.int32, (rows, LANES), 1)
    real = pl.ds(0, rows)

    def one_slot(n, _):
        first = first_ref[n]

        @pl.when(first == n)
        def _():
            states[n] = state_ref[owner_ref[n], real]
            states_lse[n] = lse_ref[owner_ref[n], real]

        @pl.when(first >= 0)
        def _():
            block = slot_ref[n].astype(jnp.float32)
            packed = block[rows : rows + 1] + block[rows + 1 : rows + 2] + block[rows + 2 : rows + 3]
            come_lse = jnp.sum(jnp.where(tall == lane, packed, 0.0), axis=1, keepdims=True)
            lse = states_lse[first]
            top = jnp.maximum(lse, come_lse)
            old = jnp.exp2(lse - top)
            come = jnp.exp2(come_lse - top)
            weight = old + come
            joined = (old * states[first] + come * block[:rows]) / weight
            states[first] = joined
            states_lse[first] = top + jnp.log2(weight)
            out_ref[owner_ref[n]] = joined.astype(jnp.bfloat16)

        return 0

    lax.fori_loop(0, count, one_slot, 0)


def join_moved(owner, first, state, state_lse, answers, shape):
    slots = first.shape[0]
    return pl.pallas_call(
        join_kernel,
        in_specs=[smem()] * 2 + [vmem()] * 3,
        out_specs=vmem(),
        out_shape=jax.ShapeDtypeStruct(shape, jnp.bfloat16),
        scratch_shapes=[pltpu.VMEM((slots,) + shape[1:], jnp.float32)] * 2,
        compiler_params=limit(8),
        cost_estimate=pl.CostEstimate(
            flops=10 * state.size, bytes_accessed=10 * state.size, transcendentals=0
        ),
        name="join_moved",
    )(owner, first, state, state_lse, answers)


def per_device(
    tokens_in, w_kv, queries, k_cache, v_cache, page_table, lengths, move_dest, move_page, move_seq
):
    groups = lax.axis_size("gen")
    tp = lax.axis_size("tp")
    seqs, steps, heads, head_dim = queries.shape
    kv_heads = k_cache.shape[1]
    scale = LOG2E / math.sqrt(head_dim)

    def exchange(array):
        return lax.all_to_all(array, "gen", split_axis=0, concat_axis=0, tiled=True)

    rows = queries.transpose(0, 2, 1, 3).reshape(seqs, heads * steps, head_dim)
    dest = move_dest.reshape(-1)
    to_send = gather(dest, move_seq, rows, groups)
    early = kv_heads // 2
    early_rows, to_send = lax.optimization_barrier((rows, to_send))
    received = exchange(to_send)
    table, lengths = page_table.T, lengths.reshape(1, seqs)
    *before, own, owner, first, partial, move_keys, move_values = early_work(
        table, lengths, move_page, early_rows, tokens_in, dest, move_seq, k_cache, v_cache, w_kv,
        groups, tp, early, scale,
    )
    pieces = []
    for k in range(1, tp):
        pairs = [(i, (i + k) % tp) for i in range(tp)]
        pieces.append(lax.ppermute(partial[k - 1], "tp", pairs))
    other = jnp.stack(pieces)
    answers = moved_attention(dest, received, move_keys, move_values, scale)
    late_rows, answers = lax.optimization_barrier((rows, answers))
    returned = exchange(answers)
    state, state_lse, query, own = late_work(
        table, lengths, late_rows, k_cache, v_cache, own, before, early, scale
    )
    new_kv, state, state_lse = join_new(
        own, other, query, state, state_lse, heads * steps // kv_heads, steps, scale
    )
    attended = join_moved(
        owner, first, state, state_lse, returned, (seqs, heads * steps, head_dim)
    )
    attended = attended.reshape(seqs, heads, steps, head_dim).transpose(0, 2, 1, 3)
    return (attended, new_kv)


def solution(mesh):
    return jax.shard_map(
        per_device,
        mesh=mesh,
        in_specs=(
            P("gen", "tp"),
            P("tp", None),
            P("gen", None, "tp", None),
            P("gen", "tp", None, None),
            P("gen", "tp", None, None),
            P("gen", None),
            P("gen"),
            P(),
            P(),
            P(),
        ),
        out_specs=(P("gen", None, "tp", None), P("gen", "tp")),
        check_vma=False,
    )
```

```python
import functools
import math

import jax
import jax.numpy as jnp
from jax import lax
from jax.experimental import pallas as pl
from jax.experimental.pallas import tpu as pltpu
from jax.sharding import PartitionSpec as P

CAP = 2
NEGATIVE = -1e30
LOG2E = 1.4426950408889634
LANES = 128
MIB = 1024 * 1024


def vmem():
    return pl.BlockSpec(memory_space=pltpu.VMEM)


def hbm():
    return pl.BlockSpec(memory_space=pltpu.HBM)


def stay(array):
    return pltpu.with_memory_space_constraint(array, pltpu.HBM)


def limit(mib):
    return pltpu.CompilerParams(vmem_limit_bytes=mib * MIB)


def padded(rows):
    return (rows + 7) // 8 * 8


def answer_rows(rows):
    return (rows + 3 + 15) // 16 * 16


def fill_owner(dest, seq, me, owner, per_source):
    groups = dest.shape[0] // per_source
    slots = groups * CAP

    short = dest.shape[0] <= 256

    def clear(n, _):
        owner[n] = -1
        return 0

    def one_source(source, _):
        count = jnp.int32(0)
        for k in range(per_source):
            row = source * per_source + k
            hit = dest[row] == me
            owner[jnp.where(hit, source * CAP + count, slots)] = seq[row]
            count = count + hit.astype(jnp.int32)
        return 0

    repeat(slots, clear, short)
    repeat(groups, one_source, short)


def repeat(count, step, unrolled):
    if unrolled:
        for n in range(count):
            step(n, 0)
    else:
        lax.fori_loop(0, count, step, 0)


def first_slots(owner, first, seen):
    def unseen(n, _):
        seen[n] = -1
        return 0

    short = first.shape[0] <= 32
    repeat(seen.shape[0], unseen, short)

    def first_slot(n, _):
        sequence = owner[n]
        place = jnp.maximum(sequence, 0)
        earlier = seen[place]
        mine = jnp.where(earlier < 0, n, earlier)
        seen[place] = jnp.where(sequence < 0, earlier, mine)
        first[n] = jnp.where(sequence < 0, -1, mine)
        return 0

    repeat(first.shape[0], first_slot, short)


def gather_kernel(
    dest_hbm, seq_hbm, q_hbm, out_ref, dest, seq, owner, queries, sems, *, per_source
):
    me = lax.axis_index("gen")
    copies = [
        pltpu.make_async_copy(dest_hbm, dest, sems.at[0]),
        pltpu.make_async_copy(seq_hbm, seq, sems.at[1]),
        pltpu.make_async_copy(q_hbm, queries, sems.at[2]),
    ]
    for copy in copies:
        copy.start()
    copies[0].wait()
    copies[1].wait()
    fill_owner(dest, seq, me, owner, per_source)
    copies[2].wait()

    def one_slot(n, _):
        out_ref[n] = queries[jnp.maximum(owner[n], 0)]
        return 0

    lax.fori_loop(0, out_ref.shape[0], one_slot, 0, unroll=8)


def gather(dest, seq, queries, groups):
    slots = groups * CAP
    _, rows, head_dim = queries.shape
    return pl.pallas_call(
        functools.partial(gather_kernel, per_source=dest.shape[0] // groups),
        in_specs=[hbm()] * 3,
        out_specs=vmem(),
        out_shape=jax.ShapeDtypeStruct((slots, rows, head_dim), jnp.bfloat16),
        scratch_shapes=[
            pltpu.SMEM(dest.shape, jnp.int32),
            pltpu.SMEM(seq.shape, jnp.int32),
            pltpu.SMEM((slots + 1,), jnp.int32),
            pltpu.VMEM(queries.shape, jnp.bfloat16),
            pltpu.SemaphoreType.DMA((3,)),
        ],
        compiler_params=limit(4),
        cost_estimate=pl.CostEstimate(flops=0, bytes_accessed=4 * queries.size, transcendentals=0),
        name="gather_queries",
    )(stay(dest), stay(seq), stay(queries))


def make_bias(table_ref, length_ref, bias, page):
    blocks, seqs, width = bias.shape
    pool = padded(blocks * width // page)
    lengths = length_ref[...].astype(jnp.float32)
    page_id = lax.broadcasted_iota(jnp.int32, (pool, seqs), 0)
    used = jnp.zeros((pool, seqs), jnp.float32)
    for j in range(table_ref.shape[0]):
        inside = jnp.clip(lengths - float(page * j), 0.0, float(page))
        used = used + jnp.where(table_ref[j : j + 1, :] == page_id, inside, 0.0)
    used = used.T.astype(jnp.bfloat16)

    def one_block(b, _):
        key = lax.broadcasted_iota(jnp.int32, (pool, width), 1) + b * width
        owner = lax.broadcasted_iota(jnp.int32, (pool, width), 0)
        expand = jnp.where(key // page == owner, 1.0, 0.0).astype(jnp.bfloat16)
        count = jnp.dot(used, expand, preferred_element_type=jnp.float32)
        position = lax.broadcasted_iota(jnp.int32, (seqs, width), 1) % page
        bias[b] = jnp.where(position.astype(jnp.float32) < count, 0.0, NEGATIVE)
        return 0

    lax.fori_loop(0, blocks, one_block, 0)


class Attend:
    def __init__(self, packed, bias, keys, values, scores, tops, totals, scale, per_head):
        self.packed, self.bias, self.keys, self.values = packed, bias, keys, values
        self.scores, self.tops, self.totals = scores, tops, totals
        self.scale, self.per_head = scale, per_head
        self.blocks, self.seqs, self.width = bias.shape
        self.head_dim = packed.shape[2]
        self.rows = per_head * self.seqs
        self.pages = self.width // keys.shape[2]

    def start_scores(self, h):
        self.tops[h] = jnp.full((self.rows, LANES), NEGATIVE, jnp.float32)

    def score_block(self, h, b):
        keys = self.keys[h, pl.ds(b * self.pages, self.pages)].reshape(self.width, self.head_dim)
        s = lax.dot_general(
            self.packed[self.first + h], keys, (((1,), (1,)), ((), ())),
            preferred_element_type=jnp.float32,
        )
        s = s.reshape(self.per_head, self.seqs, self.width) + self.bias[b][None]
        s = s.reshape(self.rows, self.width)
        self.scores[h % 2][b] = s
        largest = s[:, :LANES]
        for t in range(1, self.width // LANES):
            largest = jnp.maximum(largest, s[:, t * LANES : (t + 1) * LANES])
        self.tops[h] = jnp.maximum(self.tops[h], largest)

    def start_values(self, h):
        top = jnp.max(self.tops[h], axis=1, keepdims=True)
        self.tops[h] = jnp.broadcast_to(top, (self.rows, LANES))
        self.totals[h] = jnp.zeros((self.rows, 2 * self.head_dim), jnp.float32)

    def weigh(self, weights, values):
        return jnp.dot(
            weights,
            jnp.concatenate([values, jnp.ones(values.shape, jnp.bfloat16)], axis=1),
            preferred_element_type=jnp.float32,
        )

    def value_block(self, h, b):
        scores, biggest = self.scores[h % 2], self.tops[h]
        values = self.values[h, pl.ds(b * self.pages, self.pages)]
        weights = []
        for t in range(self.width // LANES):
            s = scores[b, :, t * LANES : (t + 1) * LANES]
            weights.append(jnp.exp2((s - biggest) * self.scale).astype(jnp.bfloat16))
        self.totals[h] += self.weigh(
            jnp.concatenate(weights, axis=1), values.reshape(self.width, self.head_dim)
        )

    def run(self, first, count, keys_ready, values_ready, done):
        self.first = first
        for h in range(count + 1):
            if h < count:
                self.start_scores(h)
                keys_ready(h, 0)
            if h > 0:
                values_ready(h - 1)
                self.start_values(h - 1)

            def one_block(b, _, h=h):
                if h < count:
                    self.score_block(h, b)
                if h > 0:
                    self.value_block(h - 1, b)
                return 0

            if h == 0:
                self.score_block(0, 0)
                keys_ready(0, 1)
                self.score_block(0, 1)
            else:
                if h < count:
                    keys_ready(h, 1)
                lax.fori_loop(0, self.blocks, one_block, 0)
            if h > 0:
                done(h - 1)


def attend_scratch(seqs, per_head, pool, page, head_dim, pairs):
    keys = pool * page
    width = keys // 2
    rows = per_head * seqs
    scores = [pltpu.VMEM((keys // width, rows, width), jnp.float32) for _ in range(pairs)]
    return scores


def start_all(copies):
    for copy in copies:
        copy.start()


def wait_all(copies):
    for copy in copies:
        copy.wait()


def key_part(hbm_ref, head, target, sems, part):
    half = target.shape[0] // 2
    pages = pl.ds(part * half, half)
    return pltpu.make_async_copy(hbm_ref.at[pages, head], target.at[pages], sems.at[part])


def early_kernel(
    table_hbm, length_hbm, q_hbm, pages_hbm, dest_hbm, seq_hbm, x_hbm, k_hbm, v_hbm, w_hbm, *refs,
    tp, scale, count, per_head,
):
    outs = 2 if count else 0
    local_hbm = refs[:outs]
    owner_hbm, first_hbm, packed_hbm, send_ref, move_keys, move_values = refs[outs : outs + 6]
    (table, lengths, pages, raw, query, packed, bias, x, dest, seq, owner, first, seen, w, keys, values,
     small_sems, key_sems, value_sems, move_sems, w_sems, out_sems, *attend_refs) = refs[outs + 6 :]
    pairs = min(count, 2)
    blocks, _, width = w.shape
    moves = move_keys.shape[0]
    per_owner = blocks // (tp - 1)
    columns = per_owner * width
    me, place = lax.axis_index("gen"), lax.axis_index("tp")
    small = [
        pltpu.make_async_copy(source, target, small_sems.at[k])
        for k, (source, target) in enumerate(
            [(table_hbm, table), (length_hbm, lengths), (q_hbm, raw), (pages_hbm, pages),
             (dest_hbm, dest), (seq_hbm, seq), (x_hbm, x)]
        )
    ]
    owner_copy = pltpu.make_async_copy(owner, owner_hbm, out_sems.at[4, 0])
    first_copy = pltpu.make_async_copy(first, first_hbm, out_sems.at[0, 0])
    packed_copy = pltpu.make_async_copy(packed, packed_hbm, out_sems.at[3, 0])
    seqs = bias.shape[1]
    stride = query.shape[0] // seqs

    def pack(head):
        for r in range(per_head):
            rows = query[pl.ds(head * per_head + r, seqs, stride=stride), :]
            packed[head, pl.ds(r * seqs, seqs), :] = rows.astype(jnp.bfloat16)

    def key_copy(h, part):
        return key_part(k_hbm, h, keys.at[h], key_sems.at[h], part)

    def value_copy(h):
        return pltpu.make_async_copy(v_hbm.at[:, h], values.at[h], value_sems.at[h])

    def w_copy(b):
        target = lax.rem(place + 1 + b // per_owner, tp)
        start = pl.multiple_of(target * columns + b % per_owner * width, width)
        return pltpu.make_async_copy(w_hbm.at[:, pl.ds(start, width)], w.at[b], w_sems.at[b])

    def move_copies(k):
        page = pages[me * moves + k]
        return (
            pltpu.make_async_copy(k_hbm.at[page], move_keys.at[k], move_sems.at[0, k]),
            pltpu.make_async_copy(v_hbm.at[page], move_values.at[k], move_sems.at[1, k]),
        )

    def start_move(k, _):
        start_all(move_copies(k))
        return 0

    def wait_move(k, _):
        wait_all(move_copies(k))
        return 0

    def start_weights(start, stop):
        for b in range(start, stop):
            w_copy(b).start()

    start_all(small[:3])
    if count:
        key_copy(0, 0).start()
        key_copy(0, 1).start()
    start_all(small[3:6])
    wait_all(small[:2])
    if count:
        make_bias(table, lengths, bias, keys.shape[2])
    small[2].wait()
    query[...] = raw[...].astype(jnp.float32)
    for head in range(count):
        pack(head)
    if count:
        totals, tops = attend_refs[pairs:]
        attend = Attend(
            packed, bias, keys, values, attend_refs[:pairs], tops, totals, scale, per_head
        )

        def local_copies(h):
            return [
                pltpu.make_async_copy(totals.at[h], local_hbm[0].at[h], out_sems.at[1, h]),
                pltpu.make_async_copy(tops.at[h], local_hbm[1].at[h], out_sems.at[2, h]),
            ]

        def keys_ready(h, b):
            key_copy(h, b).wait()
            if b == 0:
                value_copy(h).start()
                if h + 1 < count:
                    key_copy(h + 1, 0).start()
                    key_copy(h + 1, 1).start()
                if h == count - 1:
                    small[6].start()
                    start_weights(0, (blocks + 1) // 2)

        def values_ready(h):
            value_copy(h).wait()
            if h == count - 1:
                start_weights((blocks + 1) // 2, blocks)
                small[3].wait()
                lax.fori_loop(0, moves, start_move, 0)

        attend.run(0, count, keys_ready, values_ready, lambda h: start_all(local_copies(h)))
    else:
        small[6].start()
        start_weights(0, blocks)
        small[3].wait()
        lax.fori_loop(0, moves, start_move, 0)
    for head in range(count, packed.shape[0]):
        pack(head)
    packed_copy.start()
    wait_all(small[4:])
    for b in range(blocks):
        w_copy(b).wait()
        product = jnp.dot(x[...], w[b], preferred_element_type=jnp.float32)
        part = slice(b % per_owner * width, (b % per_owner + 1) * width)
        send_ref[b // per_owner, :, part] = product.astype(jnp.bfloat16)
        if b == 0:
            fill_owner(dest, seq, me, owner, moves)
            first_slots(owner, first, seen)
            owner_copy.start()
            first_copy.start()
    lax.fori_loop(0, moves, wait_move, 0)
    owner_copy.wait()
    first_copy.wait()
    packed_copy.wait()
    for h in range(count):
        wait_all(local_copies(h))


def early_work(
    table, lengths, pages, queries, tokens, dest, seq, k_cache, v_cache, w_kv, groups, tp, count, scale
):
    seqs, stride, head_dim = queries.shape
    pool, kv_heads, page, _ = k_cache.shape
    per_head = stride // kv_heads
    rows, depth = tokens.shape
    moves, slots = pages.shape[0] // groups, groups * CAP
    columns = w_kv.shape[1] // tp
    width = min(512, columns)
    blocks = (tp - 1) * columns // width
    keys = pool * page
    held = max(count, 1)
    f32, bf16 = jnp.float32, jnp.bfloat16
    total_shape = (count, per_head * seqs, 2 * head_dim)
    top_shape = (count, per_head * seqs, LANES)
    local = [pltpu.HBM(total_shape, f32), pltpu.HBM(top_shape, f32)] if count else []
    scratch = [
        pltpu.VMEM(table.shape, jnp.int32),
        pltpu.VMEM(lengths.shape, jnp.int32),
        pltpu.SMEM(pages.shape, jnp.int32),
        pltpu.VMEM((seqs * stride, head_dim), bf16),
        pltpu.VMEM((seqs * stride, head_dim), f32),
        pltpu.VMEM((kv_heads, per_head * seqs, head_dim), bf16),
        pltpu.VMEM((2, seqs, keys // 2), f32),
        pltpu.VMEM((rows, depth), bf16),
        pltpu.SMEM(dest.shape, jnp.int32),
        pltpu.SMEM(seq.shape, jnp.int32),
        pltpu.SMEM((slots + 1,), jnp.int32),
        pltpu.SMEM((slots,), jnp.int32),
        pltpu.SMEM((seqs,), jnp.int32),
        pltpu.VMEM((blocks, depth, width), bf16),
        pltpu.VMEM((held, pool, page, head_dim), bf16),
        pltpu.VMEM((held, pool, page, head_dim), bf16),
        pltpu.SemaphoreType.DMA((7,)),
        pltpu.SemaphoreType.DMA((held, 2)),
        pltpu.SemaphoreType.DMA((held,)),
        pltpu.SemaphoreType.DMA((2, moves)),
        pltpu.SemaphoreType.DMA((blocks,)),
        pltpu.SemaphoreType.DMA((5, held)),
    ]
    if count:
        scratch += attend_scratch(seqs, per_head, pool, page, head_dim, min(count, 2))
        scratch += [pltpu.VMEM(total_shape, f32), pltpu.VMEM(top_shape, f32)]
    return pl.pallas_call(
        functools.partial(early_kernel, tp=tp, scale=scale, count=count, per_head=per_head),
        in_specs=[hbm()] * 10,
        out_specs=[hbm()] * (len(local) + 3) + [vmem()] * 3,
        out_shape=local + [
            pltpu.HBM((slots + 1,), jnp.int32),
            pltpu.HBM((slots,), jnp.int32),
            pltpu.HBM((kv_heads, per_head * seqs, head_dim), bf16),
            jax.ShapeDtypeStruct((tp - 1, rows, columns), bf16),
            jax.ShapeDtypeStruct((moves,) + k_cache.shape[1:], bf16),
            jax.ShapeDtypeStruct((moves,) + k_cache.shape[1:], bf16),
        ],
        scratch_shapes=scratch,
        compiler_params=limit(40),
        cost_estimate=pl.CostEstimate(
            flops=tokens.size * w_kv.shape[1] + 8 * count * per_head * seqs * keys * head_dim,
            bytes_accessed=w_kv.size + 4 * count * keys * head_dim,
            transcendentals=count * per_head * seqs * keys,
        ),
        name="early_heads_and_sent_kv",
    )(
        stay(table), stay(lengths), stay(queries.reshape(seqs * stride, head_dim)), stay(pages),
        stay(dest), stay(seq), stay(tokens), stay(k_cache), stay(v_cache), stay(w_kv),
    )


def late_kernel(
    table_hbm, length_hbm, q_hbm, k_hbm, v_hbm, x_hbm, w_hbm, *refs, scale, early, count, per_head
):
    ins = 2 if early else 0
    before_hbm = refs[:ins]
    totals, tops, packed, x, w = refs[ins : ins + 5]
    before = refs[ins + 5 : 2 * ins + 5]
    table, lengths, bias, keys, values, sems, key_sems, value_sems, *scores = refs[2 * ins + 5 :]
    columns = w.shape[1]
    start = pl.multiple_of(lax.axis_index("tp") * columns, columns)
    pairs_in = [
        (table_hbm, table), (length_hbm, lengths), (q_hbm, packed), (x_hbm, x),
        (w_hbm.at[:, pl.ds(start, columns)], w),
    ] + list(zip(before_hbm, before))
    small = [
        pltpu.make_async_copy(source, target, sems.at[k])
        for k, (source, target) in enumerate(pairs_in)
    ]

    def key_copy(h, part):
        return key_part(k_hbm, early + h, keys.at[h], key_sems.at[h], part)

    def value_copy(h):
        return pltpu.make_async_copy(v_hbm.at[:, early + h], values.at[h], value_sems.at[h])

    start_all(small[:3])
    key_copy(0, 0).start()
    key_copy(0, 1).start()
    wait_all(small[:2])
    make_bias(table, lengths, bias, keys.shape[2])
    small[2].wait()
    attend = Attend(packed, bias, keys, values, scores, tops, totals, scale, per_head)

    def keys_ready(h, b):
        key_copy(h, b).wait()
        if b == 0:
            value_copy(h).start()
            if h + 1 < count:
                key_copy(h + 1, 0).start()
                key_copy(h + 1, 1).start()
            if h == count - 1:
                start_all(small[3:])

    attend.run(early, count, keys_ready, lambda h: value_copy(h).wait(), lambda h: None)
    wait_all(small[3:])


def late_work(table, lengths, packed, k_cache, v_cache, tokens, w_kv, before, tp, early, scale):
    pool, kv_heads, page, head_dim = k_cache.shape
    _, rows, _ = packed.shape
    seqs = lengths.shape[1]
    per_head = rows // seqs
    count = kv_heads - early
    keys = pool * page
    f32, bf16 = jnp.float32, jnp.bfloat16
    return pl.pallas_call(
        functools.partial(late_kernel, scale=scale, early=early, count=count, per_head=per_head),
        in_specs=[hbm()] * (7 + len(before)),
        out_specs=[vmem()] * (5 + len(before)),
        out_shape=[
            jax.ShapeDtypeStruct((count, rows, 2 * head_dim), f32),
            jax.ShapeDtypeStruct((count, rows, LANES), f32),
            jax.ShapeDtypeStruct(packed.shape, bf16),
            jax.ShapeDtypeStruct(tokens.shape, bf16),
            jax.ShapeDtypeStruct((w_kv.shape[0], w_kv.shape[1] // tp), bf16),
        ] + [jax.ShapeDtypeStruct(array.shape, f32) for array in before],
        scratch_shapes=[
            pltpu.VMEM(table.shape, jnp.int32),
            pltpu.VMEM(lengths.shape, jnp.int32),
            pltpu.VMEM((2, seqs, keys // 2), f32),
            pltpu.VMEM((count, pool, page, head_dim), bf16),
            pltpu.VMEM((count, pool, page, head_dim), bf16),
            pltpu.SemaphoreType.DMA((7,)),
            pltpu.SemaphoreType.DMA((count, 2)),
            pltpu.SemaphoreType.DMA((count,)),
        ] + attend_scratch(seqs, per_head, pool, page, head_dim, min(count, 2)),
        compiler_params=limit(36),
        cost_estimate=pl.CostEstimate(
            flops=8 * count * rows * keys * head_dim,
            bytes_accessed=4 * count * keys * head_dim,
            transcendentals=count * rows * keys,
        ),
        name="late_heads",
    )(
        stay(table), stay(lengths), stay(packed), stay(k_cache), stay(v_cache), stay(tokens), stay(w_kv),
        *[stay(array) for array in before],
    )


def new_kernel(
    other_ref, packed, x, w, *refs, parts, per_head, steps, scale
):
    local = refs[: 2 * parts]
    new_hbm, state, state_lse, new, fresh, sem = refs[2 * parts :]
    seqs, stride, head_dim = state.shape
    flat = (seqs * stride, head_dim)
    rows, rows_lse = state.reshape(flat), state_lse.reshape(flat)
    width = 2 * head_dim
    head = 0
    for part in range(parts):
        totals, tops = local[2 * part], local[2 * part + 1]
        for h in range(totals.shape[0]):
            columns = slice(head * width, (head + 1) * width)
            if head % 2 == 0:
                both = jnp.dot(
                    x[...], w[:, head * width : (head + 2) * width], preferred_element_type=jnp.float32
                )
            partial = both[:, head % 2 * width : (head % 2 + 1) * width]
            for k in range(other_ref.shape[0]):
                partial = partial + other_ref[k, :, columns].astype(jnp.float32)
            rounded = partial.astype(jnp.bfloat16)
            new[:, columns] = rounded
            fresh[head, 0] = rounded[:, :head_dim].astype(jnp.float32)
            fresh[head, 1] = rounded[:, head_dim:].astype(jnp.float32)
            new_keys, new_values = [], []
            for j in range(steps):
                every = pl.ds(j, seqs, stride=steps)
                new_keys.append(fresh[head, 0, every, :])
                new_values.append(fresh[head, 1, every, :])
            for r in range(per_head):
                place = pl.ds(head * per_head + r, seqs, stride=stride)
                block = pl.ds(r * seqs, seqs)
                q = packed[head, block, :].astype(jnp.float32)
                scores = [
                    jnp.sum(q * new_keys[j], axis=1, keepdims=True) * scale
                    for j in range(r % steps + 1)
                ]
                biggest = tops[h, block, :] * scale
                top = biggest
                for s in scores:
                    top = jnp.maximum(top, s)
                factor = jnp.exp2(biggest - top)
                weight = factor * totals[h, block, head_dim:]
                summed = factor * totals[h, block, :head_dim]
                for j, s in enumerate(scores):
                    share = jnp.exp2(s - top)
                    weight = weight + share
                    summed = summed + share * new_values[j]
                rows[place, :] = summed / weight
                rows_lse[place, :] = top + jnp.log2(weight)
            head += 1
    copy = pltpu.make_async_copy(new, new_hbm, sem.at[0])
    copy.start()
    copy.wait()


def join_new(other, packed, x, w, local, seqs, per_head, steps, scale):
    kv_heads, rows, head_dim = packed.shape
    columns = w.shape[1]
    state = jax.ShapeDtypeStruct((seqs, padded(kv_heads * per_head), head_dim), jnp.float32)
    return pl.pallas_call(
        functools.partial(
            new_kernel, parts=len(local) // 2, per_head=per_head, steps=steps, scale=scale
        ),
        in_specs=[vmem()] * (4 + len(local)),
        out_specs=[hbm(), vmem(), vmem()],
        out_shape=[jax.ShapeDtypeStruct((x.shape[0], columns), jnp.bfloat16), state, state],
        scratch_shapes=[
            pltpu.VMEM((x.shape[0], columns), jnp.bfloat16),
            pltpu.VMEM((columns // (2 * head_dim), 2, x.shape[0], head_dim), jnp.float32),
            pltpu.SemaphoreType.DMA((1,)),
        ],
        compiler_params=limit(8),
        cost_estimate=pl.CostEstimate(
            flops=20 * packed.size + 2 * x.shape[0] * w.size,
            bytes_accessed=20 * packed.size,
            transcendentals=4 * packed.size,
        ),
        name="join_new",
    )(other, packed, x, w, *local)


def moved_kernel(dest_hbm, q_ref, keys, values, out_ref, dest_ref, slot, sem, *, scale):
    moves, kv_heads, page, head_dim = keys.shape
    rows = q_ref.shape[1]
    padding = out_ref.shape[1] - rows
    columns = kv_heads * page
    me = lax.axis_index("gen")
    dest_copy = pltpu.make_async_copy(dest_hbm, dest_ref, sem.at[0])
    dest_copy.start()
    out_ref[...] = jnp.zeros(out_ref.shape, jnp.bfloat16)
    row = lax.broadcasted_iota(jnp.int32, (rows, columns), 0)
    column = lax.broadcasted_iota(jnp.int32, (rows, columns), 1)
    other_head = jnp.where(row // (rows // kv_heads) == column // page, 0.0, NEGATIVE)
    tall = lax.broadcasted_iota(jnp.int32, (rows, LANES), 0)
    lane = lax.broadcasted_iota(jnp.int32, (rows, LANES), 1)
    spare = lax.broadcasted_iota(jnp.int32, (padding, LANES), 0)
    ones = jnp.ones((columns, head_dim), jnp.bfloat16)

    def one_move(k):
        s = lax.dot_general(
            q_ref[slot[k]],
            keys[k].reshape(columns, head_dim),
            (((1,), (1,)), ((), ())),
            preferred_element_type=jnp.float32,
        )
        s = s + other_head
        biggest = jnp.max(s, axis=1, keepdims=True)
        weights = jnp.exp2((s - biggest) * scale).astype(jnp.bfloat16)
        both = jnp.concatenate([values[k].reshape(columns, head_dim), ones], axis=1)
        summed = jnp.dot(weights, both, preferred_element_type=jnp.float32)
        weight_sum = summed[:, head_dim:]
        lse = biggest * scale + jnp.log2(weight_sum)
        lse = jnp.sum(jnp.where(tall == lane, lse, 0.0), axis=0, keepdims=True)
        high = lse.astype(jnp.bfloat16).astype(jnp.float32)
        middle = (lse - high).astype(jnp.bfloat16).astype(jnp.float32)
        low = lse - high - middle
        pieces = jnp.where(spare == 0, high, jnp.where(spare == 1, middle, low))
        result = jnp.concatenate([summed[:, :head_dim] / weight_sum, pieces], axis=0)
        return result.astype(jnp.bfloat16)

    dest_copy.wait()
    for k in range(moves):
        mine = dest_ref[me * moves + k]
        rank = jnp.int32(0)
        for j in range(k):
            rank = rank + (dest_ref[me * moves + j] == mine).astype(jnp.int32)
        slot[k] = mine * CAP + rank
    batch = min(16, moves)

    def some_moves(b, _):
        results = [one_move(b * batch + k) for k in range(batch)]
        for k in range(batch):
            out_ref[slot[b * batch + k]] = results[k]
        return 0

    lax.fori_loop(0, moves // batch, some_moves, 0)


def moved_attention(dest, received, move_keys, move_values, scale):
    moves, kv_heads, page, head_dim = move_keys.shape
    count, rows, _ = received.shape
    return pl.pallas_call(
        functools.partial(moved_kernel, scale=scale),
        in_specs=[hbm(), vmem(), vmem(), vmem()],
        out_specs=vmem(),
        out_shape=jax.ShapeDtypeStruct((count, answer_rows(rows), head_dim), jnp.bfloat16),
        scratch_shapes=[
            pltpu.SMEM(dest.shape, jnp.int32),
            pltpu.SMEM((moves,), jnp.int32),
            pltpu.SemaphoreType.DMA((1,)),
        ],
        compiler_params=limit(4),
        cost_estimate=pl.CostEstimate(
            flops=4 * moves * rows * kv_heads * page * head_dim,
            bytes_accessed=4 * received.size,
            transcendentals=moves * rows * kv_heads * page,
        ),
        name="moved_attention",
    )(stay(dest), received, move_keys, move_values)


def join_kernel(
    owner_hbm, first_hbm, state_ref, lse_ref, slot_ref, out_ref, owner_ref, first_ref, states,
    states_lse, come_lses, sems,
):
    seqs, rows, head_dim = out_ref.shape
    count = slot_ref.shape[0]
    copies = [
        pltpu.make_async_copy(owner_hbm, owner_ref, sems.at[0]),
        pltpu.make_async_copy(first_hbm, first_ref, sems.at[1]),
    ]
    start_all(copies)
    real = pl.ds(0, rows)
    tall = lax.broadcasted_iota(jnp.int32, (rows, LANES), 0)
    lane = lax.broadcasted_iota(jnp.int32, (rows, LANES), 1)
    out_ref[...] = state_ref[:, :rows, :].astype(jnp.bfloat16)

    def answer_lse(n, _):
        pieces = slot_ref[n, pl.ds(rows // 8 * 8, slot_ref.shape[1] - rows // 8 * 8)]
        pieces = pieces.astype(jnp.float32)[rows % 8 :]
        packed = pieces[0:1] + pieces[1:2] + pieces[2:3]
        lse = jnp.sum(jnp.where(tall == lane, packed, 0.0), axis=1, keepdims=True)
        come_lses[n] = jnp.broadcast_to(lse, (rows, LANES))
        return 0

    lax.fori_loop(0, count, answer_lse, 0, unroll=8)
    wait_all(copies)

    def join(n, old_sum, old_lse):
        come_lse = come_lses[n]
        top = jnp.maximum(old_lse, come_lse)
        old = jnp.exp2(old_lse - top)
        come = jnp.exp2(come_lse - top)
        weight = old + come
        come_sum = slot_ref[n].astype(jnp.float32)[:rows]
        return (old * old_sum + come * come_sum) / weight, top + jnp.log2(weight)

    def every_slot(n, _):
        seq = jnp.maximum(owner_ref[n], 0)
        states[n], states_lse[n] = join(n, state_ref[seq, real], lse_ref[seq, real])
        return 0

    def later_slot(n, _):
        first = first_ref[n]

        @pl.when((first >= 0) & (first < n))
        def _():
            states[first], states_lse[first] = join(n, states[first], states_lse[first])

        return 0

    def store_slot(n, _):
        @pl.when(first_ref[n] == n)
        def _():
            out_ref[owner_ref[n]] = states[n].astype(jnp.bfloat16)

        return 0

    lax.fori_loop(0, count, every_slot, 0, unroll=8)
    lax.fori_loop(0, count, later_slot, 0)
    lax.fori_loop(0, count, store_slot, 0)


def join_moved(owner, first, state, state_lse, answers, shape):
    slots = first.shape[0]
    block = pltpu.VMEM((slots,) + shape[1:], jnp.float32)
    return pl.pallas_call(
        join_kernel,
        in_specs=[hbm()] * 2 + [vmem()] * 3,
        out_specs=vmem(),
        out_shape=jax.ShapeDtypeStruct(shape, jnp.bfloat16),
        scratch_shapes=[
            pltpu.SMEM(owner.shape, jnp.int32),
            pltpu.SMEM(first.shape, jnp.int32),
            block, block, block,
            pltpu.SemaphoreType.DMA((2,)),
        ],
        compiler_params=limit(8),
        cost_estimate=pl.CostEstimate(
            flops=10 * state.size, bytes_accessed=10 * state.size, transcendentals=0
        ),
        name="join_moved",
    )(stay(owner), stay(first), state, state_lse, answers)


def per_device(
    tokens_in, w_kv, queries, k_cache, v_cache, page_table, lengths, move_dest, move_page, move_seq
):
    groups = lax.axis_size("gen")
    tp = lax.axis_size("tp")
    seqs, steps, heads, head_dim = queries.shape
    kv_heads = k_cache.shape[1]
    scale = LOG2E / math.sqrt(head_dim)

    def exchange(array):
        return lax.all_to_all(array, "gen", split_axis=0, concat_axis=0, tiled=True)

    rows = queries.transpose(0, 2, 1, 3).reshape(seqs, heads * steps, head_dim)
    dest = move_dest.reshape(-1)
    to_send = gather(dest, move_seq, rows, groups)
    early = kv_heads // 2
    early_rows, to_send = lax.optimization_barrier((rows, to_send))
    received = exchange(to_send)
    table, lengths = page_table.T, lengths.reshape(1, seqs)
    *before, owner, first, packed, partial, move_keys, move_values = early_work(
        table, lengths, move_page, early_rows, tokens_in, dest, move_seq, k_cache, v_cache, w_kv,
        groups, tp, early, scale,
    )
    pieces = []
    for k in range(1, tp):
        pairs = [(i, (i + k) % tp) for i in range(tp)]
        pieces.append(lax.ppermute(partial[k - 1], "tp", pairs))
    other = jnp.stack(pieces)
    answers = moved_attention(dest, received, move_keys, move_values, scale)
    packed, answers = lax.optimization_barrier((packed, answers))
    returned = exchange(answers)
    totals, tops, packed, x, w, *before = late_work(
        table, lengths, packed, k_cache, v_cache, tokens_in, w_kv, before, tp, early, scale
    )
    new_kv, state, state_lse = join_new(
        other, packed, x, w, before + [totals, tops], seqs, heads * steps // kv_heads, steps, scale
    )
    attended = join_moved(
        owner, first, state, state_lse, returned, (seqs, heads * steps, head_dim)
    )
    attended = attended.reshape(seqs, heads, steps, head_dim).transpose(0, 2, 1, 3)
    return (attended, new_kv)


def solution(mesh):
    return jax.shard_map(
        per_device,
        mesh=mesh,
        in_specs=(
            P("gen", "tp"),
            P("tp", None),
            P("gen", None, "tp", None),
            P("gen", "tp", None, None),
            P("gen", "tp", None, None),
            P("gen", None),
            P("gen"),
            P(),
            P(),
            P(),
        ),
        out_specs=(P("gen", None, "tp", None), P("gen", "tp")),
        check_vma=False,
    )
```

```python
import functools
import math

import jax
import jax.numpy as jnp
from jax import lax
from jax.experimental import pallas as pl
from jax.experimental.pallas import tpu as pltpu
from jax.sharding import PartitionSpec as P

CAP = 2
NEGATIVE = -1e30
LOG2E = 1.4426950408889634
LANES = 128
MIB = 1024 * 1024


def vmem():
    return pl.BlockSpec(memory_space=pltpu.VMEM)


def hbm():
    return pl.BlockSpec(memory_space=pltpu.HBM)


def stay(array):
    return pltpu.with_memory_space_constraint(array, pltpu.HBM)


def limit(mib):
    return pltpu.CompilerParams(vmem_limit_bytes=mib * MIB)


def padded(rows):
    return (rows + 7) // 8 * 8


def answer_rows(rows):
    return (rows + 3 + 15) // 16 * 16


def fill_owner(dest, seq, me, owner, per_source):
    groups = dest.shape[0] // per_source
    slots = groups * CAP

    short = dest.shape[0] <= 256

    def clear(n, _):
        owner[n] = -1
        return 0

    def one_source(source, _):
        count = jnp.int32(0)
        for k in range(per_source):
            row = source * per_source + k
            hit = dest[row] == me
            owner[jnp.where(hit, source * CAP + count, slots)] = seq[row]
            count = count + hit.astype(jnp.int32)
        return 0

    repeat(slots, clear, short)
    repeat(groups, one_source, short)


def repeat(count, step, unrolled, carry=0):
    if not unrolled:
        return lax.fori_loop(0, count, step, carry)
    for n in range(count):
        carry = step(n, carry)
    return carry


def plan_size(slots):
    return 3 * slots + 3


def plan_joins(owner, plan, seen, slots):
    short = slots <= 32
    spare = 3 * slots + 2

    def unseen(n, _):
        seen[n] = -1
        return 0

    def one_slot(n, counts):
        firsts, laters = counts
        sequence = owner[n]
        place = jnp.maximum(sequence, 0)
        earlier = seen[place]
        landed = sequence >= 0
        is_first = landed & (earlier < 0)
        is_later = landed & (earlier >= 0)
        mine = jnp.where(earlier < 0, n, earlier)
        seen[place] = jnp.where(landed, mine, earlier)
        plan[n] = mine
        plan[jnp.where(is_first, slots + firsts, spare)] = n
        plan[jnp.where(is_later, 2 * slots + laters, spare)] = n
        return firsts + is_first.astype(jnp.int32), laters + is_later.astype(jnp.int32)

    repeat(seen.shape[0], unseen, short)
    firsts, laters = repeat(slots, one_slot, short, (jnp.int32(0), jnp.int32(0)))
    plan[3 * slots] = firsts
    plan[3 * slots + 1] = laters


def gather_kernel(
    dest_hbm, seq_hbm, q_hbm, out_ref, dest, seq, owner, queries, sems, *, per_source
):
    me = lax.axis_index("gen")
    copies = [
        pltpu.make_async_copy(dest_hbm, dest, sems.at[0]),
        pltpu.make_async_copy(seq_hbm, seq, sems.at[1]),
        pltpu.make_async_copy(q_hbm, queries, sems.at[2]),
    ]
    for copy in copies:
        copy.start()
    copies[0].wait()
    copies[1].wait()
    fill_owner(dest, seq, me, owner, per_source)
    copies[2].wait()

    def one_slot(n, _):
        out_ref[n] = queries[jnp.maximum(owner[n], 0)]
        return 0

    lax.fori_loop(0, out_ref.shape[0], one_slot, 0, unroll=8)


def gather(dest, seq, queries, groups):
    slots = groups * CAP
    _, rows, head_dim = queries.shape
    return pl.pallas_call(
        functools.partial(gather_kernel, per_source=dest.shape[0] // groups),
        in_specs=[hbm()] * 3,
        out_specs=vmem(),
        out_shape=jax.ShapeDtypeStruct((slots, rows, head_dim), jnp.bfloat16),
        scratch_shapes=[
            pltpu.SMEM(dest.shape, jnp.int32),
            pltpu.SMEM(seq.shape, jnp.int32),
            pltpu.SMEM((slots + 1,), jnp.int32),
            pltpu.VMEM(queries.shape, jnp.bfloat16),
            pltpu.SemaphoreType.DMA((3,)),
        ],
        compiler_params=limit(4),
        cost_estimate=pl.CostEstimate(flops=0, bytes_accessed=4 * queries.size, transcendentals=0),
        name="gather_queries",
    )(stay(dest), stay(seq), stay(queries))


def make_bias(table_ref, length_ref, bias, page):
    blocks, seqs, width = bias.shape
    pool = padded(blocks * width // page)
    lengths = length_ref[...].astype(jnp.float32)
    page_id = lax.broadcasted_iota(jnp.int32, (pool, seqs), 0)
    used = jnp.zeros((pool, seqs), jnp.float32)
    for j in range(table_ref.shape[0]):
        inside = jnp.clip(lengths - float(page * j), 0.0, float(page))
        used = used + jnp.where(table_ref[j : j + 1, :] == page_id, inside, 0.0)
    used = used.T.astype(jnp.bfloat16)

    def one_block(b, _):
        key = lax.broadcasted_iota(jnp.int32, (pool, width), 1) + b * width
        owner = lax.broadcasted_iota(jnp.int32, (pool, width), 0)
        expand = jnp.where(key // page == owner, 1.0, 0.0).astype(jnp.bfloat16)
        count = jnp.dot(used, expand, preferred_element_type=jnp.float32)
        position = lax.broadcasted_iota(jnp.int32, (seqs, width), 1) % page
        bias[b] = jnp.where(position.astype(jnp.float32) < count, 0.0, NEGATIVE)
        return 0

    lax.fori_loop(0, blocks, one_block, 0)


class Attend:
    def __init__(self, packed, bias, keys, values, scores, tops, totals, scale, per_head):
        self.packed, self.bias, self.keys, self.values = packed, bias, keys, values
        self.scores, self.tops, self.totals = scores, tops, totals
        self.scale, self.per_head = scale, per_head
        self.blocks, self.seqs, self.width = bias.shape
        self.head_dim = packed.shape[2]
        self.rows = per_head * self.seqs
        self.pages = self.width // keys.shape[2]

    def start_scores(self, h):
        self.tops[h] = jnp.full((self.rows, LANES), NEGATIVE, jnp.float32)

    def score_block(self, h, b):
        keys = self.keys[h, pl.ds(b * self.pages, self.pages)].reshape(self.width, self.head_dim)
        s = lax.dot_general(
            self.packed[self.first + h], keys, (((1,), (1,)), ((), ())),
            preferred_element_type=jnp.float32,
        )
        s = s.reshape(self.per_head, self.seqs, self.width) + self.bias[b][None]
        s = s.reshape(self.rows, self.width)
        self.scores[h % 2][b] = s
        largest = s[:, :LANES]
        for t in range(1, self.width // LANES):
            largest = jnp.maximum(largest, s[:, t * LANES : (t + 1) * LANES])
        self.tops[h] = jnp.maximum(self.tops[h], largest)

    def start_values(self, h):
        top = jnp.max(self.tops[h], axis=1, keepdims=True)
        self.tops[h] = jnp.broadcast_to(top, (self.rows, LANES))
        self.totals[h] = jnp.zeros((self.rows, 2 * self.head_dim), jnp.float32)

    def weigh(self, weights, values):
        return jnp.dot(
            weights,
            jnp.concatenate([values, jnp.ones(values.shape, jnp.bfloat16)], axis=1),
            preferred_element_type=jnp.float32,
        )

    def value_block(self, h, b):
        scores, biggest = self.scores[h % 2], self.tops[h]
        values = self.values[h, pl.ds(b * self.pages, self.pages)]
        weights = []
        for t in range(self.width // LANES):
            s = scores[b, :, t * LANES : (t + 1) * LANES]
            weights.append(jnp.exp2((s - biggest) * self.scale).astype(jnp.bfloat16))
        self.totals[h] += self.weigh(
            jnp.concatenate(weights, axis=1), values.reshape(self.width, self.head_dim)
        )

    def run(self, first, count, keys_ready, values_ready, done):
        self.first = first
        for h in range(count + 1):
            if h < count:
                self.start_scores(h)
                keys_ready(h, 0)
            if h > 0:
                values_ready(h - 1)
                self.start_values(h - 1)

            def one_block(b, _, h=h):
                if h < count:
                    self.score_block(h, b)
                if h > 0:
                    self.value_block(h - 1, b)
                return 0

            if h < count:
                keys_ready(h, 1)
            lax.fori_loop(0, self.blocks, one_block, 0)
            if h > 0:
                done(h - 1)


def attend_scratch(seqs, per_head, pool, page, head_dim, pairs):
    keys = pool * page
    width = keys // 2
    rows = per_head * seqs
    scores = [pltpu.VMEM((keys // width, rows, width), jnp.float32) for _ in range(pairs)]
    return scores


def start_all(copies):
    for copy in copies:
        copy.start()


def wait_all(copies):
    for copy in copies:
        copy.wait()


def key_part(hbm_ref, head, target, sems, part):
    half = target.shape[0] // 2
    pages = pl.ds(part * half, half)
    return pltpu.make_async_copy(hbm_ref.at[pages, head], target.at[pages], sems.at[part])


def early_kernel(
    table_hbm, length_hbm, q_hbm, pages_hbm, dest_hbm, seq_hbm, x_hbm, k_hbm, v_hbm, w_hbm, *refs,
    tp, scale, count, per_head,
):
    outs = 2 if count else 0
    local_hbm = refs[:outs]
    owner_hbm, plan_hbm, packed_hbm, send_ref, move_keys, move_values = refs[outs : outs + 6]
    (table, lengths, pages, raw, query, packed, bias, x, dest, seq, owner, plan, seen, w, keys, values,
     small_sems, key_sems, value_sems, move_sems, w_sems, out_sems, *attend_refs) = refs[outs + 6 :]
    pairs = min(count, 2)
    blocks, _, width = w.shape
    moves = move_keys.shape[0]
    per_owner = blocks // (tp - 1)
    columns = per_owner * width
    me, place = lax.axis_index("gen"), lax.axis_index("tp")
    small = [
        pltpu.make_async_copy(source, target, small_sems.at[k])
        for k, (source, target) in enumerate(
            [(table_hbm, table), (length_hbm, lengths), (q_hbm, raw), (pages_hbm, pages),
             (dest_hbm, dest), (seq_hbm, seq), (x_hbm, x)]
        )
    ]
    owner_copy = pltpu.make_async_copy(owner, owner_hbm, out_sems.at[4, 0])
    plan_copy = pltpu.make_async_copy(plan, plan_hbm, out_sems.at[0, 0])
    packed_copy = pltpu.make_async_copy(packed, packed_hbm, out_sems.at[3, 0])
    seqs = bias.shape[1]
    stride = query.shape[0] // seqs

    def pack(head):
        for r in range(per_head):
            rows = query[pl.ds(head * per_head + r, seqs, stride=stride), :]
            packed[head, pl.ds(r * seqs, seqs), :] = rows.astype(jnp.bfloat16)

    def key_copy(h, part):
        return key_part(k_hbm, h, keys.at[h], key_sems.at[h], part)

    def value_copy(h):
        return pltpu.make_async_copy(v_hbm.at[:, h], values.at[h], value_sems.at[h])

    def w_copy(b):
        target = lax.rem(place + 1 + b // per_owner, tp)
        start = pl.multiple_of(target * columns + b % per_owner * width, width)
        return pltpu.make_async_copy(w_hbm.at[:, pl.ds(start, width)], w.at[b], w_sems.at[b])

    def move_copies(k):
        page = pages[me * moves + k]
        return (
            pltpu.make_async_copy(k_hbm.at[page], move_keys.at[k], move_sems.at[0, k]),
            pltpu.make_async_copy(v_hbm.at[page], move_values.at[k], move_sems.at[1, k]),
        )

    def start_move(k, _):
        start_all(move_copies(k))
        return 0

    def wait_move(k, _):
        wait_all(move_copies(k))
        return 0

    def start_weights(start, stop):
        for b in range(start, stop):
            w_copy(b).start()

    start_all(small[:3])
    if count:
        key_copy(0, 0).start()
        key_copy(0, 1).start()
    start_all(small[3:6])
    wait_all(small[:2])
    if count:
        make_bias(table, lengths, bias, keys.shape[2])
    small[2].wait()
    query[...] = raw[...].astype(jnp.float32)
    for head in range(count):
        pack(head)
    if count:
        totals, tops = attend_refs[pairs:]
        attend = Attend(
            packed, bias, keys, values, attend_refs[:pairs], tops, totals, scale, per_head
        )

        def local_copies(h):
            return [
                pltpu.make_async_copy(totals.at[h], local_hbm[0].at[h], out_sems.at[1, h]),
                pltpu.make_async_copy(tops.at[h], local_hbm[1].at[h], out_sems.at[2, h]),
            ]

        def keys_ready(h, b):
            key_copy(h, b).wait()
            if b == 0:
                value_copy(h).start()
                if h + 1 < count:
                    key_copy(h + 1, 0).start()
                    key_copy(h + 1, 1).start()
                if h == count - 1:
                    small[6].start()
                    start_weights(0, (blocks + 1) // 2)

        def values_ready(h):
            value_copy(h).wait()
            if h == count - 1:
                start_weights((blocks + 1) // 2, blocks)
                small[3].wait()
                lax.fori_loop(0, moves, start_move, 0)

        attend.run(0, count, keys_ready, values_ready, lambda h: start_all(local_copies(h)))
    else:
        small[6].start()
        start_weights(0, blocks)
        small[3].wait()
        lax.fori_loop(0, moves, start_move, 0)
    for head in range(count, packed.shape[0]):
        pack(head)
    packed_copy.start()
    wait_all(small[4:])
    for b in range(blocks):
        w_copy(b).wait()
        product = jnp.dot(x[...], w[b], preferred_element_type=jnp.float32)
        part = slice(b % per_owner * width, (b % per_owner + 1) * width)
        send_ref[b // per_owner, :, part] = product.astype(jnp.bfloat16)
        if b == 0:
            fill_owner(dest, seq, me, owner, moves)
            plan_joins(owner, plan, seen, owner.shape[0] - 1)
            owner_copy.start()
            plan_copy.start()
    lax.fori_loop(0, moves, wait_move, 0)
    owner_copy.wait()
    plan_copy.wait()
    packed_copy.wait()
    for h in range(count):
        wait_all(local_copies(h))


def early_work(
    table, lengths, pages, queries, tokens, dest, seq, k_cache, v_cache, w_kv, groups, tp, count, scale
):
    seqs, stride, head_dim = queries.shape
    pool, kv_heads, page, _ = k_cache.shape
    per_head = stride // kv_heads
    rows, depth = tokens.shape
    moves, slots = pages.shape[0] // groups, groups * CAP
    columns = w_kv.shape[1] // tp
    width = min(512, columns)
    blocks = (tp - 1) * columns // width
    keys = pool * page
    held = max(count, 1)
    f32, bf16 = jnp.float32, jnp.bfloat16
    total_shape = (count, per_head * seqs, 2 * head_dim)
    top_shape = (count, per_head * seqs, LANES)
    local = [pltpu.HBM(total_shape, f32), pltpu.HBM(top_shape, f32)] if count else []
    scratch = [
        pltpu.VMEM(table.shape, jnp.int32),
        pltpu.VMEM(lengths.shape, jnp.int32),
        pltpu.SMEM(pages.shape, jnp.int32),
        pltpu.VMEM((seqs * stride, head_dim), bf16),
        pltpu.VMEM((seqs * stride, head_dim), f32),
        pltpu.VMEM((kv_heads, per_head * seqs, head_dim), bf16),
        pltpu.VMEM((2, seqs, keys // 2), f32),
        pltpu.VMEM((rows, depth), bf16),
        pltpu.SMEM(dest.shape, jnp.int32),
        pltpu.SMEM(seq.shape, jnp.int32),
        pltpu.SMEM((slots + 1,), jnp.int32),
        pltpu.SMEM((plan_size(slots),), jnp.int32),
        pltpu.SMEM((seqs,), jnp.int32),
        pltpu.VMEM((blocks, depth, width), bf16),
        pltpu.VMEM((held, pool, page, head_dim), bf16),
        pltpu.VMEM((held, pool, page, head_dim), bf16),
        pltpu.SemaphoreType.DMA((7,)),
        pltpu.SemaphoreType.DMA((held, 2)),
        pltpu.SemaphoreType.DMA((held,)),
        pltpu.SemaphoreType.DMA((2, moves)),
        pltpu.SemaphoreType.DMA((blocks,)),
        pltpu.SemaphoreType.DMA((5, held)),
    ]
    if count:
        scratch += attend_scratch(seqs, per_head, pool, page, head_dim, min(count, 2))
        scratch += [pltpu.VMEM(total_shape, f32), pltpu.VMEM(top_shape, f32)]
    return pl.pallas_call(
        functools.partial(early_kernel, tp=tp, scale=scale, count=count, per_head=per_head),
        in_specs=[hbm()] * 10,
        out_specs=[hbm()] * (len(local) + 3) + [vmem()] * 3,
        out_shape=local + [
            pltpu.HBM((slots + 1,), jnp.int32),
            pltpu.HBM((plan_size(slots),), jnp.int32),
            pltpu.HBM((kv_heads, per_head * seqs, head_dim), bf16),
            jax.ShapeDtypeStruct((tp - 1, rows, columns), bf16),
            jax.ShapeDtypeStruct((moves,) + k_cache.shape[1:], bf16),
            jax.ShapeDtypeStruct((moves,) + k_cache.shape[1:], bf16),
        ],
        scratch_shapes=scratch,
        compiler_params=limit(40),
        cost_estimate=pl.CostEstimate(
            flops=tokens.size * w_kv.shape[1] + 8 * count * per_head * seqs * keys * head_dim,
            bytes_accessed=w_kv.size + 4 * count * keys * head_dim,
            transcendentals=count * per_head * seqs * keys,
        ),
        name="early_heads_and_sent_kv",
    )(
        stay(table), stay(lengths), stay(queries.reshape(seqs * stride, head_dim)), stay(pages),
        stay(dest), stay(seq), stay(tokens), stay(k_cache), stay(v_cache), stay(w_kv),
    )


def late_kernel(
    table_hbm, length_hbm, q_hbm, k_hbm, v_hbm, x_hbm, w_hbm, *refs, scale, early, count, per_head
):
    ins = 2 if early else 0
    before_hbm = refs[:ins]
    totals, tops, packed, x, w = refs[ins : ins + 5]
    before = refs[ins + 5 : 2 * ins + 5]
    table, lengths, bias, keys, values, sems, key_sems, value_sems, *scores = refs[2 * ins + 5 :]
    columns = w.shape[1]
    start = pl.multiple_of(lax.axis_index("tp") * columns, columns)
    pairs_in = [
        (table_hbm, table), (length_hbm, lengths), (q_hbm, packed), (x_hbm, x),
        (w_hbm.at[:, pl.ds(start, columns)], w),
    ] + list(zip(before_hbm, before))
    small = [
        pltpu.make_async_copy(source, target, sems.at[k])
        for k, (source, target) in enumerate(pairs_in)
    ]

    def key_copy(h, part):
        return key_part(k_hbm, early + h, keys.at[h], key_sems.at[h], part)

    def value_copy(h):
        return pltpu.make_async_copy(v_hbm.at[:, early + h], values.at[h], value_sems.at[h])

    start_all(small[:3])
    key_copy(0, 0).start()
    key_copy(0, 1).start()
    wait_all(small[:2])
    make_bias(table, lengths, bias, keys.shape[2])
    small[2].wait()
    attend = Attend(packed, bias, keys, values, scores, tops, totals, scale, per_head)

    def keys_ready(h, b):
        key_copy(h, b).wait()
        if b == 0:
            value_copy(h).start()
            if h + 1 < count:
                key_copy(h + 1, 0).start()
                key_copy(h + 1, 1).start()
            if h == count - 1:
                start_all(small[3:])

    attend.run(early, count, keys_ready, lambda h: value_copy(h).wait(), lambda h: None)
    wait_all(small[3:])


def late_work(table, lengths, packed, k_cache, v_cache, tokens, w_kv, before, tp, early, scale):
    pool, kv_heads, page, head_dim = k_cache.shape
    _, rows, _ = packed.shape
    seqs = lengths.shape[1]
    per_head = rows // seqs
    count = kv_heads - early
    keys = pool * page
    f32, bf16 = jnp.float32, jnp.bfloat16
    return pl.pallas_call(
        functools.partial(late_kernel, scale=scale, early=early, count=count, per_head=per_head),
        in_specs=[hbm()] * (7 + len(before)),
        out_specs=[vmem()] * (5 + len(before)),
        out_shape=[
            jax.ShapeDtypeStruct((count, rows, 2 * head_dim), f32),
            jax.ShapeDtypeStruct((count, rows, LANES), f32),
            jax.ShapeDtypeStruct(packed.shape, bf16),
            jax.ShapeDtypeStruct(tokens.shape, bf16),
            jax.ShapeDtypeStruct((w_kv.shape[0], w_kv.shape[1] // tp), bf16),
        ] + [jax.ShapeDtypeStruct(array.shape, f32) for array in before],
        scratch_shapes=[
            pltpu.VMEM(table.shape, jnp.int32),
            pltpu.VMEM(lengths.shape, jnp.int32),
            pltpu.VMEM((2, seqs, keys // 2), f32),
            pltpu.VMEM((count, pool, page, head_dim), bf16),
            pltpu.VMEM((count, pool, page, head_dim), bf16),
            pltpu.SemaphoreType.DMA((7,)),
            pltpu.SemaphoreType.DMA((count, 2)),
            pltpu.SemaphoreType.DMA((count,)),
        ] + attend_scratch(seqs, per_head, pool, page, head_dim, min(count, 2)),
        compiler_params=limit(36),
        cost_estimate=pl.CostEstimate(
            flops=8 * count * rows * keys * head_dim,
            bytes_accessed=4 * count * keys * head_dim,
            transcendentals=count * rows * keys,
        ),
        name="late_heads",
    )(
        stay(table), stay(lengths), stay(packed), stay(k_cache), stay(v_cache), stay(tokens), stay(w_kv),
        *[stay(array) for array in before],
    )


def new_kernel(
    other_ref, packed, x, w, *refs, parts, per_head, steps, scale
):
    local = refs[: 2 * parts]
    new_hbm, state, state_lse, new, fresh, sem = refs[2 * parts :]
    seqs, stride, head_dim = state.shape
    flat = (seqs * stride, head_dim)
    rows, rows_lse = state.reshape(flat), state_lse.reshape(flat)
    width = 2 * head_dim
    head = 0
    for part in range(parts):
        totals, tops = local[2 * part], local[2 * part + 1]
        for h in range(totals.shape[0]):
            columns = slice(head * width, (head + 1) * width)
            if head % 2 == 0:
                both = jnp.dot(
                    x[...], w[:, head * width : (head + 2) * width], preferred_element_type=jnp.float32
                )
            partial = both[:, head % 2 * width : (head % 2 + 1) * width]
            for k in range(other_ref.shape[0]):
                partial = partial + other_ref[k, :, columns].astype(jnp.float32)
            rounded = partial.astype(jnp.bfloat16)
            new[:, columns] = rounded
            fresh[head, 0] = rounded[:, :head_dim].astype(jnp.float32)
            fresh[head, 1] = rounded[:, head_dim:].astype(jnp.float32)
            new_keys, new_values = [], []
            for j in range(steps):
                every = pl.ds(j, seqs, stride=steps)
                new_keys.append(fresh[head, 0, every, :])
                new_values.append(fresh[head, 1, every, :])
            for r in range(per_head):
                place = pl.ds(head * per_head + r, seqs, stride=stride)
                block = pl.ds(r * seqs, seqs)
                q = packed[head, block, :].astype(jnp.float32)
                scores = [
                    jnp.sum(q * new_keys[j], axis=1, keepdims=True) * scale
                    for j in range(r % steps + 1)
                ]
                biggest = tops[h, block, :] * scale
                top = biggest
                for s in scores:
                    top = jnp.maximum(top, s)
                factor = jnp.exp2(biggest - top)
                weight = factor * totals[h, block, head_dim:]
                summed = factor * totals[h, block, :head_dim]
                for j, s in enumerate(scores):
                    share = jnp.exp2(s - top)
                    weight = weight + share
                    summed = summed + share * new_values[j]
                rows[place, :] = summed / weight
                rows_lse[place, :] = top + jnp.log2(weight)
            head += 1
    copy = pltpu.make_async_copy(new, new_hbm, sem.at[0])
    copy.start()
    copy.wait()


def join_new(other, packed, x, w, local, seqs, per_head, steps, scale):
    kv_heads, rows, head_dim = packed.shape
    columns = w.shape[1]
    state = jax.ShapeDtypeStruct((seqs, padded(kv_heads * per_head), head_dim), jnp.float32)
    return pl.pallas_call(
        functools.partial(
            new_kernel, parts=len(local) // 2, per_head=per_head, steps=steps, scale=scale
        ),
        in_specs=[vmem()] * (4 + len(local)),
        out_specs=[hbm(), vmem(), vmem()],
        out_shape=[jax.ShapeDtypeStruct((x.shape[0], columns), jnp.bfloat16), state, state],
        scratch_shapes=[
            pltpu.VMEM((x.shape[0], columns), jnp.bfloat16),
            pltpu.VMEM((columns // (2 * head_dim), 2, x.shape[0], head_dim), jnp.float32),
            pltpu.SemaphoreType.DMA((1,)),
        ],
        compiler_params=limit(8),
        cost_estimate=pl.CostEstimate(
            flops=20 * packed.size + 2 * x.shape[0] * w.size,
            bytes_accessed=20 * packed.size,
            transcendentals=4 * packed.size,
        ),
        name="join_new",
    )(other, packed, x, w, *local)


def moved_kernel(dest_hbm, q_ref, keys, values, out_ref, dest_ref, slot, sem, *, scale):
    moves, kv_heads, page, head_dim = keys.shape
    rows = q_ref.shape[1]
    padding = out_ref.shape[1] - rows
    columns = kv_heads * page
    me = lax.axis_index("gen")
    dest_copy = pltpu.make_async_copy(dest_hbm, dest_ref, sem.at[0])
    dest_copy.start()
    out_ref[...] = jnp.zeros(out_ref.shape, jnp.bfloat16)
    row = lax.broadcasted_iota(jnp.int32, (rows, columns), 0)
    column = lax.broadcasted_iota(jnp.int32, (rows, columns), 1)
    other_head = jnp.where(row // (rows // kv_heads) == column // page, 0.0, NEGATIVE)
    tall = lax.broadcasted_iota(jnp.int32, (rows, LANES), 0)
    lane = lax.broadcasted_iota(jnp.int32, (rows, LANES), 1)
    spare = lax.broadcasted_iota(jnp.int32, (padding, LANES), 0)
    ones = jnp.ones((columns, head_dim), jnp.bfloat16)

    def one_move(k):
        s = lax.dot_general(
            q_ref[slot[k]],
            keys[k].reshape(columns, head_dim),
            (((1,), (1,)), ((), ())),
            preferred_element_type=jnp.float32,
        )
        s = s + other_head
        biggest = jnp.max(s, axis=1, keepdims=True)
        weights = jnp.exp2((s - biggest) * scale).astype(jnp.bfloat16)
        both = jnp.concatenate([values[k].reshape(columns, head_dim), ones], axis=1)
        summed = jnp.dot(weights, both, preferred_element_type=jnp.float32)
        weight_sum = summed[:, head_dim:]
        lse = biggest * scale + jnp.log2(weight_sum)
        lse = jnp.sum(jnp.where(tall == lane, lse, 0.0), axis=0, keepdims=True)
        high = lse.astype(jnp.bfloat16).astype(jnp.float32)
        middle = (lse - high).astype(jnp.bfloat16).astype(jnp.float32)
        low = lse - high - middle
        pieces = jnp.where(spare == 0, high, jnp.where(spare == 1, middle, low))
        result = jnp.concatenate([summed[:, :head_dim] / weight_sum, pieces], axis=0)
        return result.astype(jnp.bfloat16)

    dest_copy.wait()
    for k in range(moves):
        mine = dest_ref[me * moves + k]
        rank = jnp.int32(0)
        for j in range(k):
            rank = rank + (dest_ref[me * moves + j] == mine).astype(jnp.int32)
        slot[k] = mine * CAP + rank
    batch = min(16, moves)

    def some_moves(b, _):
        results = [one_move(b * batch + k) for k in range(batch)]
        for k in range(batch):
            out_ref[slot[b * batch + k]] = results[k]
        return 0

    lax.fori_loop(0, moves // batch, some_moves, 0)


def moved_attention(dest, received, move_keys, move_values, scale):
    moves, kv_heads, page, head_dim = move_keys.shape
    count, rows, _ = received.shape
    return pl.pallas_call(
        functools.partial(moved_kernel, scale=scale),
        in_specs=[hbm(), vmem(), vmem(), vmem()],
        out_specs=vmem(),
        out_shape=jax.ShapeDtypeStruct((count, answer_rows(rows), head_dim), jnp.bfloat16),
        scratch_shapes=[
            pltpu.SMEM(dest.shape, jnp.int32),
            pltpu.SMEM((moves,), jnp.int32),
            pltpu.SemaphoreType.DMA((1,)),
        ],
        compiler_params=limit(4),
        cost_estimate=pl.CostEstimate(
            flops=4 * moves * rows * kv_heads * page * head_dim,
            bytes_accessed=4 * received.size,
            transcendentals=moves * rows * kv_heads * page,
        ),
        name="moved_attention",
    )(dest, received, move_keys, move_values)


def join_kernel(
    owner_hbm, plan_hbm, state_ref, lse_ref, slot_ref, out_ref, owner_ref, plan, states,
    states_lse, come_lses, sems,
):
    seqs, rows, head_dim = out_ref.shape
    count = slot_ref.shape[0]
    copies = [
        pltpu.make_async_copy(owner_hbm, owner_ref, sems.at[0]),
        pltpu.make_async_copy(plan_hbm, plan, sems.at[1]),
    ]
    start_all(copies)
    real = pl.ds(0, rows)
    tall = lax.broadcasted_iota(jnp.int32, (rows, LANES), 0)
    lane = lax.broadcasted_iota(jnp.int32, (rows, LANES), 1)
    out_ref[...] = state_ref[:, :rows, :].astype(jnp.bfloat16)

    def answer_lse(n, _):
        pieces = slot_ref[n, pl.ds(rows // 8 * 8, slot_ref.shape[1] - rows // 8 * 8)]
        pieces = pieces.astype(jnp.float32)[rows % 8 :]
        packed = pieces[0:1] + pieces[1:2] + pieces[2:3]
        lse = jnp.sum(jnp.where(tall == lane, packed, 0.0), axis=1, keepdims=True)
        come_lses[n] = jnp.broadcast_to(lse, (rows, LANES))
        return 0

    lax.fori_loop(0, count, answer_lse, 0, unroll=8)
    wait_all(copies)

    def join(n, old_sum, old_lse):
        come_lse = come_lses[n]
        top = jnp.maximum(old_lse, come_lse)
        old = jnp.exp2(old_lse - top)
        come = jnp.exp2(come_lse - top)
        weight = old + come
        come_sum = slot_ref[n].astype(jnp.float32)[:rows]
        return (old * old_sum + come * come_sum) / weight, top + jnp.log2(weight)

    def every_slot(n, _):
        seq = jnp.maximum(owner_ref[n], 0)
        states[n], states_lse[n] = join(n, state_ref[seq, real], lse_ref[seq, real])
        return 0

    def later_slot(k, _):
        n = plan[2 * count + k]
        first = plan[n]
        states[first], states_lse[first] = join(n, states[first], states_lse[first])
        return 0

    def store_slot(k, _):
        n = plan[count + k]
        out_ref[owner_ref[n]] = states[n].astype(jnp.bfloat16)
        return 0

    lax.fori_loop(0, count, every_slot, 0, unroll=8)
    lax.fori_loop(0, plan[3 * count + 1], later_slot, 0)
    lax.fori_loop(0, plan[3 * count], store_slot, 0)


def join_moved(owner, plan, state, state_lse, answers, shape):
    slots = answers.shape[0]
    block = pltpu.VMEM((slots,) + shape[1:], jnp.float32)
    return pl.pallas_call(
        join_kernel,
        in_specs=[hbm()] * 2 + [vmem()] * 3,
        out_specs=vmem(),
        out_shape=jax.ShapeDtypeStruct(shape, jnp.bfloat16),
        scratch_shapes=[
            pltpu.SMEM(owner.shape, jnp.int32),
            pltpu.SMEM(plan.shape, jnp.int32),
            block, block, block,
            pltpu.SemaphoreType.DMA((2,)),
        ],
        compiler_params=limit(8),
        cost_estimate=pl.CostEstimate(
            flops=10 * state.size, bytes_accessed=10 * state.size, transcendentals=0
        ),
        name="join_moved",
    )(stay(owner), stay(plan), state, state_lse, answers)


def per_device(
    tokens_in, w_kv, queries, k_cache, v_cache, page_table, lengths, move_dest, move_page, move_seq
):
    groups = lax.axis_size("gen")
    tp = lax.axis_size("tp")
    seqs, steps, heads, head_dim = queries.shape
    kv_heads = k_cache.shape[1]
    scale = LOG2E / math.sqrt(head_dim)

    def exchange(array):
        return lax.all_to_all(array, "gen", split_axis=0, concat_axis=0, tiled=True)

    rows = queries.transpose(0, 2, 1, 3).reshape(seqs, heads * steps, head_dim)
    dest = move_dest.reshape(-1)
    to_send = gather(dest, move_seq, rows, groups)
    early = kv_heads // 2
    early_rows, to_send = lax.optimization_barrier((rows, to_send))
    received = exchange(to_send)
    table, lengths = page_table.T, lengths.reshape(1, seqs)
    *before, owner, plan, packed, partial, move_keys, move_values = early_work(
        table, lengths, move_page, early_rows, tokens_in, dest, move_seq, k_cache, v_cache, w_kv,
        groups, tp, early, scale,
    )
    pieces = []
    for k in range(1, tp):
        pairs = [(i, (i + k) % tp) for i in range(tp)]
        pieces.append(lax.ppermute(partial[k - 1], "tp", pairs))
    other = jnp.stack(pieces)
    answers = moved_attention(dest, received, move_keys, move_values, scale)
    packed, answers = lax.optimization_barrier((packed, answers))
    returned = exchange(answers)
    totals, tops, packed, x, w, *before = late_work(
        table, lengths, packed, k_cache, v_cache, tokens_in, w_kv, before, tp, early, scale
    )
    new_kv, state, state_lse = join_new(
        other, packed, x, w, before + [totals, tops], seqs, heads * steps // kv_heads, steps, scale
    )
    attended = join_moved(
        owner, plan, state, state_lse, returned, (seqs, heads * steps, head_dim)
    )
    attended = attended.reshape(seqs, heads, steps, head_dim).transpose(0, 2, 1, 3)
    return (attended, new_kv)


def solution(mesh):
    return jax.shard_map(
        per_device,
        mesh=mesh,
        in_specs=(
            P("gen", "tp"),
            P("tp", None),
            P("gen", None, "tp", None),
            P("gen", "tp", None, None),
            P("gen", "tp", None, None),
            P("gen", None),
            P("gen"),
            P(),
            P(),
            P(),
        ),
        out_specs=(P("gen", None, "tp", None), P("gen", "tp")),
        check_vma=False,
    )
```

```python
import functools
import math

import jax
import jax.numpy as jnp
from jax import lax
from jax.experimental import pallas as pl
from jax.experimental.pallas import tpu as pltpu
from jax.sharding import PartitionSpec as P

CAP = 2
NEGATIVE = -1e30
LOG2E = 1.4426950408889634
LANES = 128
MIB = 1024 * 1024


def vmem():
    return pl.BlockSpec(memory_space=pltpu.VMEM)


def hbm():
    return pl.BlockSpec(memory_space=pltpu.HBM)


def stay(array):
    return pltpu.with_memory_space_constraint(array, pltpu.HBM)


def limit(mib):
    return pltpu.CompilerParams(vmem_limit_bytes=mib * MIB)


def padded(rows):
    return (rows + 7) // 8 * 8


def answer_rows(rows):
    return CAP * padded(rows) + 8


def piece_mask(rows):
    tall = lax.broadcasted_iota(jnp.int32, (rows, LANES), 0)
    lane = lax.broadcasted_iota(jnp.int32, (rows, LANES), 1)
    return (lane == tall) | (lane == tall + rows) | (lane == tall + 2 * rows)


def fill_owner(dest, seq, me, owner, per_source):
    groups = dest.shape[0] // per_source
    slots = groups * CAP

    short = dest.shape[0] <= 256

    def clear(n, _):
        owner[n] = -1
        return 0

    def one_source(source, _):
        count = jnp.int32(0)
        for k in range(per_source):
            row = source * per_source + k
            hit = dest[row] == me
            owner[jnp.where(hit, source * CAP + count, slots)] = seq[row]
            count = count + hit.astype(jnp.int32)
        return 0

    repeat(slots, clear, short)
    repeat(groups, one_source, short)


def repeat(count, step, unrolled, carry=0):
    if not unrolled:
        return lax.fori_loop(0, count, step, carry)
    for n in range(count):
        carry = step(n, carry)
    return carry


def plan_size(slots):
    return 3 * slots + 3


def plan_joins(owner, plan, seen, slots):
    short = slots <= 32
    spare = 3 * slots + 2

    def unseen(n, _):
        seen[n] = -1
        return 0

    def one_slot(n, counts):
        firsts, laters = counts
        sequence = owner[n]
        place = jnp.maximum(sequence, 0)
        earlier = seen[place]
        landed = sequence >= 0
        is_first = landed & (earlier < 0)
        is_later = landed & (earlier >= 0)
        mine = jnp.where(earlier < 0, n, earlier)
        seen[place] = jnp.where(landed, mine, earlier)
        plan[n] = mine
        plan[jnp.where(is_first, slots + firsts, spare)] = n
        plan[jnp.where(is_later, 2 * slots + laters, spare)] = n
        return firsts + is_first.astype(jnp.int32), laters + is_later.astype(jnp.int32)

    repeat(seen.shape[0], unseen, short)
    firsts, laters = repeat(slots, one_slot, short, (jnp.int32(0), jnp.int32(0)))
    plan[3 * slots] = firsts
    plan[3 * slots + 1] = laters


def gather_kernel(
    dest_hbm, seq_hbm, q_hbm, out_ref, dest, seq, owner, queries, sems, *, per_source
):
    me = lax.axis_index("gen")
    copies = [
        pltpu.make_async_copy(dest_hbm, dest, sems.at[0]),
        pltpu.make_async_copy(seq_hbm, seq, sems.at[1]),
        pltpu.make_async_copy(q_hbm, queries, sems.at[2]),
    ]
    for copy in copies:
        copy.start()
    copies[0].wait()
    copies[1].wait()
    fill_owner(dest, seq, me, owner, per_source)
    copies[2].wait()

    def one_slot(n, _):
        out_ref[n] = queries[jnp.maximum(owner[n], 0)]
        return 0

    lax.fori_loop(0, out_ref.shape[0], one_slot, 0, unroll=8)


def gather(dest, seq, queries, groups):
    slots = groups * CAP
    _, rows, head_dim = queries.shape
    return pl.pallas_call(
        functools.partial(gather_kernel, per_source=dest.shape[0] // groups),
        in_specs=[hbm()] * 3,
        out_specs=vmem(),
        out_shape=jax.ShapeDtypeStruct((slots, rows, head_dim), jnp.bfloat16),
        scratch_shapes=[
            pltpu.SMEM(dest.shape, jnp.int32),
            pltpu.SMEM(seq.shape, jnp.int32),
            pltpu.SMEM((slots + 1,), jnp.int32),
            pltpu.VMEM(queries.shape, jnp.bfloat16),
            pltpu.SemaphoreType.DMA((3,)),
        ],
        compiler_params=limit(4),
        cost_estimate=pl.CostEstimate(flops=0, bytes_accessed=4 * queries.size, transcendentals=0),
        name="gather_queries",
    )(stay(dest), stay(seq), stay(queries))


def make_bias(table_ref, length_ref, bias, page):
    blocks, seqs, width = bias.shape
    pool = padded(blocks * width // page)
    lengths = length_ref[...].astype(jnp.float32)
    page_id = lax.broadcasted_iota(jnp.int32, (pool, seqs), 0)
    used = jnp.zeros((pool, seqs), jnp.float32)
    for j in range(table_ref.shape[0]):
        inside = jnp.clip(lengths - float(page * j), 0.0, float(page))
        used = used + jnp.where(table_ref[j : j + 1, :] == page_id, inside, 0.0)
    used = used.T.astype(jnp.bfloat16)

    def one_block(b, _):
        key = lax.broadcasted_iota(jnp.int32, (pool, width), 1) + b * width
        owner = lax.broadcasted_iota(jnp.int32, (pool, width), 0)
        expand = jnp.where(key // page == owner, 1.0, 0.0).astype(jnp.bfloat16)
        count = jnp.dot(used, expand, preferred_element_type=jnp.float32)
        position = lax.broadcasted_iota(jnp.int32, (seqs, width), 1) % page
        bias[b] = jnp.where(position.astype(jnp.float32) < count, 0.0, NEGATIVE)
        return 0

    lax.fori_loop(0, blocks, one_block, 0)


class Attend:
    def __init__(self, packed, bias, keys, values, scores, tops, totals, scale, per_head):
        self.packed, self.bias, self.keys, self.values = packed, bias, keys, values
        self.scores, self.tops, self.totals = scores, tops, totals
        self.scale, self.per_head = scale, per_head
        self.blocks, self.seqs, self.width = bias.shape
        self.head_dim = packed.shape[2]
        self.rows = per_head * self.seqs
        self.pages = self.width // keys.shape[2]

    def start_scores(self, h):
        self.tops[h] = jnp.full((self.rows, LANES), NEGATIVE, jnp.float32)

    def score_block(self, h, b):
        keys = self.keys[h, pl.ds(b * self.pages, self.pages)].reshape(self.width, self.head_dim)
        s = lax.dot_general(
            self.packed[self.first + h], keys, (((1,), (1,)), ((), ())),
            preferred_element_type=jnp.float32,
        )
        s = s.reshape(self.per_head, self.seqs, self.width) + self.bias[b][None]
        s = s.reshape(self.rows, self.width)
        self.scores[h % 2][b] = s
        largest = s[:, :LANES]
        for t in range(1, self.width // LANES):
            largest = jnp.maximum(largest, s[:, t * LANES : (t + 1) * LANES])
        self.tops[h] = jnp.maximum(self.tops[h], largest)

    def start_values(self, h):
        top = jnp.max(self.tops[h], axis=1, keepdims=True)
        self.tops[h] = jnp.broadcast_to(top, (self.rows, LANES))
        self.totals[h] = jnp.zeros((self.rows, 2 * self.head_dim), jnp.float32)

    def weigh(self, weights, values):
        return jnp.dot(
            weights,
            jnp.concatenate([values, jnp.ones(values.shape, jnp.bfloat16)], axis=1),
            preferred_element_type=jnp.float32,
        )

    def value_block(self, h, b):
        scores, biggest = self.scores[h % 2], self.tops[h]
        values = self.values[h, pl.ds(b * self.pages, self.pages)]
        weights = []
        for t in range(self.width // LANES):
            s = scores[b, :, t * LANES : (t + 1) * LANES]
            weights.append(jnp.exp2((s - biggest) * self.scale).astype(jnp.bfloat16))
        self.totals[h] += self.weigh(
            jnp.concatenate(weights, axis=1), values.reshape(self.width, self.head_dim)
        )

    def run(self, first, count, keys_ready, values_ready, done):
        self.first = first
        for h in range(count + 1):
            if h < count:
                self.start_scores(h)
                keys_ready(h, 0)
            if h > 0:
                values_ready(h - 1)
                self.start_values(h - 1)

            def one_block(b, _, h=h):
                if h < count:
                    self.score_block(h, b)
                if h > 0:
                    self.value_block(h - 1, b)
                return 0

            if h < count:
                keys_ready(h, 1)
            lax.fori_loop(0, self.blocks, one_block, 0)
            if h > 0:
                done(h - 1)


def attend_scratch(seqs, per_head, pool, page, head_dim, pairs):
    keys = pool * page
    width = keys // 2
    rows = per_head * seqs
    scores = [pltpu.VMEM((keys // width, rows, width), jnp.float32) for _ in range(pairs)]
    return scores


def start_all(copies):
    for copy in copies:
        copy.start()


def wait_all(copies):
    for copy in copies:
        copy.wait()


def key_part(hbm_ref, head, target, sems, part):
    half = target.shape[0] // 2
    pages = pl.ds(part * half, half)
    return pltpu.make_async_copy(hbm_ref.at[pages, head], target.at[pages], sems.at[part])


def early_kernel(
    table_hbm, length_hbm, q_hbm, pages_hbm, dest_hbm, seq_hbm, x_hbm, k_hbm, v_hbm, w_hbm, *refs,
    tp, scale, count, per_head,
):
    outs = 2 if count else 0
    local_hbm = refs[:outs]
    owner_hbm, plan_hbm, packed_hbm, send_ref, move_keys, move_values = refs[outs : outs + 6]
    (table, lengths, pages, raw, query, packed, bias, x, dest, seq, owner, plan, seen, w, keys, values,
     small_sems, key_sems, value_sems, move_sems, w_sems, out_sems, *attend_refs) = refs[outs + 6 :]
    pairs = min(count, 2)
    blocks, _, width = w.shape
    moves = move_keys.shape[0]
    per_owner = blocks // (tp - 1)
    columns = per_owner * width
    me, place = lax.axis_index("gen"), lax.axis_index("tp")
    small = [
        pltpu.make_async_copy(source, target, small_sems.at[k])
        for k, (source, target) in enumerate(
            [(table_hbm, table), (length_hbm, lengths), (q_hbm, raw), (pages_hbm, pages),
             (dest_hbm, dest), (seq_hbm, seq), (x_hbm, x)]
        )
    ]
    owner_copy = pltpu.make_async_copy(owner, owner_hbm, out_sems.at[4, 0])
    plan_copy = pltpu.make_async_copy(plan, plan_hbm, out_sems.at[0, 0])
    packed_copy = pltpu.make_async_copy(packed, packed_hbm, out_sems.at[3, 0])
    seqs = bias.shape[1]
    stride = query.shape[0] // seqs

    def pack(head):
        for r in range(per_head):
            rows = query[pl.ds(head * per_head + r, seqs, stride=stride), :]
            packed[head, pl.ds(r * seqs, seqs), :] = rows.astype(jnp.bfloat16)

    def key_copy(h, part):
        return key_part(k_hbm, h, keys.at[h], key_sems.at[h], part)

    def value_copy(h):
        return pltpu.make_async_copy(v_hbm.at[:, h], values.at[h], value_sems.at[h])

    def w_copy(b):
        target = lax.rem(place + 1 + b // per_owner, tp)
        start = pl.multiple_of(target * columns + b % per_owner * width, width)
        return pltpu.make_async_copy(w_hbm.at[:, pl.ds(start, width)], w.at[b], w_sems.at[b])

    def move_copies(k):
        page = pages[me * moves + k]
        return (
            pltpu.make_async_copy(k_hbm.at[page], move_keys.at[k], move_sems.at[0, k]),
            pltpu.make_async_copy(v_hbm.at[page], move_values.at[k], move_sems.at[1, k]),
        )

    def start_move(k, _):
        start_all(move_copies(k))
        return 0

    def wait_move(k, _):
        wait_all(move_copies(k))
        return 0

    def start_weights(start, stop):
        for b in range(start, stop):
            w_copy(b).start()

    start_all(small[:3])
    if count:
        key_copy(0, 0).start()
        key_copy(0, 1).start()
    start_all(small[3:6])
    wait_all(small[:2])
    if count:
        make_bias(table, lengths, bias, keys.shape[2])
    small[2].wait()
    query[...] = raw[...].astype(jnp.float32)
    for head in range(count):
        pack(head)
    if count:
        totals, tops = attend_refs[pairs:]
        attend = Attend(
            packed, bias, keys, values, attend_refs[:pairs], tops, totals, scale, per_head
        )

        def local_copies(h):
            return [
                pltpu.make_async_copy(totals.at[h], local_hbm[0].at[h], out_sems.at[1, h]),
                pltpu.make_async_copy(tops.at[h], local_hbm[1].at[h], out_sems.at[2, h]),
            ]

        def keys_ready(h, b):
            key_copy(h, b).wait()
            if b == 0:
                value_copy(h).start()
                if h + 1 < count:
                    key_copy(h + 1, 0).start()
                    key_copy(h + 1, 1).start()
                if h == count - 1:
                    small[6].start()
                    start_weights(0, (blocks + 1) // 2)

        def values_ready(h):
            value_copy(h).wait()
            if h == count - 1:
                start_weights((blocks + 1) // 2, blocks)
                small[3].wait()
                lax.fori_loop(0, moves, start_move, 0)

        attend.run(0, count, keys_ready, values_ready, lambda h: start_all(local_copies(h)))
    else:
        small[6].start()
        start_weights(0, blocks)
        small[3].wait()
        lax.fori_loop(0, moves, start_move, 0)
    for head in range(count, packed.shape[0]):
        pack(head)
    packed_copy.start()
    wait_all(small[4:])
    for b in range(blocks):
        w_copy(b).wait()
        product = jnp.dot(x[...], w[b], preferred_element_type=jnp.float32)
        part = slice(b % per_owner * width, (b % per_owner + 1) * width)
        send_ref[b // per_owner, :, part] = product.astype(jnp.bfloat16)
        if b == 0:
            fill_owner(dest, seq, me, owner, moves)
            plan_joins(owner, plan, seen, owner.shape[0] - 1)
            owner_copy.start()
            plan_copy.start()
    lax.fori_loop(0, moves, wait_move, 0)
    owner_copy.wait()
    plan_copy.wait()
    packed_copy.wait()
    for h in range(count):
        wait_all(local_copies(h))


def early_work(
    table, lengths, pages, queries, tokens, dest, seq, k_cache, v_cache, w_kv, groups, tp, count, scale
):
    seqs, stride, head_dim = queries.shape
    pool, kv_heads, page, _ = k_cache.shape
    per_head = stride // kv_heads
    rows, depth = tokens.shape
    moves, slots = pages.shape[0] // groups, groups * CAP
    columns = w_kv.shape[1] // tp
    width = min(512, columns)
    blocks = (tp - 1) * columns // width
    keys = pool * page
    held = max(count, 1)
    f32, bf16 = jnp.float32, jnp.bfloat16
    total_shape = (count, per_head * seqs, 2 * head_dim)
    top_shape = (count, per_head * seqs, LANES)
    local = [pltpu.HBM(total_shape, f32), pltpu.HBM(top_shape, f32)] if count else []
    scratch = [
        pltpu.VMEM(table.shape, jnp.int32),
        pltpu.VMEM(lengths.shape, jnp.int32),
        pltpu.SMEM(pages.shape, jnp.int32),
        pltpu.VMEM((seqs * stride, head_dim), bf16),
        pltpu.VMEM((seqs * stride, head_dim), f32),
        pltpu.VMEM((kv_heads, per_head * seqs, head_dim), bf16),
        pltpu.VMEM((2, seqs, keys // 2), f32),
        pltpu.VMEM((rows, depth), bf16),
        pltpu.SMEM(dest.shape, jnp.int32),
        pltpu.SMEM(seq.shape, jnp.int32),
        pltpu.SMEM((slots + 1,), jnp.int32),
        pltpu.SMEM((plan_size(slots),), jnp.int32),
        pltpu.SMEM((seqs,), jnp.int32),
        pltpu.VMEM((blocks, depth, width), bf16),
        pltpu.VMEM((held, pool, page, head_dim), bf16),
        pltpu.VMEM((held, pool, page, head_dim), bf16),
        pltpu.SemaphoreType.DMA((7,)),
        pltpu.SemaphoreType.DMA((held, 2)),
        pltpu.SemaphoreType.DMA((held,)),
        pltpu.SemaphoreType.DMA((2, moves)),
        pltpu.SemaphoreType.DMA((blocks,)),
        pltpu.SemaphoreType.DMA((5, held)),
    ]
    if count:
        scratch += attend_scratch(seqs, per_head, pool, page, head_dim, min(count, 2))
        scratch += [pltpu.VMEM(total_shape, f32), pltpu.VMEM(top_shape, f32)]
    return pl.pallas_call(
        functools.partial(early_kernel, tp=tp, scale=scale, count=count, per_head=per_head),
        in_specs=[hbm()] * 10,
        out_specs=[hbm()] * (len(local) + 3) + [vmem()] * 3,
        out_shape=local + [
            pltpu.HBM((slots + 1,), jnp.int32),
            pltpu.HBM((plan_size(slots),), jnp.int32),
            pltpu.HBM((kv_heads, per_head * seqs, head_dim), bf16),
            jax.ShapeDtypeStruct((tp - 1, rows, columns), bf16),
            jax.ShapeDtypeStruct((moves,) + k_cache.shape[1:], bf16),
            jax.ShapeDtypeStruct((moves,) + k_cache.shape[1:], bf16),
        ],
        scratch_shapes=scratch,
        compiler_params=limit(40),
        cost_estimate=pl.CostEstimate(
            flops=tokens.size * w_kv.shape[1] + 8 * count * per_head * seqs * keys * head_dim,
            bytes_accessed=w_kv.size + 4 * count * keys * head_dim,
            transcendentals=count * per_head * seqs * keys,
        ),
        name="early_heads_and_sent_kv",
    )(
        stay(table), stay(lengths), stay(queries.reshape(seqs * stride, head_dim)), stay(pages),
        stay(dest), stay(seq), stay(tokens), stay(k_cache), stay(v_cache), stay(w_kv),
    )


def late_kernel(
    table_hbm, length_hbm, q_hbm, k_hbm, v_hbm, x_hbm, w_hbm, *refs, scale, early, count, per_head
):
    ins = 2 if early else 0
    before_hbm = refs[:ins]
    totals, tops, packed, x, w = refs[ins : ins + 5]
    before = refs[ins + 5 : 2 * ins + 5]
    table, lengths, bias, keys, values, sems, key_sems, value_sems, *scores = refs[2 * ins + 5 :]
    columns = w.shape[1]
    start = pl.multiple_of(lax.axis_index("tp") * columns, columns)
    pairs_in = [
        (table_hbm, table), (length_hbm, lengths), (q_hbm, packed), (x_hbm, x),
        (w_hbm.at[:, pl.ds(start, columns)], w),
    ] + list(zip(before_hbm, before))
    small = [
        pltpu.make_async_copy(source, target, sems.at[k])
        for k, (source, target) in enumerate(pairs_in)
    ]

    def key_copy(h, part):
        return key_part(k_hbm, early + h, keys.at[h], key_sems.at[h], part)

    def value_copy(h):
        return pltpu.make_async_copy(v_hbm.at[:, early + h], values.at[h], value_sems.at[h])

    start_all(small[:3])
    key_copy(0, 0).start()
    key_copy(0, 1).start()
    wait_all(small[:2])
    make_bias(table, lengths, bias, keys.shape[2])
    small[2].wait()
    attend = Attend(packed, bias, keys, values, scores, tops, totals, scale, per_head)

    def keys_ready(h, b):
        key_copy(h, b).wait()
        if b == 0:
            value_copy(h).start()
            if h + 1 < count:
                key_copy(h + 1, 0).start()
                key_copy(h + 1, 1).start()
            if h == count - 1:
                start_all(small[3:])

    attend.run(early, count, keys_ready, lambda h: value_copy(h).wait(), lambda h: None)
    wait_all(small[3:])


def late_work(table, lengths, packed, k_cache, v_cache, tokens, w_kv, before, tp, early, scale):
    pool, kv_heads, page, head_dim = k_cache.shape
    _, rows, _ = packed.shape
    seqs = lengths.shape[1]
    per_head = rows // seqs
    count = kv_heads - early
    keys = pool * page
    f32, bf16 = jnp.float32, jnp.bfloat16
    return pl.pallas_call(
        functools.partial(late_kernel, scale=scale, early=early, count=count, per_head=per_head),
        in_specs=[hbm()] * (7 + len(before)),
        out_specs=[vmem()] * (5 + len(before)),
        out_shape=[
            jax.ShapeDtypeStruct((count, rows, 2 * head_dim), f32),
            jax.ShapeDtypeStruct((count, rows, LANES), f32),
            jax.ShapeDtypeStruct(packed.shape, bf16),
            jax.ShapeDtypeStruct(tokens.shape, bf16),
            jax.ShapeDtypeStruct((w_kv.shape[0], w_kv.shape[1] // tp), bf16),
        ] + [jax.ShapeDtypeStruct(array.shape, f32) for array in before],
        scratch_shapes=[
            pltpu.VMEM(table.shape, jnp.int32),
            pltpu.VMEM(lengths.shape, jnp.int32),
            pltpu.VMEM((2, seqs, keys // 2), f32),
            pltpu.VMEM((count, pool, page, head_dim), bf16),
            pltpu.VMEM((count, pool, page, head_dim), bf16),
            pltpu.SemaphoreType.DMA((7,)),
            pltpu.SemaphoreType.DMA((count, 2)),
            pltpu.SemaphoreType.DMA((count,)),
        ] + attend_scratch(seqs, per_head, pool, page, head_dim, min(count, 2)),
        compiler_params=limit(36),
        cost_estimate=pl.CostEstimate(
            flops=8 * count * rows * keys * head_dim,
            bytes_accessed=4 * count * keys * head_dim,
            transcendentals=count * rows * keys,
        ),
        name="late_heads",
    )(
        stay(table), stay(lengths), stay(packed), stay(k_cache), stay(v_cache), stay(tokens), stay(w_kv),
        *[stay(array) for array in before],
    )


def new_kernel(
    other_ref, packed, x, w, *refs, parts, per_head, steps, scale
):
    local = refs[: 2 * parts]
    new_hbm, state, state_lse, new, fresh, sem = refs[2 * parts :]
    seqs, stride, head_dim = state.shape
    flat = (seqs * stride, head_dim)
    rows, rows_lse = state.reshape(flat), state_lse.reshape(flat)
    width = 2 * head_dim
    head = 0
    for part in range(parts):
        totals, tops = local[2 * part], local[2 * part + 1]
        for h in range(totals.shape[0]):
            columns = slice(head * width, (head + 1) * width)
            if head % 2 == 0:
                both = jnp.dot(
                    x[...], w[:, head * width : (head + 2) * width], preferred_element_type=jnp.float32
                )
            partial = both[:, head % 2 * width : (head % 2 + 1) * width]
            for k in range(other_ref.shape[0]):
                partial = partial + other_ref[k, :, columns].astype(jnp.float32)
            rounded = partial.astype(jnp.bfloat16)
            new[:, columns] = rounded
            fresh[head, 0] = rounded[:, :head_dim].astype(jnp.float32)
            fresh[head, 1] = rounded[:, head_dim:].astype(jnp.float32)
            new_keys, new_values = [], []
            for j in range(steps):
                every = pl.ds(j, seqs, stride=steps)
                new_keys.append(fresh[head, 0, every, :])
                new_values.append(fresh[head, 1, every, :])
            for r in range(per_head):
                place = pl.ds(head * per_head + r, seqs, stride=stride)
                block = pl.ds(r * seqs, seqs)
                q = packed[head, block, :].astype(jnp.float32)
                scores = [
                    jnp.sum(q * new_keys[j], axis=1, keepdims=True) * scale
                    for j in range(r % steps + 1)
                ]
                biggest = tops[h, block, :] * scale
                top = biggest
                for s in scores:
                    top = jnp.maximum(top, s)
                factor = jnp.exp2(biggest - top)
                weight = factor * totals[h, block, head_dim:]
                summed = factor * totals[h, block, :head_dim]
                for j, s in enumerate(scores):
                    share = jnp.exp2(s - top)
                    weight = weight + share
                    summed = summed + share * new_values[j]
                rows[place, :] = summed / weight
                rows_lse[place, :] = top + jnp.log2(weight)
            head += 1
    copy = pltpu.make_async_copy(new, new_hbm, sem.at[0])
    copy.start()
    copy.wait()


def join_new(other, packed, x, w, local, seqs, per_head, steps, scale):
    kv_heads, rows, head_dim = packed.shape
    columns = w.shape[1]
    state = jax.ShapeDtypeStruct((seqs, padded(kv_heads * per_head), head_dim), jnp.float32)
    return pl.pallas_call(
        functools.partial(
            new_kernel, parts=len(local) // 2, per_head=per_head, steps=steps, scale=scale
        ),
        in_specs=[vmem()] * (4 + len(local)),
        out_specs=[hbm(), vmem(), vmem()],
        out_shape=[jax.ShapeDtypeStruct((x.shape[0], columns), jnp.bfloat16), state, state],
        scratch_shapes=[
            pltpu.VMEM((x.shape[0], columns), jnp.bfloat16),
            pltpu.VMEM((columns // (2 * head_dim), 2, x.shape[0], head_dim), jnp.float32),
            pltpu.SemaphoreType.DMA((1,)),
        ],
        compiler_params=limit(8),
        cost_estimate=pl.CostEstimate(
            flops=20 * packed.size + 2 * x.shape[0] * w.size,
            bytes_accessed=20 * packed.size,
            transcendentals=4 * packed.size,
        ),
        name="join_new",
    )(other, packed, x, w, *local)


def moved_kernel(
    dest_hbm, q_ref, keys, values, out_ref, dest_ref, slot, place, lse_place, flat, sem, *, scale
):
    moves, kv_heads, page, head_dim = keys.shape
    rows = q_ref.shape[1]
    columns = kv_heads * page
    me = lax.axis_index("gen")
    dest_copy = pltpu.make_async_copy(dest_hbm, dest_ref, sem.at[0])
    dest_copy.start()
    flat[...] = jnp.zeros(flat.shape, jnp.float32)
    row = lax.broadcasted_iota(jnp.int32, (rows, columns), 0)
    column = lax.broadcasted_iota(jnp.int32, (rows, columns), 1)
    other_head = jnp.where(row // (rows // kv_heads) == column // page, 0.0, NEGATIVE)
    lane = lax.broadcasted_iota(jnp.int32, (rows, LANES), 1)
    mask = piece_mask(rows)
    ones = jnp.ones((columns, head_dim), jnp.bfloat16)

    def one_move(k):
        s = lax.dot_general(
            q_ref[slot[k]],
            keys[k].reshape(columns, head_dim),
            (((1,), (1,)), ((), ())),
            preferred_element_type=jnp.float32,
        )
        s = s + other_head
        biggest = jnp.max(s, axis=1, keepdims=True)
        weights = jnp.exp2((s - biggest) * scale).astype(jnp.bfloat16)
        both = jnp.concatenate([values[k].reshape(columns, head_dim), ones], axis=1)
        summed = jnp.dot(weights, both, preferred_element_type=jnp.float32)
        weight_sum = summed[:, head_dim:]
        lse = biggest * scale + jnp.log2(weight_sum)
        high = lse.astype(jnp.bfloat16).astype(jnp.float32)
        middle = (lse - high).astype(jnp.bfloat16).astype(jnp.float32)
        low = lse - high - middle
        piece = jnp.where(lane < rows, high, jnp.where(lane < 2 * rows, middle, low))
        return (
            summed[:, :head_dim] / weight_sum,
            jnp.sum(jnp.where(mask, piece, 0.0), axis=0, keepdims=True),
        )

    dest_copy.wait()
    for k in range(moves):
        mine = dest_ref[me * moves + k]
        rank = jnp.int32(0)
        for j in range(k):
            rank = rank + (dest_ref[me * moves + j] == mine).astype(jnp.int32)
        slot[k] = mine * CAP + rank
        first = mine * answer_rows(rows)
        place[k] = first + rank * padded(rows)
        lse_place[k] = first + CAP * padded(rows) + rank
    batch = min(16, moves)

    def some_moves(b, _):
        results = [one_move(b * batch + k) for k in range(batch)]
        for k, (result, lse) in enumerate(results):
            move = b * batch + k
            flat[pl.ds(pl.multiple_of(place[move], 8), rows), :] = result
            flat[pl.ds(lse_place[move], 1), :] = lse
        return 0

    lax.fori_loop(0, moves // batch, some_moves, 0)
    out_ref[...] = flat[...].astype(jnp.bfloat16)


def moved_attention(dest, received, move_keys, move_values, scale):
    moves, kv_heads, page, head_dim = move_keys.shape
    count, rows, _ = received.shape
    shape = (count // CAP * answer_rows(rows), head_dim)
    return pl.pallas_call(
        functools.partial(moved_kernel, scale=scale),
        in_specs=[hbm(), vmem(), vmem(), vmem()],
        out_specs=vmem(),
        out_shape=jax.ShapeDtypeStruct(shape, jnp.bfloat16),
        scratch_shapes=[
            pltpu.SMEM(dest.shape, jnp.int32),
            pltpu.SMEM((moves,), jnp.int32),
            pltpu.SMEM((moves,), jnp.int32),
            pltpu.SMEM((moves,), jnp.int32),
            pltpu.VMEM(shape, jnp.float32),
            pltpu.SemaphoreType.DMA((1,)),
        ],
        compiler_params=limit(4),
        cost_estimate=pl.CostEstimate(
            flops=4 * moves * rows * kv_heads * page * head_dim,
            bytes_accessed=4 * received.size,
            transcendentals=moves * rows * kv_heads * page,
        ),
        name="moved_attention",
    )(dest, received, move_keys, move_values)


def join_kernel(
    owner_hbm, plan_hbm, state_ref, lse_ref, slot_ref, out_ref, owner_ref, plan, states,
    states_lse, come_lses, flat, sems,
):
    seqs, rows, head_dim = out_ref.shape
    count = states.shape[0]
    copies = [
        pltpu.make_async_copy(owner_hbm, owner_ref, sems.at[0]),
        pltpu.make_async_copy(plan_hbm, plan, sems.at[1]),
    ]
    start_all(copies)
    real = pl.ds(0, rows)
    mask = piece_mask(rows)
    out_ref[...] = state_ref[:, :rows, :].astype(jnp.bfloat16)
    flat[...] = slot_ref[...].astype(jnp.float32)

    def answer_lse(n, _):
        row = n // CAP * answer_rows(rows) + CAP * padded(rows) + n % CAP
        lse = jnp.sum(jnp.where(mask, flat[pl.ds(row, 1), :], 0.0), axis=1, keepdims=True)
        come_lses[n] = jnp.broadcast_to(lse, (rows, LANES))
        return 0

    lax.fori_loop(0, count, answer_lse, 0, unroll=8)
    wait_all(copies)

    def join(n, old_sum, old_lse):
        come_lse = come_lses[n]
        top = jnp.maximum(old_lse, come_lse)
        old = jnp.exp2(old_lse - top)
        come = jnp.exp2(come_lse - top)
        weight = old + come
        place = n // CAP * answer_rows(rows) + n % CAP * padded(rows)
        come_sum = flat[pl.ds(pl.multiple_of(place, 8), rows), :]
        return (old * old_sum + come * come_sum) / weight, top + jnp.log2(weight)

    def every_slot(n, _):
        seq = jnp.maximum(owner_ref[n], 0)
        states[n], states_lse[n] = join(n, state_ref[seq, real], lse_ref[seq, real])
        return 0

    def later_slot(k, _):
        n = plan[2 * count + k]
        first = plan[n]
        states[first], states_lse[first] = join(n, states[first], states_lse[first])
        return 0

    def store_slot(k, _):
        n = plan[count + k]
        out_ref[owner_ref[n]] = states[n].astype(jnp.bfloat16)
        return 0

    lax.fori_loop(0, count, every_slot, 0, unroll=8)
    lax.fori_loop(0, plan[3 * count + 1], later_slot, 0)
    lax.fori_loop(0, plan[3 * count], store_slot, 0)


def join_moved(owner, plan, state, state_lse, answers, shape):
    slots = answers.shape[0] // answer_rows(shape[1]) * CAP
    block = pltpu.VMEM((slots,) + shape[1:], jnp.float32)
    return pl.pallas_call(
        join_kernel,
        in_specs=[hbm()] * 2 + [vmem()] * 3,
        out_specs=vmem(),
        out_shape=jax.ShapeDtypeStruct(shape, jnp.bfloat16),
        scratch_shapes=[
            pltpu.SMEM(owner.shape, jnp.int32),
            pltpu.SMEM(plan.shape, jnp.int32),
            block, block, block,
            pltpu.VMEM(answers.shape, jnp.float32),
            pltpu.SemaphoreType.DMA((2,)),
        ],
        compiler_params=limit(8),
        cost_estimate=pl.CostEstimate(
            flops=10 * state.size, bytes_accessed=10 * state.size, transcendentals=0
        ),
        name="join_moved",
    )(stay(owner), stay(plan), state, state_lse, answers)


def per_device(
    tokens_in, w_kv, queries, k_cache, v_cache, page_table, lengths, move_dest, move_page, move_seq
):
    groups = lax.axis_size("gen")
    tp = lax.axis_size("tp")
    seqs, steps, heads, head_dim = queries.shape
    kv_heads = k_cache.shape[1]
    scale = LOG2E / math.sqrt(head_dim)

    def exchange(array):
        return lax.all_to_all(array, "gen", split_axis=0, concat_axis=0, tiled=True)

    rows = queries.transpose(0, 2, 1, 3).reshape(seqs, heads * steps, head_dim)
    dest = move_dest.reshape(-1)
    to_send = gather(dest, move_seq, rows, groups)
    early = kv_heads // 2
    early_rows, to_send = lax.optimization_barrier((rows, to_send))
    received = exchange(to_send)
    table, lengths = page_table.T, lengths.reshape(1, seqs)
    *before, owner, plan, packed, partial, move_keys, move_values = early_work(
        table, lengths, move_page, early_rows, tokens_in, dest, move_seq, k_cache, v_cache, w_kv,
        groups, tp, early, scale,
    )
    pieces = []
    for k in range(1, tp):
        pairs = [(i, (i + k) % tp) for i in range(tp)]
        pieces.append(lax.ppermute(partial[k - 1], "tp", pairs))
    other = jnp.stack(pieces)
    answers = moved_attention(dest, received, move_keys, move_values, scale)
    packed, answers = lax.optimization_barrier((packed, answers))
    returned = exchange(answers)
    totals, tops, packed, x, w, *before = late_work(
        table, lengths, packed, k_cache, v_cache, tokens_in, w_kv, before, tp, early, scale
    )
    new_kv, state, state_lse = join_new(
        other, packed, x, w, before + [totals, tops], seqs, heads * steps // kv_heads, steps, scale
    )
    attended = join_moved(
        owner, plan, state, state_lse, returned, (seqs, heads * steps, head_dim)
    )
    attended = attended.reshape(seqs, heads, steps, head_dim).transpose(0, 2, 1, 3)
    return (attended, new_kv)


def solution(mesh):
    return jax.shard_map(
        per_device,
        mesh=mesh,
        in_specs=(
            P("gen", "tp"),
            P("tp", None),
            P("gen", None, "tp", None),
            P("gen", "tp", None, None),
            P("gen", "tp", None, None),
            P("gen", None),
            P("gen"),
            P(),
            P(),
            P(),
        ),
        out_specs=(P("gen", None, "tp", None), P("gen", "tp")),
        check_vma=False,
    )
```

```python
import functools
import math

import jax
import jax.numpy as jnp
from jax import lax
from jax.experimental import pallas as pl
from jax.experimental.pallas import tpu as pltpu
from jax.sharding import PartitionSpec as P

CAP = 2
NEGATIVE = -1e30
LOG2E = 1.4426950408889634
LANES = 128
MIB = 1024 * 1024


def vmem():
    return pl.BlockSpec(memory_space=pltpu.VMEM)


def hbm():
    return pl.BlockSpec(memory_space=pltpu.HBM)


def stay(array):
    return pltpu.with_memory_space_constraint(array, pltpu.HBM)


def limit(mib):
    return pltpu.CompilerParams(vmem_limit_bytes=mib * MIB)


def padded(rows):
    return (rows + 7) // 8 * 8


def answer_rows(rows):
    return CAP * padded(rows) + 8


def piece_mask(rows):
    tall = lax.broadcasted_iota(jnp.int32, (rows, LANES), 0)
    lane = lax.broadcasted_iota(jnp.int32, (rows, LANES), 1)
    return (lane == tall) | (lane == tall + rows) | (lane == tall + 2 * rows)


def fill_owner(dest, seq, me, owner, per_source):
    groups = dest.shape[0] // per_source
    slots = groups * CAP

    short = dest.shape[0] <= 256

    def clear(n, _):
        owner[n] = -1
        return 0

    def one_source(source, _):
        count = jnp.int32(0)
        for k in range(per_source):
            row = source * per_source + k
            hit = dest[row] == me
            owner[jnp.where(hit, source * CAP + count, slots)] = seq[row]
            count = count + hit.astype(jnp.int32)
        return 0

    repeat(slots, clear, short)
    repeat(groups, one_source, short)


def repeat(count, step, unrolled, carry=0):
    if not unrolled:
        return lax.fori_loop(0, count, step, carry)
    for n in range(count):
        carry = step(n, carry)
    return carry


def plan_size(slots):
    return 3 * slots + 3


def plan_joins(owner, plan, seen, slots):
    short = slots <= 32
    spare = 3 * slots + 2

    def unseen(n, _):
        seen[n] = -1
        return 0

    def one_slot(n, counts):
        firsts, laters = counts
        sequence = owner[n]
        place = jnp.maximum(sequence, 0)
        earlier = seen[place]
        landed = sequence >= 0
        is_first = landed & (earlier < 0)
        is_later = landed & (earlier >= 0)
        mine = jnp.where(earlier < 0, n, earlier)
        seen[place] = jnp.where(landed, mine, earlier)
        plan[n] = mine
        plan[jnp.where(is_first, slots + firsts, spare)] = n
        plan[jnp.where(is_later, 2 * slots + laters, spare)] = n
        return firsts + is_first.astype(jnp.int32), laters + is_later.astype(jnp.int32)

    repeat(seen.shape[0], unseen, short)
    firsts, laters = repeat(slots, one_slot, short, (jnp.int32(0), jnp.int32(0)))
    plan[3 * slots] = firsts
    plan[3 * slots + 1] = laters


def gather_kernel(
    dest_hbm, seq_hbm, q_hbm, out_ref, dest, seq, owner, queries, sems, *, per_source
):
    me = lax.axis_index("gen")
    copies = [
        pltpu.make_async_copy(dest_hbm, dest, sems.at[0]),
        pltpu.make_async_copy(seq_hbm, seq, sems.at[1]),
        pltpu.make_async_copy(q_hbm, queries, sems.at[2]),
    ]
    for copy in copies:
        copy.start()
    copies[0].wait()
    copies[1].wait()
    fill_owner(dest, seq, me, owner, per_source)
    copies[2].wait()

    def one_slot(n, _):
        out_ref[n] = queries[jnp.maximum(owner[n], 0)]
        return 0

    lax.fori_loop(0, out_ref.shape[0], one_slot, 0, unroll=8)


def gather(dest, seq, queries, groups):
    slots = groups * CAP
    _, rows, head_dim = queries.shape
    return pl.pallas_call(
        functools.partial(gather_kernel, per_source=dest.shape[0] // groups),
        in_specs=[hbm()] * 3,
        out_specs=vmem(),
        out_shape=jax.ShapeDtypeStruct((slots, rows, head_dim), jnp.bfloat16),
        scratch_shapes=[
            pltpu.SMEM(dest.shape, jnp.int32),
            pltpu.SMEM(seq.shape, jnp.int32),
            pltpu.SMEM((slots + 1,), jnp.int32),
            pltpu.VMEM(queries.shape, jnp.bfloat16),
            pltpu.SemaphoreType.DMA((3,)),
        ],
        compiler_params=limit(4),
        cost_estimate=pl.CostEstimate(flops=0, bytes_accessed=4 * queries.size, transcendentals=0),
        name="gather_queries",
    )(stay(dest), stay(seq), stay(queries))


def make_bias(table_ref, length_ref, bias, page):
    blocks, seqs, width = bias.shape
    pool = padded(blocks * width // page)
    lengths = length_ref[...].astype(jnp.float32)
    page_id = lax.broadcasted_iota(jnp.int32, (pool, seqs), 0)
    used = jnp.zeros((pool, seqs), jnp.float32)
    for j in range(table_ref.shape[0]):
        inside = jnp.clip(lengths - float(page * j), 0.0, float(page))
        used = used + jnp.where(table_ref[j : j + 1, :] == page_id, inside, 0.0)
    used = used.T.astype(jnp.bfloat16)

    def one_block(b, _):
        key = lax.broadcasted_iota(jnp.int32, (pool, width), 1) + b * width
        owner = lax.broadcasted_iota(jnp.int32, (pool, width), 0)
        expand = jnp.where(key // page == owner, 1.0, 0.0).astype(jnp.bfloat16)
        count = jnp.dot(used, expand, preferred_element_type=jnp.float32)
        position = lax.broadcasted_iota(jnp.int32, (seqs, width), 1) % page
        bias[b] = jnp.where(position.astype(jnp.float32) < count, 0.0, NEGATIVE)
        return 0

    lax.fori_loop(0, blocks, one_block, 0)


class Attend:
    def __init__(self, packed, bias, keys, values, scores, tops, totals, scale, per_head):
        self.packed, self.bias, self.keys, self.values = packed, bias, keys, values
        self.scores, self.tops, self.totals = scores, tops, totals
        self.scale, self.per_head = scale, per_head
        self.blocks, self.seqs, self.width = bias.shape
        self.head_dim = packed.shape[2]
        self.rows = per_head * self.seqs
        self.pages = self.width // keys.shape[2]

    def start_scores(self, h):
        self.tops[h] = jnp.full((self.rows, LANES), NEGATIVE, jnp.float32)

    def score_block(self, h, b):
        keys = self.keys[h, pl.ds(b * self.pages, self.pages)].reshape(self.width, self.head_dim)
        s = lax.dot_general(
            self.packed[self.first + h], keys, (((1,), (1,)), ((), ())),
            preferred_element_type=jnp.float32,
        )
        s = s.reshape(self.per_head, self.seqs, self.width) + self.bias[b][None]
        s = s.reshape(self.rows, self.width)
        self.scores[h % 2][b] = s
        largest = s[:, :LANES]
        for t in range(1, self.width // LANES):
            largest = jnp.maximum(largest, s[:, t * LANES : (t + 1) * LANES])
        self.tops[h] = jnp.maximum(self.tops[h], largest)

    def start_values(self, h):
        top = jnp.max(self.tops[h], axis=1, keepdims=True)
        self.tops[h] = jnp.broadcast_to(top, (self.rows, LANES))
        self.totals[h] = jnp.zeros((self.rows, 2 * self.head_dim), jnp.float32)

    def weigh(self, weights, values):
        return jnp.dot(
            weights,
            jnp.concatenate([values, jnp.ones(values.shape, jnp.bfloat16)], axis=1),
            preferred_element_type=jnp.float32,
        )

    def value_block(self, h, b):
        scores, biggest = self.scores[h % 2], self.tops[h]
        values = self.values[h, pl.ds(b * self.pages, self.pages)]
        weights = []
        for t in range(self.width // LANES):
            s = scores[b, :, t * LANES : (t + 1) * LANES]
            weights.append(jnp.exp2((s - biggest) * self.scale).astype(jnp.bfloat16))
        self.totals[h] += self.weigh(
            jnp.concatenate(weights, axis=1), values.reshape(self.width, self.head_dim)
        )

    def run(self, first, count, keys_ready, values_ready, done):
        self.first = first
        for h in range(count + 1):
            if h < count:
                self.start_scores(h)
                keys_ready(h, 0)
            if h > 0:
                values_ready(h - 1)
                self.start_values(h - 1)

            def one_block(b, _, h=h):
                if h < count:
                    self.score_block(h, b)
                if h > 0:
                    self.value_block(h - 1, b)
                return 0

            if h < count:
                keys_ready(h, 1)
            lax.fori_loop(0, self.blocks, one_block, 0)
            if h > 0:
                done(h - 1)


def attend_scratch(seqs, per_head, pool, page, head_dim, pairs):
    keys = pool * page
    width = keys // 2
    rows = per_head * seqs
    scores = [pltpu.VMEM((keys // width, rows, width), jnp.float32) for _ in range(pairs)]
    return scores


def start_all(copies):
    for copy in copies:
        copy.start()


def wait_all(copies):
    for copy in copies:
        copy.wait()


def key_part(hbm_ref, head, target, sems, part):
    half = target.shape[0] // 2
    pages = pl.ds(part * half, half)
    return pltpu.make_async_copy(hbm_ref.at[pages, head], target.at[pages], sems.at[part])


def early_kernel(
    table_hbm, length_hbm, q_hbm, pages_hbm, dest_hbm, seq_hbm, x_hbm, k_hbm, v_hbm, w_hbm, *refs,
    tp, scale, count, per_head,
):
    outs = 2 if count else 0
    local_hbm = refs[:outs]
    owner_hbm, plan_hbm, packed_hbm, send_ref, move_keys, move_values = refs[outs : outs + 6]
    (table, lengths, pages, raw, query, packed, bias, x, dest, seq, owner, plan, seen, w, keys, values,
     small_sems, key_sems, value_sems, move_sems, w_sems, out_sems, *attend_refs) = refs[outs + 6 :]
    pairs = min(count, 2)
    blocks, _, width = w.shape
    moves = move_keys.shape[0]
    per_owner = blocks // (tp - 1)
    columns = per_owner * width
    me, place = lax.axis_index("gen"), lax.axis_index("tp")
    small = [
        pltpu.make_async_copy(source, target, small_sems.at[k])
        for k, (source, target) in enumerate(
            [(table_hbm, table), (length_hbm, lengths), (q_hbm, raw), (pages_hbm, pages),
             (dest_hbm, dest), (seq_hbm, seq), (x_hbm, x)]
        )
    ]
    owner_copy = pltpu.make_async_copy(owner, owner_hbm, out_sems.at[4, 0])
    plan_copy = pltpu.make_async_copy(plan, plan_hbm, out_sems.at[0, 0])
    packed_copy = pltpu.make_async_copy(packed, packed_hbm, out_sems.at[3, 0])
    seqs = bias.shape[1]
    stride = query.shape[0] // seqs

    def pack(head):
        for r in range(per_head):
            rows = query[pl.ds(head * per_head + r, seqs, stride=stride), :]
            packed[head, pl.ds(r * seqs, seqs), :] = rows.astype(jnp.bfloat16)

    def key_copy(h, part):
        return key_part(k_hbm, h, keys.at[h], key_sems.at[h], part)

    def value_copy(h):
        return pltpu.make_async_copy(v_hbm.at[:, h], values.at[h], value_sems.at[h])

    def w_copy(b):
        target = lax.rem(place + 1 + b // per_owner, tp)
        start = pl.multiple_of(target * columns + b % per_owner * width, width)
        return pltpu.make_async_copy(w_hbm.at[:, pl.ds(start, width)], w.at[b], w_sems.at[b])

    def move_copies(k):
        page = pages[me * moves + k]
        return (
            pltpu.make_async_copy(k_hbm.at[page], move_keys.at[k], move_sems.at[0, k]),
            pltpu.make_async_copy(v_hbm.at[page], move_values.at[k], move_sems.at[1, k]),
        )

    def start_move(k, _):
        start_all(move_copies(k))
        return 0

    def wait_move(k, _):
        wait_all(move_copies(k))
        return 0

    def start_weights(start, stop):
        for b in range(start, stop):
            w_copy(b).start()

    start_all(small[:3])
    if count:
        key_copy(0, 0).start()
        key_copy(0, 1).start()
    start_all(small[3:6])
    wait_all(small[:2])
    if count:
        make_bias(table, lengths, bias, keys.shape[2])
    small[2].wait()
    query[...] = raw[...].astype(jnp.float32)
    for head in range(count):
        pack(head)
    if count:
        totals, tops = attend_refs[pairs:]
        attend = Attend(
            packed, bias, keys, values, attend_refs[:pairs], tops, totals, scale, per_head
        )

        def local_copies(h):
            return [
                pltpu.make_async_copy(totals.at[h], local_hbm[0].at[h], out_sems.at[1, h]),
                pltpu.make_async_copy(tops.at[h], local_hbm[1].at[h], out_sems.at[2, h]),
            ]

        def keys_ready(h, b):
            key_copy(h, b).wait()
            if b == 0:
                value_copy(h).start()
                if h + 1 < count:
                    key_copy(h + 1, 0).start()
                    key_copy(h + 1, 1).start()
                if h == count - 1:
                    small[6].start()
                    start_weights(0, (blocks + 1) // 2)

        def values_ready(h):
            value_copy(h).wait()
            if h == count - 1:
                start_weights((blocks + 1) // 2, blocks)
                small[3].wait()
                lax.fori_loop(0, moves, start_move, 0)

        attend.run(0, count, keys_ready, values_ready, lambda h: start_all(local_copies(h)))
    else:
        small[6].start()
        start_weights(0, blocks)
        small[3].wait()
        lax.fori_loop(0, moves, start_move, 0)
    for head in range(count, packed.shape[0]):
        pack(head)
    packed_copy.start()
    wait_all(small[4:])
    for b in range(blocks):
        w_copy(b).wait()
        product = jnp.dot(x[...], w[b], preferred_element_type=jnp.float32)
        part = slice(b % per_owner * width, (b % per_owner + 1) * width)
        send_ref[b // per_owner, :, part] = product.astype(jnp.bfloat16)
        if b == 0:
            fill_owner(dest, seq, me, owner, moves)
            plan_joins(owner, plan, seen, owner.shape[0] - 1)
            owner_copy.start()
            plan_copy.start()
    lax.fori_loop(0, moves, wait_move, 0)
    owner_copy.wait()
    plan_copy.wait()
    packed_copy.wait()
    for h in range(count):
        wait_all(local_copies(h))


def early_work(
    table, lengths, pages, queries, tokens, dest, seq, k_cache, v_cache, w_kv, groups, tp, count, scale
):
    seqs, stride, head_dim = queries.shape
    pool, kv_heads, page, _ = k_cache.shape
    per_head = stride // kv_heads
    rows, depth = tokens.shape
    moves, slots = pages.shape[0] // groups, groups * CAP
    columns = w_kv.shape[1] // tp
    width = min(512, columns)
    blocks = (tp - 1) * columns // width
    keys = pool * page
    held = max(count, 1)
    f32, bf16 = jnp.float32, jnp.bfloat16
    total_shape = (count, per_head * seqs, 2 * head_dim)
    top_shape = (count, per_head * seqs, LANES)
    local = [pltpu.HBM(total_shape, f32), pltpu.HBM(top_shape, f32)] if count else []
    scratch = [
        pltpu.VMEM(table.shape, jnp.int32),
        pltpu.VMEM(lengths.shape, jnp.int32),
        pltpu.SMEM(pages.shape, jnp.int32),
        pltpu.VMEM((seqs * stride, head_dim), bf16),
        pltpu.VMEM((seqs * stride, head_dim), f32),
        pltpu.VMEM((kv_heads, per_head * seqs, head_dim), bf16),
        pltpu.VMEM((2, seqs, keys // 2), f32),
        pltpu.VMEM((rows, depth), bf16),
        pltpu.SMEM(dest.shape, jnp.int32),
        pltpu.SMEM(seq.shape, jnp.int32),
        pltpu.SMEM((slots + 1,), jnp.int32),
        pltpu.SMEM((plan_size(slots),), jnp.int32),
        pltpu.SMEM((seqs,), jnp.int32),
        pltpu.VMEM((blocks, depth, width), bf16),
        pltpu.VMEM((held, pool, page, head_dim), bf16),
        pltpu.VMEM((held, pool, page, head_dim), bf16),
        pltpu.SemaphoreType.DMA((7,)),
        pltpu.SemaphoreType.DMA((held, 2)),
        pltpu.SemaphoreType.DMA((held,)),
        pltpu.SemaphoreType.DMA((2, moves)),
        pltpu.SemaphoreType.DMA((blocks,)),
        pltpu.SemaphoreType.DMA((5, held)),
    ]
    if count:
        scratch += attend_scratch(seqs, per_head, pool, page, head_dim, min(count, 2))
        scratch += [pltpu.VMEM(total_shape, f32), pltpu.VMEM(top_shape, f32)]
    return pl.pallas_call(
        functools.partial(early_kernel, tp=tp, scale=scale, count=count, per_head=per_head),
        in_specs=[hbm()] * 10,
        out_specs=[hbm()] * (len(local) + 3) + [vmem()] * 3,
        out_shape=local + [
            pltpu.HBM((slots + 1,), jnp.int32),
            pltpu.HBM((plan_size(slots),), jnp.int32),
            pltpu.HBM((kv_heads, per_head * seqs, head_dim), bf16),
            jax.ShapeDtypeStruct((tp - 1, rows, columns), bf16),
            jax.ShapeDtypeStruct((moves,) + k_cache.shape[1:], bf16),
            jax.ShapeDtypeStruct((moves,) + k_cache.shape[1:], bf16),
        ],
        scratch_shapes=scratch,
        compiler_params=limit(40),
        cost_estimate=pl.CostEstimate(
            flops=tokens.size * w_kv.shape[1] + 8 * count * per_head * seqs * keys * head_dim,
            bytes_accessed=w_kv.size + 4 * count * keys * head_dim,
            transcendentals=count * per_head * seqs * keys,
        ),
        name="early_heads_and_sent_kv",
    )(
        stay(table), stay(lengths), stay(queries.reshape(seqs * stride, head_dim)), stay(pages),
        stay(dest), stay(seq), stay(tokens), stay(k_cache), stay(v_cache), stay(w_kv),
    )


def late_kernel(
    table_hbm, length_hbm, q_hbm, k_hbm, v_hbm, x_hbm, w_hbm, *refs, scale, early, count, per_head
):
    ins = 2 if early else 0
    before_hbm = refs[:ins]
    totals, tops, packed, x, w = refs[ins : ins + 5]
    before = refs[ins + 5 : 2 * ins + 5]
    table, lengths, bias, keys, values, sems, key_sems, value_sems, *scores = refs[2 * ins + 5 :]
    columns = w.shape[1]
    start = pl.multiple_of(lax.axis_index("tp") * columns, columns)
    pairs_in = [
        (table_hbm, table), (length_hbm, lengths), (q_hbm, packed), (x_hbm, x),
        (w_hbm.at[:, pl.ds(start, columns)], w),
    ] + list(zip(before_hbm, before))
    small = [
        pltpu.make_async_copy(source, target, sems.at[k])
        for k, (source, target) in enumerate(pairs_in)
    ]

    def key_copy(h, part):
        return key_part(k_hbm, early + h, keys.at[h], key_sems.at[h], part)

    def value_copy(h):
        return pltpu.make_async_copy(v_hbm.at[:, early + h], values.at[h], value_sems.at[h])

    start_all(small[:3])
    key_copy(0, 0).start()
    key_copy(0, 1).start()
    wait_all(small[:2])
    make_bias(table, lengths, bias, keys.shape[2])
    small[2].wait()
    attend = Attend(packed, bias, keys, values, scores, tops, totals, scale, per_head)

    def keys_ready(h, b):
        key_copy(h, b).wait()
        if b == 0:
            value_copy(h).start()
            if h + 1 < count:
                key_copy(h + 1, 0).start()
                key_copy(h + 1, 1).start()
            if h == count - 1:
                start_all(small[3:])

    attend.run(early, count, keys_ready, lambda h: value_copy(h).wait(), lambda h: None)
    wait_all(small[3:])


def late_work(table, lengths, packed, k_cache, v_cache, tokens, w_kv, before, tp, early, scale):
    pool, kv_heads, page, head_dim = k_cache.shape
    _, rows, _ = packed.shape
    seqs = lengths.shape[1]
    per_head = rows // seqs
    count = kv_heads - early
    keys = pool * page
    f32, bf16 = jnp.float32, jnp.bfloat16
    return pl.pallas_call(
        functools.partial(late_kernel, scale=scale, early=early, count=count, per_head=per_head),
        in_specs=[hbm()] * (7 + len(before)),
        out_specs=[vmem()] * (5 + len(before)),
        out_shape=[
            jax.ShapeDtypeStruct((count, rows, 2 * head_dim), f32),
            jax.ShapeDtypeStruct((count, rows, LANES), f32),
            jax.ShapeDtypeStruct(packed.shape, bf16),
            jax.ShapeDtypeStruct(tokens.shape, bf16),
            jax.ShapeDtypeStruct((w_kv.shape[0], w_kv.shape[1] // tp), bf16),
        ] + [jax.ShapeDtypeStruct(array.shape, f32) for array in before],
        scratch_shapes=[
            pltpu.VMEM(table.shape, jnp.int32),
            pltpu.VMEM(lengths.shape, jnp.int32),
            pltpu.VMEM((2, seqs, keys // 2), f32),
            pltpu.VMEM((count, pool, page, head_dim), bf16),
            pltpu.VMEM((count, pool, page, head_dim), bf16),
            pltpu.SemaphoreType.DMA((7,)),
            pltpu.SemaphoreType.DMA((count, 2)),
            pltpu.SemaphoreType.DMA((count,)),
        ] + attend_scratch(seqs, per_head, pool, page, head_dim, min(count, 2)),
        compiler_params=limit(36),
        cost_estimate=pl.CostEstimate(
            flops=8 * count * rows * keys * head_dim,
            bytes_accessed=4 * count * keys * head_dim,
            transcendentals=count * rows * keys,
        ),
        name="late_heads",
    )(
        stay(table), stay(lengths), stay(packed), stay(k_cache), stay(v_cache), stay(tokens), stay(w_kv),
        *[stay(array) for array in before],
    )


def new_kernel(
    other_ref, packed, x, w, *refs, parts, per_head, steps, scale
):
    local = refs[: 2 * parts]
    new_hbm, state, state_lse, new, fresh, sem = refs[2 * parts :]
    seqs, stride, head_dim = state.shape
    flat = (seqs * stride, head_dim)
    rows, rows_lse = state.reshape(flat), state_lse.reshape(flat)
    width = 2 * head_dim
    head = 0
    copies = []
    for part in range(parts):
        totals, tops = local[2 * part], local[2 * part + 1]
        for h in range(totals.shape[0]):
            if head % 2 == 0:
                pair = slice(head * width, min((head + 2) * width, w.shape[1]))
                partial = jnp.dot(x[...], w[:, pair], preferred_element_type=jnp.float32)
                for k in range(other_ref.shape[0]):
                    partial = partial + other_ref[k, :, pair].astype(jnp.float32)
                both = partial.astype(jnp.bfloat16)
                new[:, pair] = both
                part = pl.ds(pair.start, pair.stop - pair.start)
                copies.append(
                    pltpu.make_async_copy(
                        new.at[:, part], new_hbm.at[:, part], sem.at[len(copies)]
                    )
                )
                copies[-1].start()
            rounded = both[:, head % 2 * width : (head % 2 + 1) * width]
            fresh[head, 0] = rounded[:, :head_dim].astype(jnp.float32)
            fresh[head, 1] = rounded[:, head_dim:].astype(jnp.float32)
            new_keys, new_values = [], []
            for j in range(steps):
                every = pl.ds(j, seqs, stride=steps)
                new_keys.append(fresh[head, 0, every, :])
                new_values.append(fresh[head, 1, every, :])
            for r in range(per_head):
                place = pl.ds(head * per_head + r, seqs, stride=stride)
                block = pl.ds(r * seqs, seqs)
                q = packed[head, block, :].astype(jnp.float32)
                scores = [
                    jnp.sum(q * new_keys[j], axis=1, keepdims=True) * scale
                    for j in range(r % steps + 1)
                ]
                biggest = tops[h, block, :] * scale
                top = biggest
                for s in scores:
                    top = jnp.maximum(top, s)
                factor = jnp.exp2(biggest - top)
                weight = factor * totals[h, block, head_dim:]
                summed = factor * totals[h, block, :head_dim]
                for j, s in enumerate(scores):
                    share = jnp.exp2(s - top)
                    weight = weight + share
                    summed = summed + share * new_values[j]
                rows[place, :] = summed / weight
                rows_lse[place, :] = top + jnp.log2(weight)
            head += 1
    wait_all(copies)


def join_new(other, packed, x, w, local, seqs, per_head, steps, scale):
    kv_heads, rows, head_dim = packed.shape
    columns = w.shape[1]
    state = jax.ShapeDtypeStruct((seqs, padded(kv_heads * per_head), head_dim), jnp.float32)
    return pl.pallas_call(
        functools.partial(
            new_kernel, parts=len(local) // 2, per_head=per_head, steps=steps, scale=scale
        ),
        in_specs=[vmem()] * (4 + len(local)),
        out_specs=[hbm(), vmem(), vmem()],
        out_shape=[jax.ShapeDtypeStruct((x.shape[0], columns), jnp.bfloat16), state, state],
        scratch_shapes=[
            pltpu.VMEM((x.shape[0], columns), jnp.bfloat16),
            pltpu.VMEM((columns // (2 * head_dim), 2, x.shape[0], head_dim), jnp.float32),
            pltpu.SemaphoreType.DMA(((kv_heads + 1) // 2,)),
        ],
        compiler_params=limit(8),
        cost_estimate=pl.CostEstimate(
            flops=20 * packed.size + 2 * x.shape[0] * w.size,
            bytes_accessed=20 * packed.size,
            transcendentals=4 * packed.size,
        ),
        name="join_new",
    )(other, packed, x, w, *local)


def moved_kernel(
    dest_hbm, q_ref, keys, values, out_ref, dest_ref, slot, place, lse_place, flat, sem, *, scale
):
    moves, kv_heads, page, head_dim = keys.shape
    rows = q_ref.shape[1]
    columns = kv_heads * page
    me = lax.axis_index("gen")
    dest_copy = pltpu.make_async_copy(dest_hbm, dest_ref, sem.at[0])
    dest_copy.start()
    flat[...] = jnp.zeros(flat.shape, jnp.float32)
    row = lax.broadcasted_iota(jnp.int32, (rows, columns), 0)
    column = lax.broadcasted_iota(jnp.int32, (rows, columns), 1)
    other_head = jnp.where(row // (rows // kv_heads) == column // page, 0.0, NEGATIVE)
    lane = lax.broadcasted_iota(jnp.int32, (rows, LANES), 1)
    mask = piece_mask(rows)
    ones = jnp.ones((columns, head_dim), jnp.bfloat16)

    def one_move(k):
        s = lax.dot_general(
            q_ref[slot[k]],
            keys[k].reshape(columns, head_dim),
            (((1,), (1,)), ((), ())),
            preferred_element_type=jnp.float32,
        )
        s = s + other_head
        biggest = jnp.max(s, axis=1, keepdims=True)
        weights = jnp.exp2((s - biggest) * scale).astype(jnp.bfloat16)
        both = jnp.concatenate([values[k].reshape(columns, head_dim), ones], axis=1)
        summed = jnp.dot(weights, both, preferred_element_type=jnp.float32)
        weight_sum = summed[:, head_dim:]
        lse = biggest * scale + jnp.log2(weight_sum)
        high = lse.astype(jnp.bfloat16).astype(jnp.float32)
        middle = (lse - high).astype(jnp.bfloat16).astype(jnp.float32)
        low = lse - high - middle
        piece = jnp.where(lane < rows, high, jnp.where(lane < 2 * rows, middle, low))
        return (
            summed[:, :head_dim] / weight_sum,
            jnp.sum(jnp.where(mask, piece, 0.0), axis=0, keepdims=True),
        )

    dest_copy.wait()
    for k in range(moves):
        mine = dest_ref[me * moves + k]
        rank = jnp.int32(0)
        for j in range(k):
            rank = rank + (dest_ref[me * moves + j] == mine).astype(jnp.int32)
        slot[k] = mine * CAP + rank
        first = mine * answer_rows(rows)
        place[k] = first + rank * padded(rows)
        lse_place[k] = first + CAP * padded(rows) + rank
    batch = min(16, moves)

    def some_moves(b, _):
        results = [one_move(b * batch + k) for k in range(batch)]
        for k, (result, lse) in enumerate(results):
            move = b * batch + k
            flat[pl.ds(pl.multiple_of(place[move], 8), rows), :] = result
            flat[pl.ds(lse_place[move], 1), :] = lse
        return 0

    lax.fori_loop(0, moves // batch, some_moves, 0)
    out_ref[...] = flat[...].astype(jnp.bfloat16)


def moved_attention(dest, received, move_keys, move_values, scale):
    moves, kv_heads, page, head_dim = move_keys.shape
    count, rows, _ = received.shape
    shape = (count // CAP * answer_rows(rows), head_dim)
    return pl.pallas_call(
        functools.partial(moved_kernel, scale=scale),
        in_specs=[hbm(), vmem(), vmem(), vmem()],
        out_specs=vmem(),
        out_shape=jax.ShapeDtypeStruct(shape, jnp.bfloat16),
        scratch_shapes=[
            pltpu.SMEM(dest.shape, jnp.int32),
            pltpu.SMEM((moves,), jnp.int32),
            pltpu.SMEM((moves,), jnp.int32),
            pltpu.SMEM((moves,), jnp.int32),
            pltpu.VMEM(shape, jnp.float32),
            pltpu.SemaphoreType.DMA((1,)),
        ],
        compiler_params=limit(4),
        cost_estimate=pl.CostEstimate(
            flops=4 * moves * rows * kv_heads * page * head_dim,
            bytes_accessed=4 * received.size,
            transcendentals=moves * rows * kv_heads * page,
        ),
        name="moved_attention",
    )(dest, received, move_keys, move_values)


def join_kernel(
    owner_hbm, plan_hbm, state_ref, lse_ref, slot_ref, out_ref, owner_ref, plan, states,
    states_lse, come_lses, flat, sems,
):
    seqs, rows, head_dim = out_ref.shape
    count = states.shape[0]
    copies = [
        pltpu.make_async_copy(owner_hbm, owner_ref, sems.at[0]),
        pltpu.make_async_copy(plan_hbm, plan, sems.at[1]),
    ]
    start_all(copies)
    real = pl.ds(0, rows)
    mask = piece_mask(rows)
    out_ref[...] = state_ref[:, :rows, :].astype(jnp.bfloat16)
    flat[...] = slot_ref[...].astype(jnp.float32)

    def answer_lse(n, _):
        row = n // CAP * answer_rows(rows) + CAP * padded(rows) + n % CAP
        lse = jnp.sum(jnp.where(mask, flat[pl.ds(row, 1), :], 0.0), axis=1, keepdims=True)
        come_lses[n] = jnp.broadcast_to(lse, (rows, LANES))
        return 0

    lax.fori_loop(0, count, answer_lse, 0, unroll=8)
    wait_all(copies)

    def join(n, old_sum, old_lse):
        come_lse = come_lses[n]
        top = jnp.maximum(old_lse, come_lse)
        old = jnp.exp2(old_lse - top)
        come = jnp.exp2(come_lse - top)
        weight = old + come
        place = n // CAP * answer_rows(rows) + n % CAP * padded(rows)
        come_sum = flat[pl.ds(pl.multiple_of(place, 8), rows), :]
        return (old * old_sum + come * come_sum) / weight, top + jnp.log2(weight)

    def every_slot(n, _):
        seq = jnp.maximum(owner_ref[n], 0)
        states[n], states_lse[n] = join(n, state_ref[seq, real], lse_ref[seq, real])
        return 0

    def later_slot(k, _):
        n = plan[2 * count + k]
        first = plan[n]
        states[first], states_lse[first] = join(n, states[first], states_lse[first])
        return 0

    def store_slot(k, _):
        n = plan[count + k]
        out_ref[owner_ref[n]] = states[n].astype(jnp.bfloat16)
        return 0

    lax.fori_loop(0, count, every_slot, 0, unroll=8)
    lax.fori_loop(0, plan[3 * count + 1], later_slot, 0)
    lax.fori_loop(0, plan[3 * count], store_slot, 0)


def join_moved(owner, plan, state, state_lse, answers, shape):
    slots = answers.shape[0] // answer_rows(shape[1]) * CAP
    block = pltpu.VMEM((slots,) + shape[1:], jnp.float32)
    return pl.pallas_call(
        join_kernel,
        in_specs=[hbm()] * 2 + [vmem()] * 3,
        out_specs=vmem(),
        out_shape=jax.ShapeDtypeStruct(shape, jnp.bfloat16),
        scratch_shapes=[
            pltpu.SMEM(owner.shape, jnp.int32),
            pltpu.SMEM(plan.shape, jnp.int32),
            block, block, block,
            pltpu.VMEM(answers.shape, jnp.float32),
            pltpu.SemaphoreType.DMA((2,)),
        ],
        compiler_params=limit(8),
        cost_estimate=pl.CostEstimate(
            flops=10 * state.size, bytes_accessed=10 * state.size, transcendentals=0
        ),
        name="join_moved",
    )(stay(owner), stay(plan), state, state_lse, answers)


def per_device(
    tokens_in, w_kv, queries, k_cache, v_cache, page_table, lengths, move_dest, move_page, move_seq
):
    groups = lax.axis_size("gen")
    tp = lax.axis_size("tp")
    seqs, steps, heads, head_dim = queries.shape
    kv_heads = k_cache.shape[1]
    scale = LOG2E / math.sqrt(head_dim)

    def exchange(array):
        return lax.all_to_all(array, "gen", split_axis=0, concat_axis=0, tiled=True)

    rows = queries.transpose(0, 2, 1, 3).reshape(seqs, heads * steps, head_dim)
    dest = move_dest.reshape(-1)
    to_send = gather(dest, move_seq, rows, groups)
    early = kv_heads // 2
    early_rows, to_send = lax.optimization_barrier((rows, to_send))
    received = exchange(to_send)
    table, lengths = page_table.T, lengths.reshape(1, seqs)
    *before, owner, plan, packed, partial, move_keys, move_values = early_work(
        table, lengths, move_page, early_rows, tokens_in, dest, move_seq, k_cache, v_cache, w_kv,
        groups, tp, early, scale,
    )
    pieces = []
    for k in range(1, tp):
        pairs = [(i, (i + k) % tp) for i in range(tp)]
        pieces.append(lax.ppermute(partial[k - 1], "tp", pairs))
    other = jnp.stack(pieces)
    answers = moved_attention(dest, received, move_keys, move_values, scale)
    packed, answers = lax.optimization_barrier((packed, answers))
    returned = exchange(answers)
    totals, tops, packed, x, w, *before = late_work(
        table, lengths, packed, k_cache, v_cache, tokens_in, w_kv, before, tp, early, scale
    )
    new_kv, state, state_lse = join_new(
        other, packed, x, w, before + [totals, tops], seqs, heads * steps // kv_heads, steps, scale
    )
    attended = join_moved(
        owner, plan, state, state_lse, returned, (seqs, heads * steps, head_dim)
    )
    attended = attended.reshape(seqs, heads, steps, head_dim).transpose(0, 2, 1, 3)
    return (attended, new_kv)


def solution(mesh):
    return jax.shard_map(
        per_device,
        mesh=mesh,
        in_specs=(
            P("gen", "tp"),
            P("tp", None),
            P("gen", None, "tp", None),
            P("gen", "tp", None, None),
            P("gen", "tp", None, None),
            P("gen", None),
            P("gen"),
            P(),
            P(),
            P(),
        ),
        out_specs=(P("gen", None, "tp", None), P("gen", "tp")),
        check_vma=False,
    )
```
